32 devices in a mesh: scene: 2 (over y), cell: 4 (over z), district: 4 (over x, core).
Axes of the slice: x: 2, y: 2, z: 4, core: 2. Of those that a mesh axis runs over, the one named last changes fastest.
Arguments:
- ray_geometry: float32 [6, 8192], P(None, ('scene', 'cell', 'district')), parts along dimension 1, may hold values from -5 to 5
- segment_length: float32 [8192, 4], P(('scene', 'cell', 'district')), parts along dimension 0, may hold values from 0.3 to 1
- jitter: float32 [8192, 128], P(('scene', 'cell', 'district')), parts along dimension 0, may hold values from 0 to 1
- appearance_codes: float32 [8192, 48], P(('scene', 'cell', 'district')), parts along dimension 0, may hold values from -5 to 5
- target: float32 [3, 8192], P(None, ('scene', 'cell', 'district')), parts along dimension 1, may hold values from 0 to 1
- crossing: int32 [8192, 4], P(('scene', 'cell', 'district')), parts along dimension 0, may hold values from 0 to 15, all different within a row; in each aligned block of 256 rows (0 to 255, 256 to 511, ...) at most 128 rows name the same one
- frequencies: float32 [3, 64], replicated, may hold values from -6 to 6
- cell_layers: bfloat16 [32, 2, 128, 128], P(('scene', 'cell', 'district')), parts along dimension 0, may hold values from -0.5 to 0.5
- district_prior: bfloat16 [8, 2, 128, 128], P(('scene', 'district')), parts along dimension 0, may hold values from -0.5 to 0.5
- head_weight: bfloat16 [32, 4, 128], P(('scene', 'cell', 'district')), parts along dimension 0, may hold values from -0.5 to 0.5
- appearance_weight: float32 [32, 3, 48], P(('scene', 'cell', 'district')), parts along dimension 0, may hold values from -0.875 to 0.875
Outputs:
- rendered: float32 [3, 8192], P(None, ('scene', 'cell', 'district')), parts along dimension 1
- grad_layers: float32 [32, 2, 128, 128], P(('scene', 'cell', 'district')), parts along dimension 0
- grad_prior: float32 [8, 2, 128, 128], P(('scene', 'district')), parts along dimension 0
- grad_head: float32 [32, 4, 128], P(('scene', 'cell', 'district')), parts along dimension 0
- grad_appearance: float32 [32, 3, 48], P(('scene', 'cell', 'district')), parts along dimension 0
- grad_codes: float32 [8192, 48], P(('scene', 'cell', 'district')), parts along dimension 0
The draws below stay inside these ranges and needn't reach their ends.
There are 2 independent parts, one for each index of `scene`. The reference program is written for one: setup_inputs(seed, part) draws one part's arguments, and reference() takes and returns one part's arrays. A program takes and returns all parts, laid end to end along the dimension named above; an argument that names none is the same for every part. Nothing has to cross between parts.
Inputs may be any that keep to these rules, and one draw needn't show every extreme that they name: `crossing`: each ray names 4 different cells, in the order in which it crosses them. Among the 256 rays of one device no cell is named more than 128 times, and in every draw some device's rays name some cell exactly 128 times.
All inputs are finite; a program needn't handle non-finite values.
Results may differ from the reference program's by a relative error of at most 0.0098.
Values sent between devices are 32-bit elements; how exact they have to be, the bound alone decides.
No kernel may reach another device: no remote copies, remote signals or barrier semaphores. Data moves between devices by JAX's collectives and lax.ppermute only.
A program may use at most 192 MiB of HBM per device.

```python
import math
import jax
import jax.numpy as jnp
import numpy as np
from jax import lax

R_DEV = 256
K = 4
S = 32
F = 128
APP = 48
HALF = 64
CELLS = 16
DISTRICTS = 4
RAYS = 4096
MOST = 128
N_CELL = 4
N_DISTRICT = 4


def block_scale(rng, shape, pieces, low, largest):
    gain = 1.0
    for dim, shards_of in pieces:
        draws = jax.random.uniform(jax.random.fold_in(jax.random.fold_in(rng, 6), dim), (shards_of,), jnp.float32, low / len(pieces), largest / len(pieces))
        gain = gain * jnp.repeat(jnp.exp(draws), shape[dim] // shards_of).reshape((-1,) + (1,) * (len(shape) - 1 - dim))
    return gain


def deal_out(rng, own, number, rows, amount, top, reach, lean):
    order = jax.random.permutation(rng, amount)
    packed, common = load_shares(amount, rows * top, reach, lean, True), load_shares(amount, rows * top, reach, lean, False)
    places = jnp.arange(amount)

    def named(sizes, turn):
        used = int((sizes > 0).sum())
        fixed = max(1, used // 4)
        shifted = fixed + (places - fixed + turn * (used - fixed)) % max(1, amount - fixed)
        return jnp.zeros((amount,), jnp.int32).at[order[jnp.where(places < fixed, places, shifted)]].set(jnp.asarray(sizes, jnp.int32))

    sizes = jnp.where(number % 4 == 0, named(packed, number // 4), named(common, number - number // 4 - 1))
    mixed = jax.random.permutation(jax.random.fold_in(own, 3), amount)
    donor, sink = mixed[0:amount // 2 * 2:2], mixed[1:amount // 2 * 2:2]
    margin = jnp.minimum(sizes[donor] - 1, reach - sizes[sink]) // 2
    margin = jnp.where((donor == order[0]) | (sink == order[0]) | (sizes[sink] == 0), 0, jnp.maximum(margin, 0))
    shifted = jax.random.randint(jax.random.fold_in(own, 4), (amount // 2,), 0, 1 << 20) % (margin + 1)
    sizes = sizes.at[donor].add(-shifted).at[sink].add(shifted)
    items = jnp.searchsorted(jnp.cumsum(sizes), jnp.arange(rows * top), side="right").astype(jnp.int32)
    table = items.reshape(top, rows).T
    table = table[jax.random.permutation(jax.random.fold_in(own, 1), rows)]
    turn = jax.random.randint(jax.random.fold_in(own, 2), (rows, 1), 0, top)
    return jnp.take_along_axis(table, (jnp.arange(top)[None, :] + turn) % top, axis=1)


def load_shares(number_of, total, limit, lean, full):
    weights = [(1 << 20) // math.isqrt(standing ** lean) + 1 for standing in range(1, number_of + 1)]
    largest = limit if full else min(limit, max(-(-total // number_of), total * weights[0] // sum(weights)))
    least = 1 if total - largest >= number_of - 1 else 0
    given, surplus = [largest] + [least] * (number_of - 1), total - largest - least * (number_of - 1)
    while surplus > 0:
        movable = [i for i in range(1, number_of) if given[i] < largest] or [i for i in range(1, number_of) if given[i] < limit]
        pool, remaining = sum([weights[i] for i in movable]), surplus
        for i in movable:
            addition = min(limit - given[i], max(1, remaining * weights[i] // pool), surplus)
            given[i] = given[i] + addition
            surplus = surplus - addition
    return np.array(given)


def normal_values(rng, dims, scale, reach, shards=(), kind=jnp.bfloat16):
    array = jax.random.normal(rng, dims, jnp.float32) * scale
    if len(shards) > 0:
        array = block_scale(rng, dims, shards, -0.22, 0.18) * array
    return jnp.clip(array, min=-reach, max=reach).astype(kind)


def setup_inputs(seed: int = 0, part: int = 0) -> dict:
    key_of = jax.random.split(jax.random.key(seed), 12)
    own_keys = jax.random.split(jax.random.fold_in(key_of[11], part), 12)
    ray_geometry = normal_values(own_keys[0], (6, RAYS), 1.0, 5.0, ((1, 16),), jnp.float32)
    segment_length = jnp.clip(0.3 + 0.7 * jax.random.uniform(own_keys[1], (RAYS, K), jnp.float32) ** block_scale(own_keys[1], (RAYS, K), ((0, 16),), -0.2, 0.2), 0.3, 1.0)
    jitter = jnp.clip(1.0 * jax.random.uniform(own_keys[2], (RAYS, K * S), jnp.float32) ** block_scale(own_keys[2], (RAYS, K * S), ((0, 16),), -0.2, 0.2), 0.0, 1.0)
    appearance_codes = normal_values(own_keys[3], (RAYS, APP), 1.0, 5.0, ((0, 16),), jnp.float32)
    target = jnp.clip(1.0 * jax.random.uniform(own_keys[4], (3, RAYS), jnp.float32) ** block_scale(own_keys[4], (3, RAYS), ((1, 16),), -0.2, 0.2), 0.0, 1.0)
    crossing_keys = jax.random.split(jax.random.fold_in(own_keys[5], 1), RAYS // R_DEV)
    crossing_turns = jax.random.permutation(jax.random.fold_in(own_keys[5], 3), RAYS // R_DEV)
    crossing = jax.vmap(lambda own, number: deal_out(jax.random.fold_in(own_keys[5], 2), own, number, R_DEV, N_CELL * N_DISTRICT, K, MOST, 2))(crossing_keys, crossing_turns).reshape((RAYS, K))
    frequencies = normal_values(key_of[6], (3, HALF), 1.5, 6.0, (), jnp.float32)
    cell_layers = normal_values(own_keys[7], (CELLS, 2, F, F), F ** -0.5, 0.5, ((0, 16),))
    district_prior = normal_values(own_keys[8], (DISTRICTS, 2, F, F), F ** -0.5, 0.5, ((0, 4),))
    head_weight = normal_values(own_keys[9], (CELLS, 4, F), F ** -0.5, 0.5, ((0, 16),))
    appearance_weight = normal_values(own_keys[10], (CELLS, 3, APP), APP ** -0.5, 0.875, ((0, 16),), jnp.float32)
    return {"ray_geometry": ray_geometry, "segment_length": segment_length, "jitter": jitter, "appearance_codes": appearance_codes, "target": target, "crossing": crossing, "frequencies": frequencies, "cell_layers": cell_layers, "district_prior": district_prior, "head_weight": head_weight, "appearance_weight": appearance_weight}


GEOMETRY = 8
HIGHEST_PRECISION = lax.Precision.HIGHEST


def build_payload(ray_geometry, segment_length, jitter, appearance_codes):
    ray_count, crossings = segment_length.shape
    samples = jitter.shape[1] // crossings
    near_depth = jnp.cumsum(segment_length, axis=1) - segment_length
    geometry = jnp.broadcast_to(ray_geometry.T[:, None, :], (ray_count, crossings, 6))
    codes_wide = jnp.broadcast_to(appearance_codes[:, None, :], (ray_count, crossings, appearance_codes.shape[1]))
    payload = jnp.concatenate([geometry, near_depth[:, :, None], segment_length[:, :, None], jitter.reshape(ray_count, crossings, samples), codes_wide], axis=2)
    return payload.reshape(ray_count * crossings, payload.shape[2])


def slot_index(crossing, cell_total, capacity):
    target_cell = crossing.reshape(-1)
    onehot = (target_cell[:, None] == jnp.arange(cell_total, dtype=jnp.int32)[None, :]).astype(jnp.int32)
    earlier = jnp.cumsum(onehot, axis=0) - onehot
    position = jnp.sum(earlier * onehot, axis=1)
    return (target_cell * capacity + position).astype(jnp.int32)


def sample_spacing(payload, samples):
    near_depth = payload[:, 6:7]
    extent = payload[:, 7:8]
    offsets = jnp.arange(samples, dtype=jnp.float32)[None, :]
    depths = near_depth + extent * (offsets + payload[:, GEOMETRY:GEOMETRY + samples]) / samples
    ending = jnp.concatenate([depths[:, 1:], near_depth + extent], axis=1)
    return depths, ending - depths


def cell_forward(payload, frequencies, first_weight, second_weight, head_one, samples):
    depths, spacing = sample_spacing(payload, samples)
    phases = jnp.zeros((payload.shape[0], samples, frequencies.shape[1]), jnp.float32)
    for component in range(3):
        position = payload[:, component:component + 1] + depths * payload[:, 3 + component:4 + component]
        phases = phases + position[:, :, None] * frequencies[component][None, None, :]
    encoded = jnp.concatenate([jnp.sin(phases), jnp.cos(phases)], axis=2)
    encoded = encoded.reshape(payload.shape[0] * samples, encoded.shape[2]).astype(jnp.bfloat16)
    first_act = jax.nn.relu(jnp.dot(encoded, first_weight, preferred_element_type=jnp.float32)).astype(jnp.bfloat16)
    second_act = jax.nn.relu(jnp.dot(first_act, second_weight, preferred_element_type=jnp.float32)).astype(jnp.bfloat16)
    raw_outputs = lax.dot_general(head_one, second_act, (((1,), (1,)), ((), ())), preferred_element_type=jnp.float32)
    return (encoded, first_act, second_act, raw_outputs), spacing


def shade(raw_outputs, payload, spacing, appearance_one, samples):
    slot_count = payload.shape[0]
    outputs = raw_outputs.reshape(4, slot_count, samples)
    code_part = payload[:, GEOMETRY + samples:]
    color_shift = jnp.dot(code_part, appearance_one.T, precision=HIGHEST_PRECISION)
    density = jax.nn.softplus(outputs[0])
    colors = jax.nn.sigmoid(outputs[1:] + color_shift.T[:, :, None])
    optical = density * spacing
    transmit = jnp.exp(-(jnp.cumsum(optical, axis=1) - optical))
    opacity = 1.0 - jnp.exp(-optical)
    blend_weight = transmit * opacity
    return outputs, colors, optical, transmit, opacity, blend_weight, code_part


def segment_partials(raw_outputs, payload, spacing, appearance_one, samples):
    shaded = shade(raw_outputs, payload, spacing, appearance_one, samples)
    colors, optical, blend_weight = shaded[1], shaded[2], shaded[5]
    segment_color = jnp.sum(blend_weight[None] * colors, axis=2)
    segment_log = -jnp.sum(optical, axis=1)
    return jnp.concatenate([segment_color.T, segment_log[:, None]], axis=1)


def cell_backward(payload, saved_acts, spacing, cotangent, second_weight, head_one, appearance_one, samples):
    encoded, first_act, second_act, raw_outputs = saved_acts
    outputs, colors, optical, transmit, opacity, blend_weight, code_part = shade(raw_outputs, payload, spacing, appearance_one, samples)
    color_grad = cotangent[:, :3].T
    log_grad = cotangent[:, 3]
    blend_grad = jnp.sum(color_grad[:, :, None] * colors, axis=0)
    colors_grad = color_grad[:, :, None] * blend_weight[None]
    transmit_grad = blend_grad * opacity
    optical_grad = blend_grad * transmit * (1.0 - opacity) - log_grad[:, None]
    before_grad = -transmit_grad * transmit
    later_sum = jnp.flip(jnp.cumsum(jnp.flip(before_grad, axis=1), axis=1), axis=1) - before_grad
    optical_grad = optical_grad + later_sum
    density_grad = optical_grad * spacing * jax.nn.sigmoid(outputs[0])
    logit_grad = colors_grad * colors * (1.0 - colors)
    slot_count = payload.shape[0]
    output_grad = jnp.concatenate([density_grad[None], logit_grad], axis=0).reshape(4, slot_count * samples).astype(jnp.bfloat16)
    head_grad = jnp.dot(output_grad, second_act, preferred_element_type=jnp.float32)
    shift_grad = jnp.sum(logit_grad, axis=2)
    appearance_grad = jnp.dot(shift_grad, code_part, precision=HIGHEST_PRECISION)
    code_grad = jnp.dot(shift_grad.T, appearance_one, precision=HIGHEST_PRECISION)
    second_grad = lax.dot_general(output_grad, head_one, (((0,), (0,)), ((), ())), preferred_element_type=jnp.float32)
    second_grad = jnp.where(second_act > 0, second_grad, 0.0).astype(jnp.bfloat16)
    second_weight_grad = lax.dot_general(first_act, second_grad, (((0,), (0,)), ((), ())), preferred_element_type=jnp.float32)
    first_grad = lax.dot_general(second_grad, second_weight, (((1,), (1,)), ((), ())), preferred_element_type=jnp.float32)
    first_grad = jnp.where(first_act > 0, first_grad, 0.0).astype(jnp.bfloat16)
    first_weight_grad = lax.dot_general(encoded, first_grad, (((0,), (0,)), ((), ())), preferred_element_type=jnp.float32)
    return first_weight_grad, second_weight_grad, head_grad, appearance_grad, code_grad


def composite(gathered, target):
    segment_color = gathered[:, :, :3]
    segment_log = gathered[:, :, 3]
    reach_weight = jnp.exp(jnp.cumsum(segment_log, axis=1) - segment_log)
    rendered = jnp.sum(reach_weight[:, :, None] * segment_color, axis=1).T
    residual = rendered - target
    color_grad = reach_weight[:, :, None] * residual.T[:, None, :]
    reach_grad = jnp.sum(residual.T[:, None, :] * segment_color, axis=2) * reach_weight
    log_grad = jnp.flip(jnp.cumsum(jnp.flip(reach_grad, axis=1), axis=1), axis=1) - reach_grad
    return rendered, jnp.concatenate([color_grad, log_grad[:, :, None]], axis=2)


def reference(ray_geometry, segment_length, jitter, appearance_codes, target, crossing, frequencies, cell_layers, district_prior, head_weight, appearance_weight):
    cell_total = N_CELL * N_DISTRICT
    segments = R_DEV * K
    slot_total = cell_total * MOST
    payload = build_payload(ray_geometry, segment_length, jitter, appearance_codes)
    row_width = payload.shape[1]
    payload = payload.reshape(cell_total, segments, row_width)
    places = lax.map(lambda crossed: slot_index(crossed, cell_total, MOST), crossing.reshape(cell_total, R_DEV, K))

    def pack_rows(bundle):
        slot_rows, where_to = bundle
        return jnp.zeros((slot_total, slot_rows.shape[1]), slot_rows.dtype).at[where_to].set(slot_rows)

    def transpose_blocks(blocks):
        columns = blocks.shape[-1]
        return blocks.reshape(cell_total, cell_total, MOST, columns).transpose(1, 0, 2, 3).reshape(cell_total, slot_total, columns)

    arrived = transpose_blocks(lax.map(pack_rows, (payload, places)))
    owner_district = jnp.arange(cell_total) % N_DISTRICT
    effective = (cell_layers.astype(jnp.float32) + district_prior.astype(jnp.float32)[owner_district]).astype(jnp.bfloat16)

    def forward_cell(bundle):
        slot_rows, weight_pair, head_one, appearance_one = bundle
        saved_acts, spacing = cell_forward(slot_rows, frequencies, weight_pair[0], weight_pair[1], head_one, S)
        return segment_partials(saved_acts[3], slot_rows, spacing, appearance_one, S)

    partials = lax.map(forward_cell, (arrived, effective, head_weight, appearance_weight))
    returned = transpose_blocks(partials)
    gathered = jax.vmap(lambda lookup, where_to: lookup[where_to])(returned, places)
    rendered, cotangent = composite(gathered.reshape(cell_total * R_DEV, K, 4), target)
    incoming = transpose_blocks(lax.map(pack_rows, (cotangent.reshape(cell_total, segments, 4), places)))

    def backward_cell(bundle):
        slot_rows, weight_pair, head_one, appearance_one, incoming_rows = bundle
        saved_acts, spacing = cell_forward(slot_rows, frequencies, weight_pair[0], weight_pair[1], head_one, S)
        return cell_backward(slot_rows, saved_acts, spacing, incoming_rows, weight_pair[1], head_one, appearance_one, S)

    first_w, second_w, head_grad, appearance_grad, code_grad = lax.map(backward_cell, (arrived, effective, head_weight, appearance_weight, incoming))
    code_back = transpose_blocks(code_grad)
    code_rows = jax.vmap(lambda lookup, where_to: lookup[where_to])(code_back, places)
    grad_codes = jnp.sum(code_rows.reshape(cell_total * R_DEV, K, APP), axis=1)
    grad_layers = jnp.stack([first_w, second_w], axis=1)
    grad_prior = jnp.sum(grad_layers.reshape(N_CELL, N_DISTRICT, 2, F, F), axis=0) / N_CELL
    return rendered, grad_layers, grad_prior, head_grad, appearance_grad, grad_codes
```

```python
import functools

import jax
import jax.numpy as jnp
from jax import lax
from jax.experimental import pallas as pl
from jax.experimental.pallas import tpu as pltpu
from jax.sharding import PartitionSpec as P

GEOMETRY = 8
HIGHEST_PRECISION = lax.Precision.HIGHEST


def build_front(ray_geometry, segment_length, jitter):
    ray_count, crossings = segment_length.shape
    samples = jitter.shape[1] // crossings
    near_depth = jnp.cumsum(segment_length, axis=1) - segment_length
    geometry = jnp.broadcast_to(ray_geometry.T[:, None, :], (ray_count, crossings, 6))
    front = jnp.concatenate(
        [
            geometry,
            near_depth[:, :, None],
            segment_length[:, :, None],
            jitter.reshape(ray_count, crossings, samples),
        ],
        axis=2,
    )
    return front.reshape(ray_count * crossings, front.shape[2])


def slot_positions(crossing, cell_total, capacity):
    target_cell = crossing.reshape(-1)
    total_rows = target_cell.shape[0]
    onehot = target_cell[:, None] == jnp.arange(cell_total, dtype=jnp.int32)[None, :]
    triangle = (
        lax.broadcasted_iota(jnp.int32, (total_rows, total_rows), 0)
        > lax.broadcasted_iota(jnp.int32, (total_rows, total_rows), 1)
    ).astype(jnp.bfloat16)
    earlier = jnp.dot(triangle, onehot.astype(jnp.bfloat16), preferred_element_type=jnp.float32)
    position = jnp.sum(jnp.where(onehot, earlier, 0.0), axis=1).astype(jnp.int32)
    return target_cell * capacity + position


def sample_spacing(payload, samples):
    near_depth = payload[:, 6:7]
    extent = payload[:, 7:8]
    offsets = jnp.arange(samples, dtype=jnp.float32)[None, :]
    depths = near_depth + extent * (offsets + payload[:, GEOMETRY : GEOMETRY + samples]) / samples
    ending = jnp.concatenate([depths[:, 1:], near_depth + extent], axis=1)
    return (depths, ending - depths)


def cell_forward(payload, frequencies, first_weight, second_weight, head_one, samples):
    depths, spacing = sample_spacing(payload, samples)
    phases = jnp.zeros((payload.shape[0], samples, frequencies.shape[1]), jnp.float32)
    for component in range(3):
        position = (
            payload[:, component : component + 1]
            + depths * payload[:, 3 + component : 4 + component]
        )
        phases = phases + position[:, :, None] * frequencies[component][None, None, :]
    encoded = jnp.concatenate([jnp.sin(phases), jnp.cos(phases)], axis=2)
    encoded = encoded.reshape(payload.shape[0] * samples, encoded.shape[2]).astype(jnp.bfloat16)
    first_act = jax.nn.relu(
        jnp.dot(encoded, first_weight, preferred_element_type=jnp.float32)
    ).astype(jnp.bfloat16)
    second_act = jax.nn.relu(
        jnp.dot(first_act, second_weight, preferred_element_type=jnp.float32)
    ).astype(jnp.bfloat16)
    raw_outputs = lax.dot_general(
        head_one, second_act, (((1,), (1,)), ((), ())), preferred_element_type=jnp.float32
    )
    return ((encoded, first_act, second_act, raw_outputs), spacing)


def shade(raw_outputs, payload, spacing, appearance_one, samples):
    slot_count = payload.shape[0]
    outputs = raw_outputs.reshape(4, slot_count, samples)
    code_part = payload[:, GEOMETRY + samples :]
    color_shift = jnp.dot(code_part, appearance_one.T, precision=HIGHEST_PRECISION)
    density = jax.nn.softplus(outputs[0])
    colors = jax.nn.sigmoid(outputs[1:] + color_shift.T[:, :, None])
    optical = density * spacing
    transmit = jnp.exp(-(jnp.cumsum(optical, axis=1) - optical))
    opacity = 1.0 - jnp.exp(-optical)
    blend_weight = transmit * opacity
    return (outputs, colors, optical, transmit, opacity, blend_weight, code_part)


def segment_partials(raw_outputs, payload, spacing, appearance_one, samples):
    shaded = shade(raw_outputs, payload, spacing, appearance_one, samples)
    colors, optical, blend_weight = (shaded[1], shaded[2], shaded[5])
    segment_color = jnp.sum(blend_weight[None] * colors, axis=2)
    segment_log = -jnp.sum(optical, axis=1)
    return jnp.concatenate([segment_color.T, segment_log[:, None]], axis=1)


def cell_backward(
    payload, saved_acts, spacing, cotangent, second_weight, head_one, appearance_one, samples
):
    encoded, first_act, second_act, raw_outputs = saved_acts
    outputs, colors, optical, transmit, opacity, blend_weight, code_part = shade(
        raw_outputs, payload, spacing, appearance_one, samples
    )
    color_grad = cotangent[:, :3].T
    log_grad = cotangent[:, 3]
    blend_grad = jnp.sum(color_grad[:, :, None] * colors, axis=0)
    colors_grad = color_grad[:, :, None] * blend_weight[None]
    transmit_grad = blend_grad * opacity
    optical_grad = blend_grad * transmit * (1.0 - opacity) - log_grad[:, None]
    before_grad = -transmit_grad * transmit
    later_sum = jnp.flip(jnp.cumsum(jnp.flip(before_grad, axis=1), axis=1), axis=1) - before_grad
    optical_grad = optical_grad + later_sum
    density_grad = optical_grad * spacing * jax.nn.sigmoid(outputs[0])
    logit_grad = colors_grad * colors * (1.0 - colors)
    slot_count = payload.shape[0]
    output_grad = (
        jnp.concatenate([density_grad[None], logit_grad], axis=0)
        .reshape(4, slot_count * samples)
        .astype(jnp.bfloat16)
    )
    head_grad = jnp.dot(output_grad, second_act, preferred_element_type=jnp.float32)
    shift_grad = jnp.sum(logit_grad, axis=2)
    second_grad = lax.dot_general(
        output_grad, head_one, (((0,), (0,)), ((), ())), preferred_element_type=jnp.float32
    )
    second_grad = jnp.where(second_act > 0, second_grad, 0.0).astype(jnp.bfloat16)
    second_weight_grad = lax.dot_general(
        first_act, second_grad, (((0,), (0,)), ((), ())), preferred_element_type=jnp.float32
    )
    first_grad = lax.dot_general(
        second_grad, second_weight, (((1,), (1,)), ((), ())), preferred_element_type=jnp.float32
    )
    first_grad = jnp.where(first_act > 0, first_grad, 0.0).astype(jnp.bfloat16)
    first_weight_grad = lax.dot_general(
        encoded, first_grad, (((0,), (0,)), ((), ())), preferred_element_type=jnp.float32
    )
    return (first_weight_grad, second_weight_grad, head_grad, shift_grad, code_part)


def composite(gathered, target):
    segment_color = gathered[:, :, :3]
    segment_log = gathered[:, :, 3]
    reach_weight = jnp.exp(jnp.cumsum(segment_log, axis=1) - segment_log)
    rendered = jnp.sum(reach_weight[:, :, None] * segment_color, axis=1).T
    residual = rendered - target
    color_grad = reach_weight[:, :, None] * residual.T[:, None, :]
    reach_grad = jnp.sum(residual.T[:, None, :] * segment_color, axis=2) * reach_weight
    log_grad = jnp.flip(jnp.cumsum(jnp.flip(reach_grad, axis=1), axis=1), axis=1) - reach_grad
    return (rendered, jnp.concatenate([color_grad, log_grad[:, :, None]], axis=2))


def routed(
    ray_geometry,
    segment_length,
    jitter,
    appearance_codes,
    target,
    crossing,
    frequencies,
    cell_layers,
    district_prior,
    head_weight,
    appearance_weight,
):
    num_cell = lax.axis_size("cell")
    num_district = lax.axis_size("district")
    cell_total = num_cell * num_district
    ray_count, crossings = crossing.shape
    samples = jitter.shape[1] // crossings
    segments = ray_count * crossings
    capacity = 2 * segments // cell_total
    slot_total = cell_total * capacity
    code_width = appearance_codes.shape[1]
    front = build_front(ray_geometry, segment_length, jitter)
    codes_seg = jnp.broadcast_to(
        appearance_codes[:, None, :], (ray_count, crossings, code_width)
    ).reshape(segments, code_width)
    payload = jnp.concatenate([front, codes_seg], axis=1)
    appearance_one = appearance_weight[0]
    row_width = payload.shape[1]
    places = slot_positions(crossing, cell_total, capacity)
    outbox = (
        jnp.zeros((slot_total, row_width), jnp.float32)
        .at[places]
        .set(payload)
        .reshape(cell_total, capacity * row_width)
    )
    arrived = lax.all_to_all(outbox, ("cell", "district"), split_axis=0, concat_axis=0, tiled=True)
    arrived = arrived.reshape(slot_total, row_width)
    effective = (cell_layers[0].astype(jnp.float32) + district_prior[0].astype(jnp.float32)).astype(
        jnp.bfloat16
    )
    head_one = head_weight[0]
    block_rows = min(512, slot_total)
    blocked = arrived.reshape(slot_total // block_rows, block_rows, row_width)

    def forward_keep(slot_rows):
        saved_acts, spacing = cell_forward(
            slot_rows, frequencies, effective[0], effective[1], head_one, samples
        )
        return (
            segment_partials(saved_acts[3], slot_rows, spacing, appearance_one, samples),
            saved_acts,
        )

    partials, stored = lax.map(forward_keep, blocked)
    partials = partials.reshape(cell_total, capacity * 4)
    returned = lax.all_to_all(
        partials, ("cell", "district"), split_axis=0, concat_axis=0, tiled=True
    )
    returned = returned.reshape(slot_total, 4)
    rendered, cotangent = composite(returned[places].reshape(ray_count, crossings, 4), target)
    grad_box = (
        jnp.zeros((slot_total, 4), jnp.float32)
        .at[places]
        .set(cotangent.reshape(segments, 4))
        .reshape(cell_total, capacity * 4)
    )
    incoming = lax.all_to_all(
        grad_box, ("cell", "district"), split_axis=0, concat_axis=0, tiled=True
    )
    incoming = incoming.reshape(slot_total // block_rows, block_rows, 4)

    def finish(result):
        first_part, second_part, head_part, shift_grad, code_part = result
        appearance_part = jnp.dot(shift_grad, code_part, precision=HIGHEST_PRECISION)
        code_part_grad = jnp.dot(shift_grad.T, appearance_one, precision=HIGHEST_PRECISION)
        return (first_part, second_part, head_part, appearance_part, code_part_grad)

    def backward_keep(bundle):
        slot_rows, incoming_rows, saved_acts = bundle
        spacing = sample_spacing(slot_rows, samples)[1]
        return finish(
            cell_backward(
                slot_rows,
                saved_acts,
                spacing,
                incoming_rows,
                effective[1],
                head_one,
                appearance_one,
                samples,
            )
        )

    pieces = lax.map(backward_keep, (blocked, incoming, stored))
    first_w = jnp.sum(pieces[0], axis=0)
    second_w = jnp.sum(pieces[1], axis=0)
    head_grad = jnp.sum(pieces[2], axis=0)
    appearance_grad = jnp.sum(pieces[3], axis=0)
    code_box = pieces[4].reshape(cell_total, capacity * code_width)
    code_back = lax.all_to_all(
        code_box, ("cell", "district"), split_axis=0, concat_axis=0, tiled=True
    )
    code_back = code_back.reshape(slot_total, code_width)
    grad_codes = jnp.sum(code_back[places].reshape(ray_count, crossings, code_width), axis=1)
    grad_pair = jnp.stack([first_w, second_w], axis=0)
    grad_prior = lax.psum(grad_pair, "cell") / num_cell
    return (
        rendered,
        grad_pair[None],
        grad_prior[None],
        head_grad[None],
        appearance_grad[None],
        grad_codes,
    )


TILE = 8
UNROLL = 4
ROWS = 264
HEAD_ROW = 256
APP_ROW = 260
VMEM_LIMIT = 56 * 1024 * 1024
COS = (
    0.9999992251396179,
    -19.738981246948242,
    64.92865753173828,
    -85.27162170410156,
    58.79049301147461,
    -21.07110595703125,
)
F32 = jnp.float32
BF16 = jnp.bfloat16


def iota(shape, axis):
    return lax.broadcasted_iota(jnp.int32, shape, axis)


def dot_nn(a, b):
    return jnp.dot(a, b, preferred_element_type=F32)


def dot_nt(a, b):
    return lax.dot_general(a, b, (((1,), (1,)), ((), ())), preferred_element_type=F32)


def split3(x):
    high = x.astype(BF16)
    rest = x - high.astype(F32)
    mid = rest.astype(BF16)
    low = (rest - mid.astype(F32)).astype(BF16)
    return high, mid, low


def pick_nn(x, select):
    high, mid, low = split3(x)
    return (dot_nn(low, select) + dot_nn(mid, select)) + dot_nn(high, select)


def pick_nt(select, x):
    high, mid, low = split3(x)
    return (dot_nt(select, low) + dot_nt(select, mid)) + dot_nt(select, high)


def exact_nn(a, b):
    return jnp.dot(a, b, precision=HIGHEST_PRECISION, preferred_element_type=F32)


def put_channel(ref, c, x):
    for h in range(ref.shape[0]):
        ref[h, pl.ds(c, x.shape[0], 8), :] = x[:, 128 * h : 128 * (h + 1)]


def get_channel(ref, c):
    tiles = ref.shape[1] // 8
    return jnp.concatenate([ref[h, pl.ds(c, tiles, 8), :] for h in range(ref.shape[0])], axis=1)


def get_tile(ref, t):
    rows = pl.ds(pl.multiple_of(t * 8, 8), 8)
    return jnp.concatenate([ref[h, rows, :] for h in range(ref.shape[0])], axis=1)


def put_tile(ref, t, x):
    rows = pl.ds(pl.multiple_of(t * 8, 8), 8)
    for h in range(ref.shape[0]):
        ref[h, rows, :] = x[:, 128 * h : 128 * (h + 1)]


def pack_kernel(layers_ref, prior_ref, head_ref, app_ref, out_ref):
    for layer in range(2):
        both = layers_ref[0, layer].astype(F32) + prior_ref[0, layer].astype(F32)
        out_ref[128 * layer : 128 * (layer + 1), :] = both.T
    out_ref[HEAD_ROW:ROWS, :] = jnp.zeros((ROWS - HEAD_ROW, 128), F32)
    out_ref[HEAD_ROW : HEAD_ROW + 4, :] = head_ref[0].astype(F32)
    out_ref[APP_ROW : APP_ROW + 3, 0 : app_ref.shape[2]] = app_ref[0]


def slot_mask(place_row):
    return (iota((TILE, place_row.shape[1]), 0) == place_row.astype(jnp.int32)).astype(F32)


def tile_onehot(tile_row, tiles):
    return (iota((tiles, tile_row.shape[1]), 0) == tile_row.astype(jnp.int32)).astype(F32).astype(BF16)


def cell_onehot(cells_ref, cells):
    return [
        (iota((cells, cells_ref.shape[1]), 0) == cells_ref[k : k + 1, :]).astype(F32)
        for k in range(cells_ref.shape[0])
    ]


def lane_select(channels, lanes):
    rows = channels * TILE
    row, column = iota((rows, channels * lanes), 0), iota((rows, channels * lanes), 1)
    same = (row // TILE == column // lanes) & (row % TILE == column % TILE)
    return same.astype(F32).astype(BF16)


def encode_kernel(
    cells,
    samples,
    cells_ref,
    geometry_ref,
    length_ref,
    jitter_ref,
    frequency_ref,
    encoded_ref,
    meta_ref,
    spacing_ref,
    tile_cell_ref,
    tile_start_ref,
    position_ref,
    factor_ref,
):
    tiles = spacing_ref.shape[0]
    lanes = TILE * samples
    crossings, rays = cells_ref.shape
    segments = crossings * rays

    @pl.when(pl.program_id(0) == 0)
    def _():
        onehot = jnp.concatenate(cell_onehot(cells_ref, cells), axis=1)
        chunks = [onehot[:, 128 * c : 128 * (c + 1)] for c in range(segments // 128)]
        before = (iota((128, 128), 0) < iota((128, 128), 1)).astype(F32).astype(BF16)
        prefix = dot_nn(jnp.concatenate(chunks, axis=0).astype(BF16), before)
        running = jnp.zeros((cells, 1), F32)
        ranks = []
        for c, chunk in enumerate(chunks):
            earlier = prefix[cells * c : cells * (c + 1), :] + running
            ranks.append(jnp.sum(chunk * earlier, axis=0, keepdims=True))
            running = running + jnp.sum(chunk, axis=1, keepdims=True)
        rank = jnp.concatenate(ranks, axis=1)
        needed = jnp.broadcast_to(jnp.floor((running + (TILE - 1)) * (1.0 / TILE)), (cells, 128))
        lower = (iota((cells, cells), 1) < iota((cells, cells), 0)).astype(F32).astype(BF16)
        start = dot_nn(lower, needed.astype(BF16))
        inside = jnp.floor(rank * (1.0 / TILE))
        tile_row = jnp.sum(onehot * start[:, 0:1], axis=0, keepdims=True) + inside
        place_row = rank - inside * TILE
        meta_ref[...] = jnp.concatenate(
            [tile_row, place_row, jnp.zeros((6, segments), F32)], axis=0
        )
        ends = start[:, 0:1] + needed[:, 0:1]
        owner = jnp.sum(
            (ends <= iota((cells, tile_cell_ref.shape[1]), 1).astype(F32)).astype(F32),
            axis=0,
            keepdims=True,
        )
        owner = jnp.minimum(owner, cells - 1.0).astype(jnp.int32)
        tile_cell_ref[...] = jnp.broadcast_to(owner, tile_cell_ref.shape)
        tile_start_ref[0:cells, :] = start.astype(jnp.int32)
        tile_start_ref[cells : cells + 8, :] = jnp.broadcast_to(
            ends[cells - 1 : cells, :], (8, 128)
        ).astype(jnp.int32)

        mask = slot_mask(place_row)
        place = tile_onehot(tile_row, tiles)
        lengths = length_ref[...].T
        near = jnp.zeros((1, rays), F32)
        nears, extents = [], []
        for k in range(crossings):
            nears.append(near)
            extents.append(lengths[k : k + 1, :])
            near = near + lengths[k : k + 1, :]
        rows = [
            jnp.concatenate([geometry_ref[c : c + 1, :]] * crossings, axis=1) for c in range(6)
        ]
        rows += [jnp.concatenate(nears, axis=1), jnp.concatenate(extents, axis=1)]
        wide = pick_nt(place, jnp.concatenate([mask * row for row in rows], axis=0))
        wide = pick_nn(wide, lane_select(8, lanes))
        channel = [wide[:, lanes * c : lanes * (c + 1)] for c in range(8)]
        turned = jitter_ref[...].T
        offsets = jnp.concatenate(
            [turned[samples * k : samples * (k + 1), :] for k in range(crossings)], axis=1
        )
        dealt = jnp.concatenate([mask * offsets[i : i + 1, :] for i in range(samples)], axis=0)
        jitter = pick_nt(place, dealt)
        step = (iota((tiles, lanes), 1) // TILE).astype(F32)
        near, extent = channel[6], channel[7]
        depths = near + extent * (step + jitter) / samples
        following = pltpu.roll(depths, lanes - TILE, 1)
        ending = jnp.where(iota((tiles, lanes), 1) >= lanes - TILE, near + extent, following)
        spacing_ref[...] = ending - depths
        for c in range(3):
            put_channel(position_ref, c, channel[c] + depths * channel[3 + c])
        put_channel(position_ref, 3, jnp.ones((tiles, lanes), F32))
        for c in range(4, 8):
            put_channel(position_ref, c, jnp.zeros((tiles, lanes), F32))
        turns = frequency_ref[...] * 0.15915494309189535
        turns = jnp.concatenate([turns, turns], axis=1)
        features = turns.shape[1]
        quarter = jnp.where(iota((1, features), 1) < features // 2, -0.25, 0.0)
        block = jnp.concatenate([turns, quarter, jnp.zeros((4, features), F32)], axis=0)
        high, mid, low = [part.astype(F32) for part in split3(block)]
        stack = [high, high, high, mid, mid, low, jnp.zeros((features - 48, features), F32)]
        factor_ref[...] = jnp.concatenate(stack, axis=0).T[:, 0:48].astype(BF16)

    factor = factor_ref[...]
    for u in range(UNROLL):
        t = pl.program_id(0) * UNROLL + u
        high, mid, low = split3(get_tile(position_ref, t))
        high, mid, low = high.astype(F32), mid.astype(F32), low.astype(F32)
        points = jnp.concatenate([high, mid, low, high, mid, high], axis=0).astype(BF16)
        phase = dot_nn(factor, points)
        phase = phase - jnp.round(phase)
        square = phase * phase
        value = jnp.full_like(square, COS[5])
        for c in (4, 3, 2, 1, 0):
            value = value * square + COS[c]
        encoded_ref[u] = value.astype(BF16)


def step_kernel(
    cells,
    samples,
    num_cell,
    tile_cell_ref,
    tile_start_ref,
    near_ref,
    flip_ref,
    core_near_ref,
    core_flip_ref,
    encoded_ref,
    meta_ref,
    cells_ref,
    spacing_ref,
    codes_ref,
    target_ref,
    rendered_ref,
    codes_grad_ref,
    keep_ref,
    send_ref,
    first_ref,
    second_ref,
    forward1_ref,
    forward2_ref,
    backward2_ref,
    head_ref,
    head_turned_ref,
    outputs_ref,
    grads_ref,
    sums_ref,
    semaphore,
):
    tiles, lanes = spacing_ref.shape
    crossings, rays = cells_ref.shape
    segments = crossings * rays
    width = codes_ref.shape[1]
    used = tile_start_ref[cells, 0]
    trips = (used + UNROLL - 1) // UNROLL

    appearance = []
    for group, ref in enumerate((near_ref, flip_ref, core_near_ref, core_flip_ref)):
        for s in range(num_cell):
            v = group * num_cell + s
            forward1_ref[v] = ref[s, 0:128, :].astype(BF16)
            second = ref[s, 128:256, :]
            forward2_ref[v] = second.astype(BF16)
            backward2_ref[v] = second.T.astype(BF16)
            tail = ref[s, HEAD_ROW:ROWS, :]
            head = jnp.where(iota((8, 128), 0) < 4, tail, 0.0)
            head_ref[v] = head.astype(BF16)
            square = jnp.concatenate([head, jnp.zeros((120, 128), F32)], axis=0)
            head_turned_ref[v] = square.T[:, 0:8].astype(BF16)
            appearance.append(tail)
    outputs_ref[...] = jnp.zeros_like(outputs_ref)
    sums_ref[...] = jnp.zeros_like(sums_ref)

    def forward(trip, carry):
        for u in range(UNROLL):
            t = trip * UNROLL + u
            v = tile_cell_ref[0, t]
            first = jnp.maximum(dot_nn(forward1_ref[v], encoded_ref[t]), 0.0).astype(BF16)
            first_ref[t] = first
            second = jnp.maximum(dot_nn(forward2_ref[v], first), 0.0).astype(BF16)
            second_ref[t] = second
            put_tile(outputs_ref, t, dot_nn(head_ref[v], second))
        return carry

    lax.fori_loop(0, trips, forward, 0)

    tile_row, place_row = meta_ref[0:1, :], meta_ref[1:2, :]
    mask = slot_mask(place_row)
    place = tile_onehot(tile_row, tiles)
    onehots = cell_onehot(cells_ref, cells)
    maps = jnp.concatenate(
        [jnp.concatenate([tail[4 + c : 5 + c, :] for tail in appearance], axis=0) for c in range(3)],
        axis=0,
    )[:, 0:width]
    codes = codes_ref[...]
    shifts = lax.dot_general(
        maps,
        codes,
        (((1,), (1,)), ((), ())),
        precision=HIGHEST_PRECISION,
        preferred_element_type=F32,
    )
    rows = [
        jnp.concatenate(
            [
                jnp.sum(onehots[k] * shifts[cells * c : cells * (c + 1), :], axis=0, keepdims=True)
                for k in range(crossings)
            ],
            axis=1,
        )
        for c in range(3)
    ]
    spread3 = lane_select(4, lanes)
    shift = pick_nt(place, jnp.concatenate([mask * row for row in rows], axis=0))
    shift = pick_nn(shift, spread3[0:24, 0 : 3 * lanes])

    spacing = spacing_ref[...]
    raw = get_channel(outputs_ref, 0)
    ray = (iota((lanes, lanes), 0) % TILE) == (iota((lanes, lanes), 1) % TILE)
    earlier = (ray & (iota((lanes, lanes), 0) < iota((lanes, lanes), 1))).astype(F32).astype(BF16)
    later = (ray & (iota((lanes, lanes), 0) > iota((lanes, lanes), 1))).astype(F32).astype(BF16)
    total = ((iota((TILE, lanes), 1) % TILE) == iota((TILE, lanes), 0)).astype(F32).astype(BF16)
    density = jax.nn.softplus(raw)
    colors = [
        jax.nn.sigmoid(
            get_channel(outputs_ref, 1 + c) + shift[:, lanes * c : lanes * (c + 1)]
        )
        for c in range(3)
    ]
    optical = density * spacing
    transmit = jnp.exp(-pick_nn(optical, earlier))
    opacity = 1.0 - jnp.exp(-optical)
    blend = transmit * opacity
    sums = [pick_nt(total, blend * color) for color in colors] + [-pick_nt(total, optical)]
    dealt = pick_nn(jnp.concatenate(sums, axis=0), place)
    parts = [
        jnp.sum(mask * dealt[TILE * c : TILE * (c + 1), :], axis=0, keepdims=True) for c in range(4)
    ]

    def crossed(row, k):
        return row[:, rays * k : rays * (k + 1)]

    reach, logs = [], jnp.zeros((1, rays), F32)
    for k in range(crossings):
        reach.append(jnp.exp(logs))
        logs = logs + crossed(parts[3], k)
    residuals, channel_grads = [], [[] for _ in range(3)]
    for c in range(3):
        rendered = sum(reach[k] * crossed(parts[c], k) for k in range(crossings))
        rendered_ref[c : c + 1, :] = rendered
        residuals.append(rendered - target_ref[c : c + 1, :])
    log_grads, after = [], jnp.zeros((1, rays), F32)
    for k in reversed(range(crossings)):
        log_grads.append(after)
        weight = sum(residuals[c] * crossed(parts[c], k) for c in range(3))
        after = after + weight * reach[k]
    log_row = jnp.concatenate(log_grads[::-1], axis=1)
    color_rows = [
        jnp.concatenate([reach[k] * residuals[c] for k in range(crossings)], axis=1)
        for c in range(3)
    ]
    back = pick_nt(place, jnp.concatenate([mask * row for row in color_rows + [log_row]], axis=0))
    back = pick_nn(back, spread3)
    color_grads = [back[:, lanes * c : lanes * (c + 1)] for c in range(3)]
    log_grad = back[:, 3 * lanes : 4 * lanes]

    blend_grad = sum(color_grads[c] * colors[c] for c in range(3))
    before_grad = -(blend_grad * opacity) * transmit
    optical_grad = blend_grad * transmit * (1.0 - opacity) - log_grad
    optical_grad = optical_grad + pick_nn(before_grad, later)
    put_channel(grads_ref, 0, optical_grad * spacing * jax.nn.sigmoid(raw))
    logits = []
    for c in range(3):
        logit = color_grads[c] * blend * colors[c] * (1.0 - colors[c])
        put_channel(grads_ref, 1 + c, logit)
        put_channel(grads_ref, 4 + c, jnp.zeros((tiles, lanes), F32))
        logits.append(pick_nt(total, logit))
    put_channel(grads_ref, 7, jnp.zeros((tiles, lanes), F32))
    dealt = pick_nn(jnp.concatenate(logits, axis=0), place)
    per_cell = []
    for c in range(3):
        row = jnp.sum(mask * dealt[TILE * c : TILE * (c + 1), :], axis=0, keepdims=True)
        per_cell.append(sum(onehots[k] * crossed(row, k) for k in range(crossings)))
    per_cell = jnp.concatenate(per_cell, axis=0)
    map_grads = exact_nn(per_cell, codes)
    codes_grad_ref[...] = exact_nn(per_cell.T, maps)
    for v in range(cells):
        for c in range(3):
            sums_ref[v, APP_ROW + c : APP_ROW + c + 1, 0:width] = map_grads[
                cells * c + v : cells * c + v + 1, :
            ]

    def backward(trip, carry):
        for u in range(UNROLL):
            t = trip * UNROLL + u
            v = tile_cell_ref[0, t]
            output = get_tile(grads_ref, t).astype(BF16)
            first, second, encoded = first_ref[t], second_ref[t], encoded_ref[t]
            second_grad = dot_nn(head_turned_ref[v], output)
            second_grad = jnp.where(second.astype(F32) > 0, second_grad, 0.0).astype(BF16)
            first_grad = dot_nn(backward2_ref[v], second_grad)
            first_grad = jnp.where(first.astype(F32) > 0, first_grad, 0.0).astype(BF16)
            sums_ref[v, HEAD_ROW:ROWS, :] += dot_nt(output, second)
            sums_ref[v, 128:256, :] += dot_nt(first, second_grad)
            sums_ref[v, 0:128, :] += dot_nt(encoded, first_grad)
        return carry

    lax.fori_loop(0, trips, backward, 0)
    half = cells // 2
    copies = [
        pltpu.make_async_copy(sums_ref.at[pl.ds(0, half)], keep_ref, semaphore.at[0]),
        pltpu.make_async_copy(sums_ref.at[pl.ds(half, half)], send_ref, semaphore.at[1]),
    ]
    for copy in copies:
        copy.start()
    for copy in copies:
        copy.wait()


def resident(
    ray_geometry,
    segment_length,
    jitter,
    appearance_codes,
    target,
    crossing,
    frequencies,
    cell_layers,
    district_prior,
    head_weight,
    appearance_weight,
):
    num_cell = lax.axis_size("cell")
    num_district = lax.axis_size("district")
    cells = num_cell * num_district
    rays, crossings = crossing.shape
    samples = jitter.shape[1] // crossings
    segments = rays * crossings
    width = appearance_codes.shape[1]
    lanes = TILE * samples
    tiles = -(-(segments // TILE + cells) // 8) * 8
    me_cell, me_district = lax.axis_index("cell"), lax.axis_index("district")

    def along_cell(x, steps):
        return lax.ppermute(x, "cell", [(i, (i + steps) % num_cell) for i in range(num_cell)])

    def flip(x, bit):
        return lax.ppermute(x, "district", [(i, i ^ bit) for i in range(num_district)])

    own = pl.pallas_call(
        pack_kernel, out_shape=jax.ShapeDtypeStruct((ROWS, 128), F32), name="pack"
    )(cell_layers, district_prior, head_weight, appearance_weight)
    near = jnp.stack([own] + [along_cell(own, s) for s in range(1, num_cell)])
    flipped = flip(near, 2)
    core_near, core_flipped = flip(near, 1), flip(flipped, 1)

    away = (crossing % num_district) ^ me_district
    steps = (me_cell - crossing // num_district) % num_cell
    virtual = ((away & 1) * 2 + (away >> 1)) * num_cell + steps
    whole = lambda shape: pl.BlockSpec(shape, lambda i: (0,) * len(shape))
    encoded, meta, spacing, tile_cell, tile_start = pl.pallas_call(
        functools.partial(encode_kernel, cells, samples),
        grid=(tiles // UNROLL,),
        in_specs=[
            whole((crossings, rays)),
            whole((6, rays)),
            whole((rays, crossings)),
            whole((rays, crossings * samples)),
            whole(frequencies.shape),
        ],
        out_specs=[
            pl.BlockSpec((UNROLL, 128, lanes), lambda i: (i, 0, 0)),
            whole((8, segments)),
            whole((tiles, lanes)),
            whole((8, 256)),
            whole((cells + 8, 128)),
        ],
        out_shape=[
            jax.ShapeDtypeStruct((tiles, 128, lanes), BF16),
            jax.ShapeDtypeStruct((8, segments), F32),
            jax.ShapeDtypeStruct((tiles, lanes), F32),
            jax.ShapeDtypeStruct((8, 256), jnp.int32),
            jax.ShapeDtypeStruct((cells + 8, 128), jnp.int32),
        ],
        scratch_shapes=[
            pltpu.VMEM((lanes // 128, tiles * 8, 128), F32),
            pltpu.VMEM((128, 48), BF16),
        ],
        compiler_params=pltpu.CompilerParams(vmem_limit_bytes=VMEM_LIMIT),
        name="encode",
    )(virtual.T, ray_geometry, segment_length, jitter, frequencies)

    vmem, smem = pl.BlockSpec(memory_space=pltpu.VMEM), pl.BlockSpec(memory_space=pltpu.SMEM)
    half = cells // 2
    rendered, codes_grad, keep, send = pl.pallas_call(
        functools.partial(step_kernel, cells, samples, num_cell),
        in_specs=[smem, smem] + [vmem] * 10,
        out_specs=[vmem, vmem, pl.BlockSpec(memory_space=pl.ANY), pl.BlockSpec(memory_space=pl.ANY)],
        out_shape=[
            jax.ShapeDtypeStruct((3, rays), F32),
            jax.ShapeDtypeStruct((rays, width), F32),
            jax.ShapeDtypeStruct((half, ROWS, 128), F32),
            jax.ShapeDtypeStruct((half, ROWS, 128), F32),
        ],
        scratch_shapes=[
            pltpu.VMEM((tiles, 128, lanes), BF16),
            pltpu.VMEM((tiles, 128, lanes), BF16),
            pltpu.VMEM((cells, 128, 128), BF16),
            pltpu.VMEM((cells, 128, 128), BF16),
            pltpu.VMEM((cells, 128, 128), BF16),
            pltpu.VMEM((cells, 8, 128), BF16),
            pltpu.VMEM((cells, 128, 8), BF16),
            pltpu.VMEM((lanes // 128, tiles * 8, 128), F32),
            pltpu.VMEM((lanes // 128, tiles * 8, 128), F32),
            pltpu.VMEM((cells, ROWS, 128), F32),
            pltpu.SemaphoreType.DMA((2,)),
        ],
        compiler_params=pltpu.CompilerParams(vmem_limit_bytes=VMEM_LIMIT),
        name="step",
    )(
        tile_cell,
        tile_start,
        near,
        flipped,
        core_near,
        core_flipped,
        encoded,
        meta,
        virtual.T,
        spacing,
        appearance_codes,
        target,
    )

    summed = keep + flip(send, 1)
    summed = summed[:num_cell] + flip(summed[num_cell:], 2)
    arrived = [along_cell(summed[s], -s) for s in range(1, num_cell)]
    own_sum = summed[0] + sum(arrived)
    layers = own_sum[0:HEAD_ROW].reshape(2, 128, 128)
    others = [along_cell(layers, s) for s in range(1, num_cell)]
    prior = (layers + sum(others)) / num_cell
    return (
        rendered,
        layers[None],
        prior[None],
        own_sum[None, HEAD_ROW : HEAD_ROW + 4],
        own_sum[None, APP_ROW : APP_ROW + 3, 0:width],
        codes_grad,
    )


def local(*args):
    cells = lax.axis_size("cell") * lax.axis_size("district")
    if cells <= 16 and lax.axis_size("district") == 4:
        return resident(*args)
    return routed(*args)


def solution(mesh):
    placed = (
        P(None, ("scene", "cell", "district")),
        P(("scene", "cell", "district"), None),
        P(("scene", "cell", "district"), None),
        P(("scene", "cell", "district"), None),
        P(None, ("scene", "cell", "district")),
        P(("scene", "cell", "district"), None),
        P(),
        P(("scene", "cell", "district"), None, None, None),
        P(("scene", "district"), None, None, None),
        P(("scene", "cell", "district"), None, None),
        P(("scene", "cell", "district"), None, None),
    )
    return jax.shard_map(
        local,
        mesh=mesh,
        in_specs=placed,
        out_specs=(
            P(None, ("scene", "cell", "district")),
            P(("scene", "cell", "district"), None, None, None),
            P(("scene", "district"), None, None, None),
            P(("scene", "cell", "district"), None, None),
            P(("scene", "cell", "district"), None, None),
            P(("scene", "cell", "district"), None),
        ),
        check_vma=False,
    )
```

```python
import functools

import jax
import jax.numpy as jnp
from jax import lax
from jax.experimental import pallas as pl
from jax.experimental.pallas import tpu as pltpu
from jax.sharding import PartitionSpec as P

GEOMETRY = 8
HIGHEST_PRECISION = lax.Precision.HIGHEST


def build_front(ray_geometry, segment_length, jitter):
    ray_count, crossings = segment_length.shape
    samples = jitter.shape[1] // crossings
    near_depth = jnp.cumsum(segment_length, axis=1) - segment_length
    geometry = jnp.broadcast_to(ray_geometry.T[:, None, :], (ray_count, crossings, 6))
    front = jnp.concatenate(
        [
            geometry,
            near_depth[:, :, None],
            segment_length[:, :, None],
            jitter.reshape(ray_count, crossings, samples),
        ],
        axis=2,
    )
    return front.reshape(ray_count * crossings, front.shape[2])


def slot_positions(crossing, cell_total, capacity):
    target_cell = crossing.reshape(-1)
    total_rows = target_cell.shape[0]
    onehot = target_cell[:, None] == jnp.arange(cell_total, dtype=jnp.int32)[None, :]
    triangle = (
        lax.broadcasted_iota(jnp.int32, (total_rows, total_rows), 0)
        > lax.broadcasted_iota(jnp.int32, (total_rows, total_rows), 1)
    ).astype(jnp.bfloat16)
    earlier = jnp.dot(triangle, onehot.astype(jnp.bfloat16), preferred_element_type=jnp.float32)
    position = jnp.sum(jnp.where(onehot, earlier, 0.0), axis=1).astype(jnp.int32)
    return target_cell * capacity + position


def sample_spacing(payload, samples):
    near_depth = payload[:, 6:7]
    extent = payload[:, 7:8]
    offsets = jnp.arange(samples, dtype=jnp.float32)[None, :]
    depths = near_depth + extent * (offsets + payload[:, GEOMETRY : GEOMETRY + samples]) / samples
    ending = jnp.concatenate([depths[:, 1:], near_depth + extent], axis=1)
    return (depths, ending - depths)


def cell_forward(payload, frequencies, first_weight, second_weight, head_one, samples):
    depths, spacing = sample_spacing(payload, samples)
    phases = jnp.zeros((payload.shape[0], samples, frequencies.shape[1]), jnp.float32)
    for component in range(3):
        position = (
            payload[:, component : component + 1]
            + depths * payload[:, 3 + component : 4 + component]
        )
        phases = phases + position[:, :, None] * frequencies[component][None, None, :]
    encoded = jnp.concatenate([jnp.sin(phases), jnp.cos(phases)], axis=2)
    encoded = encoded.reshape(payload.shape[0] * samples, encoded.shape[2]).astype(jnp.bfloat16)
    first_act = jax.nn.relu(
        jnp.dot(encoded, first_weight, preferred_element_type=jnp.float32)
    ).astype(jnp.bfloat16)
    second_act = jax.nn.relu(
        jnp.dot(first_act, second_weight, preferred_element_type=jnp.float32)
    ).astype(jnp.bfloat16)
    raw_outputs = lax.dot_general(
        head_one, second_act, (((1,), (1,)), ((), ())), preferred_element_type=jnp.float32
    )
    return ((encoded, first_act, second_act, raw_outputs), spacing)


def shade(raw_outputs, payload, spacing, appearance_one, samples):
    slot_count = payload.shape[0]
    outputs = raw_outputs.reshape(4, slot_count, samples)
    code_part = payload[:, GEOMETRY + samples :]
    color_shift = jnp.dot(code_part, appearance_one.T, precision=HIGHEST_PRECISION)
    density = jax.nn.softplus(outputs[0])
    colors = jax.nn.sigmoid(outputs[1:] + color_shift.T[:, :, None])
    optical = density * spacing
    transmit = jnp.exp(-(jnp.cumsum(optical, axis=1) - optical))
    opacity = 1.0 - jnp.exp(-optical)
    blend_weight = transmit * opacity
    return (outputs, colors, optical, transmit, opacity, blend_weight, code_part)


def segment_partials(raw_outputs, payload, spacing, appearance_one, samples):
    shaded = shade(raw_outputs, payload, spacing, appearance_one, samples)
    colors, optical, blend_weight = (shaded[1], shaded[2], shaded[5])
    segment_color = jnp.sum(blend_weight[None] * colors, axis=2)
    segment_log = -jnp.sum(optical, axis=1)
    return jnp.concatenate([segment_color.T, segment_log[:, None]], axis=1)


def cell_backward(
    payload, saved_acts, spacing, cotangent, second_weight, head_one, appearance_one, samples
):
    encoded, first_act, second_act, raw_outputs = saved_acts
    outputs, colors, optical, transmit, opacity, blend_weight, code_part = shade(
        raw_outputs, payload, spacing, appearance_one, samples
    )
    color_grad = cotangent[:, :3].T
    log_grad = cotangent[:, 3]
    blend_grad = jnp.sum(color_grad[:, :, None] * colors, axis=0)
    colors_grad = color_grad[:, :, None] * blend_weight[None]
    transmit_grad = blend_grad * opacity
    optical_grad = blend_grad * transmit * (1.0 - opacity) - log_grad[:, None]
    before_grad = -transmit_grad * transmit
    later_sum = jnp.flip(jnp.cumsum(jnp.flip(before_grad, axis=1), axis=1), axis=1) - before_grad
    optical_grad = optical_grad + later_sum
    density_grad = optical_grad * spacing * jax.nn.sigmoid(outputs[0])
    logit_grad = colors_grad * colors * (1.0 - colors)
    slot_count = payload.shape[0]
    output_grad = (
        jnp.concatenate([density_grad[None], logit_grad], axis=0)
        .reshape(4, slot_count * samples)
        .astype(jnp.bfloat16)
    )
    head_grad = jnp.dot(output_grad, second_act, preferred_element_type=jnp.float32)
    shift_grad = jnp.sum(logit_grad, axis=2)
    second_grad = lax.dot_general(
        output_grad, head_one, (((0,), (0,)), ((), ())), preferred_element_type=jnp.float32
    )
    second_grad = jnp.where(second_act > 0, second_grad, 0.0).astype(jnp.bfloat16)
    second_weight_grad = lax.dot_general(
        first_act, second_grad, (((0,), (0,)), ((), ())), preferred_element_type=jnp.float32
    )
    first_grad = lax.dot_general(
        second_grad, second_weight, (((1,), (1,)), ((), ())), preferred_element_type=jnp.float32
    )
    first_grad = jnp.where(first_act > 0, first_grad, 0.0).astype(jnp.bfloat16)
    first_weight_grad = lax.dot_general(
        encoded, first_grad, (((0,), (0,)), ((), ())), preferred_element_type=jnp.float32
    )
    return (first_weight_grad, second_weight_grad, head_grad, shift_grad, code_part)


def composite(gathered, target):
    segment_color = gathered[:, :, :3]
    segment_log = gathered[:, :, 3]
    reach_weight = jnp.exp(jnp.cumsum(segment_log, axis=1) - segment_log)
    rendered = jnp.sum(reach_weight[:, :, None] * segment_color, axis=1).T
    residual = rendered - target
    color_grad = reach_weight[:, :, None] * residual.T[:, None, :]
    reach_grad = jnp.sum(residual.T[:, None, :] * segment_color, axis=2) * reach_weight
    log_grad = jnp.flip(jnp.cumsum(jnp.flip(reach_grad, axis=1), axis=1), axis=1) - reach_grad
    return (rendered, jnp.concatenate([color_grad, log_grad[:, :, None]], axis=2))


def routed(
    ray_geometry,
    segment_length,
    jitter,
    appearance_codes,
    target,
    crossing,
    frequencies,
    cell_layers,
    district_prior,
    head_weight,
    appearance_weight,
):
    num_cell = lax.axis_size("cell")
    num_district = lax.axis_size("district")
    cell_total = num_cell * num_district
    ray_count, crossings = crossing.shape
    samples = jitter.shape[1] // crossings
    segments = ray_count * crossings
    capacity = 2 * segments // cell_total
    slot_total = cell_total * capacity
    code_width = appearance_codes.shape[1]
    front = build_front(ray_geometry, segment_length, jitter)
    codes_seg = jnp.broadcast_to(
        appearance_codes[:, None, :], (ray_count, crossings, code_width)
    ).reshape(segments, code_width)
    payload = jnp.concatenate([front, codes_seg], axis=1)
    appearance_one = appearance_weight[0]
    row_width = payload.shape[1]
    places = slot_positions(crossing, cell_total, capacity)
    outbox = (
        jnp.zeros((slot_total, row_width), jnp.float32)
        .at[places]
        .set(payload)
        .reshape(cell_total, capacity * row_width)
    )
    arrived = lax.all_to_all(outbox, ("cell", "district"), split_axis=0, concat_axis=0, tiled=True)
    arrived = arrived.reshape(slot_total, row_width)
    effective = (cell_layers[0].astype(jnp.float32) + district_prior[0].astype(jnp.float32)).astype(
        jnp.bfloat16
    )
    head_one = head_weight[0]
    block_rows = min(512, slot_total)
    blocked = arrived.reshape(slot_total // block_rows, block_rows, row_width)

    def forward_keep(slot_rows):
        saved_acts, spacing = cell_forward(
            slot_rows, frequencies, effective[0], effective[1], head_one, samples
        )
        return (
            segment_partials(saved_acts[3], slot_rows, spacing, appearance_one, samples),
            saved_acts,
        )

    partials, stored = lax.map(forward_keep, blocked)
    partials = partials.reshape(cell_total, capacity * 4)
    returned = lax.all_to_all(
        partials, ("cell", "district"), split_axis=0, concat_axis=0, tiled=True
    )
    returned = returned.reshape(slot_total, 4)
    rendered, cotangent = composite(returned[places].reshape(ray_count, crossings, 4), target)
    grad_box = (
        jnp.zeros((slot_total, 4), jnp.float32)
        .at[places]
        .set(cotangent.reshape(segments, 4))
        .reshape(cell_total, capacity * 4)
    )
    incoming = lax.all_to_all(
        grad_box, ("cell", "district"), split_axis=0, concat_axis=0, tiled=True
    )
    incoming = incoming.reshape(slot_total // block_rows, block_rows, 4)

    def finish(result):
        first_part, second_part, head_part, shift_grad, code_part = result
        appearance_part = jnp.dot(shift_grad, code_part, precision=HIGHEST_PRECISION)
        code_part_grad = jnp.dot(shift_grad.T, appearance_one, precision=HIGHEST_PRECISION)
        return (first_part, second_part, head_part, appearance_part, code_part_grad)

    def backward_keep(bundle):
        slot_rows, incoming_rows, saved_acts = bundle
        spacing = sample_spacing(slot_rows, samples)[1]
        return finish(
            cell_backward(
                slot_rows,
                saved_acts,
                spacing,
                incoming_rows,
                effective[1],
                head_one,
                appearance_one,
                samples,
            )
        )

    pieces = lax.map(backward_keep, (blocked, incoming, stored))
    first_w = jnp.sum(pieces[0], axis=0)
    second_w = jnp.sum(pieces[1], axis=0)
    head_grad = jnp.sum(pieces[2], axis=0)
    appearance_grad = jnp.sum(pieces[3], axis=0)
    code_box = pieces[4].reshape(cell_total, capacity * code_width)
    code_back = lax.all_to_all(
        code_box, ("cell", "district"), split_axis=0, concat_axis=0, tiled=True
    )
    code_back = code_back.reshape(slot_total, code_width)
    grad_codes = jnp.sum(code_back[places].reshape(ray_count, crossings, code_width), axis=1)
    grad_pair = jnp.stack([first_w, second_w], axis=0)
    grad_prior = lax.psum(grad_pair, "cell") / num_cell
    return (
        rendered,
        grad_pair[None],
        grad_prior[None],
        head_grad[None],
        appearance_grad[None],
        grad_codes,
    )


TILE = 8
UNROLL = 16
ROWS = 264
HEAD_ROW = 256
APP_ROW = 260
VMEM_LIMIT = 56 * 1024 * 1024
COS = (
    0.9999992251396179,
    -19.738981246948242,
    64.92865753173828,
    -85.27162170410156,
    58.79049301147461,
    -21.07110595703125,
)
F32 = jnp.float32
BF16 = jnp.bfloat16


def iota(shape, axis):
    return lax.broadcasted_iota(jnp.int32, shape, axis)


def dot_nn(a, b):
    return jnp.dot(a, b, preferred_element_type=F32)


def dot_nt(a, b):
    return lax.dot_general(a, b, (((1,), (1,)), ((), ())), preferred_element_type=F32)


def split3(x):
    high = x.astype(BF16)
    rest = x - high.astype(F32)
    mid = rest.astype(BF16)
    low = (rest - mid.astype(F32)).astype(BF16)
    return high, mid, low


def pick_nn(x, select):
    high, mid, low = split3(x)
    return (dot_nn(low, select) + dot_nn(mid, select)) + dot_nn(high, select)


def pick_nt(select, x):
    high, mid, low = split3(x)
    return (dot_nt(select, low) + dot_nt(select, mid)) + dot_nt(select, high)


def exact_nn(a, b):
    return jnp.dot(a, b, precision=HIGHEST_PRECISION, preferred_element_type=F32)


def put_channel(ref, c, x):
    for h in range(ref.shape[0]):
        ref[h, pl.ds(c, x.shape[0], 8), :] = x[:, 128 * h : 128 * (h + 1)]


def get_channel(ref, c):
    tiles = ref.shape[1] // 8
    return jnp.concatenate([ref[h, pl.ds(c, tiles, 8), :] for h in range(ref.shape[0])], axis=1)


def get_tile(ref, t):
    rows = pl.ds(pl.multiple_of(t * 8, 8), 8)
    return jnp.concatenate([ref[h, rows, :] for h in range(ref.shape[0])], axis=1)


def put_tile(ref, t, x):
    rows = pl.ds(pl.multiple_of(t * 8, 8), 8)
    for h in range(ref.shape[0]):
        ref[h, rows, :] = x[:, 128 * h : 128 * (h + 1)]


def pack_kernel(layers_ref, prior_ref, head_ref, app_ref, out_ref):
    for layer in range(2):
        both = layers_ref[0, layer].astype(F32) + prior_ref[0, layer].astype(F32)
        out_ref[128 * layer : 128 * (layer + 1), :] = both.T
    out_ref[HEAD_ROW:ROWS, :] = jnp.zeros((ROWS - HEAD_ROW, 128), F32)
    out_ref[HEAD_ROW : HEAD_ROW + 4, :] = head_ref[0].astype(F32)
    for c in range(3):
        out_ref[APP_ROW + c : APP_ROW + c + 1, 0 : app_ref.shape[2]] = app_ref[c]


def slot_mask(place_row):
    return (iota((TILE, place_row.shape[1]), 0) == place_row.astype(jnp.int32)).astype(F32)


def tile_onehot(tile_row, tiles):
    return (iota((tiles, tile_row.shape[1]), 0) == tile_row.astype(jnp.int32)).astype(F32).astype(BF16)


def cell_onehot(cells_ref, cells):
    return [
        (iota((cells, cells_ref.shape[1]), 0) == cells_ref[k : k + 1, :]).astype(F32)
        for k in range(cells_ref.shape[0])
    ]


def lane_select(channels, lanes):
    rows = channels * TILE
    row, column = iota((rows, channels * lanes), 0), iota((rows, channels * lanes), 1)
    same = (row // TILE == column // lanes) & (row % TILE == column % TILE)
    return same.astype(F32).astype(BF16)


def deal_kernel(
    cells,
    samples,
    cells_ref,
    geometry_ref,
    length_ref,
    jitter_ref,
    frequency_ref,
    meta_ref,
    spacing_ref,
    tile_cell_ref,
    tile_start_ref,
    position_ref,
    factor_ref,
):
    tiles = spacing_ref.shape[0]
    lanes = TILE * samples
    crossings, rays = cells_ref.shape
    segments = crossings * rays

    onehot = jnp.concatenate(cell_onehot(cells_ref, cells), axis=1)
    chunks = [onehot[:, 128 * c : 128 * (c + 1)] for c in range(segments // 128)]
    before = (iota((128, 128), 0) < iota((128, 128), 1)).astype(F32).astype(BF16)
    prefix = dot_nn(jnp.concatenate(chunks, axis=0).astype(BF16), before)
    running = jnp.zeros((cells, 1), F32)
    ranks = []
    for c, chunk in enumerate(chunks):
        earlier = prefix[cells * c : cells * (c + 1), :] + running
        ranks.append(jnp.sum(chunk * earlier, axis=0, keepdims=True))
        running = running + jnp.sum(chunk, axis=1, keepdims=True)
    rank = jnp.concatenate(ranks, axis=1)
    needed = jnp.broadcast_to(jnp.floor((running + (TILE - 1)) * (1.0 / TILE)), (cells, 128))
    lower = (iota((cells, cells), 1) < iota((cells, cells), 0)).astype(F32).astype(BF16)
    start = dot_nn(lower, needed.astype(BF16))
    inside = jnp.floor(rank * (1.0 / TILE))
    tile_row = jnp.sum(onehot * start[:, 0:1], axis=0, keepdims=True) + inside
    place_row = rank - inside * TILE
    meta_ref[...] = jnp.concatenate(
        [tile_row, place_row, jnp.zeros((6, segments), F32)], axis=0
    )
    ends = start[:, 0:1] + needed[:, 0:1]
    owner = jnp.sum(
        (ends <= iota((cells, tile_cell_ref.shape[1]), 1).astype(F32)).astype(F32),
        axis=0,
        keepdims=True,
    )
    owner = jnp.minimum(owner, cells - 1.0).astype(jnp.int32)
    tile_cell_ref[...] = jnp.broadcast_to(owner, tile_cell_ref.shape)
    tile_start_ref[0:cells, :] = start.astype(jnp.int32)
    tile_start_ref[cells : cells + 8, :] = jnp.broadcast_to(
        ends[cells - 1 : cells, :], (8, 128)
    ).astype(jnp.int32)

    mask = slot_mask(place_row)
    place = tile_onehot(tile_row, tiles)
    lengths = length_ref[...]
    near = jnp.zeros((1, rays), F32)
    nears, extents = [], []
    for k in range(crossings):
        nears.append(near)
        extents.append(lengths[k : k + 1, :])
        near = near + lengths[k : k + 1, :]
    rows = [
        jnp.concatenate([geometry_ref[c : c + 1, :]] * crossings, axis=1) for c in range(6)
    ]
    rows += [jnp.concatenate(nears, axis=1), jnp.concatenate(extents, axis=1)]
    wide = pick_nt(place, jnp.concatenate([mask * row for row in rows], axis=0))
    wide = pick_nn(wide, lane_select(8, lanes))
    channel = [wide[:, lanes * c : lanes * (c + 1)] for c in range(8)]
    turned = jitter_ref[...].T
    offsets = jnp.concatenate(
        [turned[samples * k : samples * (k + 1), :] for k in range(crossings)], axis=1
    )
    dealt = jnp.concatenate([mask * offsets[i : i + 1, :] for i in range(samples)], axis=0)
    jitter = pick_nt(place, dealt)
    step = (iota((tiles, lanes), 1) // TILE).astype(F32)
    near, extent = channel[6], channel[7]
    depths = near + extent * (step + jitter) / samples
    following = pltpu.roll(depths, lanes - TILE, 1)
    ending = jnp.where(iota((tiles, lanes), 1) >= lanes - TILE, near + extent, following)
    spacing_ref[...] = ending - depths
    for c in range(3):
        put_channel(position_ref, c, channel[c] + depths * channel[3 + c])
    put_channel(position_ref, 3, jnp.ones((tiles, lanes), F32))
    for c in range(4, 8):
        put_channel(position_ref, c, jnp.zeros((tiles, lanes), F32))
    turns = frequency_ref[...] * 0.15915494309189535
    turns = jnp.concatenate([turns, turns], axis=1)
    features = turns.shape[1]
    quarter = jnp.where(iota((1, features), 1) < features // 2, -0.25, 0.0)
    block = jnp.concatenate([turns, quarter, jnp.zeros((4, features), F32)], axis=0)
    high, mid, low = [part.astype(F32) for part in split3(block)]
    stack = [high, high, high, mid, mid, low, jnp.zeros((features - 48, features), F32)]
    factor_ref[...] = jnp.concatenate(stack, axis=0).T[:, 0:48].astype(BF16)


def encode(position_ref, factor, encoded_ref, some):
    phases = []
    for t in some:
        high, mid, low = split3(get_tile(position_ref, t))
        high, mid, low = high.astype(F32), mid.astype(F32), low.astype(F32)
        points = jnp.concatenate([high, mid, low, high, mid, high], axis=0).astype(BF16)
        phases.append(dot_nn(factor, points))
    for t, phase in zip(some, phases):
        phase = phase - jnp.round(phase)
        square = phase * phase
        value = square * COS[5] + COS[4]
        for c in (3, 2, 1, 0):
            value = value * square + COS[c]
        encoded_ref[t] = value.astype(BF16)


def step_kernel(
    cells,
    samples,
    tile_cell_ref,
    tile_start_ref,
    meta_ref,
    cells_ref,
    spacing_ref,
    position_ref,
    factor_ref,
    codes_ref,
    target_ref,
    *refs,
):
    weights, refs = refs[:cells], refs[cells:]
    (
        rendered_ref,
        codes_grad_ref,
        keep_ref,
        send_ref,
        encoded_ref,
        first_ref,
        second_ref,
        forward1_ref,
        forward2_ref,
        backward2_ref,
        head_ref,
        head_turned_ref,
        outputs_ref,
        grads_ref,
        sums_ref,
        semaphore,
    ) = refs
    tiles, lanes = spacing_ref.shape
    crossings, rays = cells_ref.shape
    segments = crossings * rays
    width = codes_ref.shape[0]
    used = tile_start_ref[cells, 0]
    trips = (used + UNROLL - 1) // UNROLL

    appearance = []
    for v, ref in enumerate(weights):
        forward1_ref[v] = ref[0:128, :].astype(BF16)
        second = ref[128:256, :]
        forward2_ref[v] = second.astype(BF16)
        backward2_ref[v] = second.T.astype(BF16)
        tail = ref[HEAD_ROW:ROWS, :]
        head = jnp.where(iota((8, 128), 0) < 4, tail, 0.0)
        head_ref[v] = head.astype(BF16)
        square = jnp.concatenate([head, jnp.zeros((120, 128), F32)], axis=0)
        head_turned_ref[v] = square.T[:, 0:8].astype(BF16)
        appearance.append(tail)
    outputs_ref[...] = jnp.zeros_like(outputs_ref)
    sums_ref[...] = jnp.zeros_like(sums_ref)

    factor = factor_ref[...]
    encode(position_ref, factor, encoded_ref, range(UNROLL))

    def forward(trip, carry):
        following = jnp.minimum(trip + 1, trips - 1) * UNROLL
        some = [trip * UNROLL + u for u in range(UNROLL)]
        owner = [tile_cell_ref[0, t] for t in some]
        firsts = [dot_nn(forward1_ref[v], encoded_ref[t]) for t, v in zip(some, owner)]
        firsts = [jnp.maximum(first, 0.0).astype(BF16) for first in firsts]
        for t, first in zip(some, firsts):
            first_ref[t] = first
        seconds = [dot_nn(forward2_ref[v], first) for v, first in zip(owner, firsts)]
        seconds = [jnp.maximum(second, 0.0).astype(BF16) for second in seconds]
        for t, second in zip(some, seconds):
            second_ref[t] = second
        outputs = [dot_nn(head_ref[v], second) for v, second in zip(owner, seconds)]
        for t, output in zip(some, outputs):
            put_tile(outputs_ref, t, output)
        encode(position_ref, factor, encoded_ref, [following + u for u in range(UNROLL)])
        return carry

    lax.fori_loop(0, trips, forward, 0)

    tile_row, place_row = meta_ref[0:1, :], meta_ref[1:2, :]
    mask = slot_mask(place_row)
    place = tile_onehot(tile_row, tiles)
    onehots = cell_onehot(cells_ref, cells)
    maps = jnp.concatenate(
        [jnp.concatenate([tail[4 + c : 5 + c, :] for tail in appearance], axis=0) for c in range(3)],
        axis=0,
    )[:, 0:width]
    codes = codes_ref[...]
    shifts = exact_nn(maps, codes)
    rows = [
        jnp.concatenate(
            [
                jnp.sum(onehots[k] * shifts[cells * c : cells * (c + 1), :], axis=0, keepdims=True)
                for k in range(crossings)
            ],
            axis=1,
        )
        for c in range(3)
    ]
    spread3 = lane_select(4, lanes)
    shift = pick_nt(place, jnp.concatenate([mask * row for row in rows], axis=0))
    shift = pick_nn(shift, spread3[0:24, 0 : 3 * lanes])

    spacing = spacing_ref[...]
    raw = get_channel(outputs_ref, 0)
    ray = (iota((lanes, lanes), 0) % TILE) == (iota((lanes, lanes), 1) % TILE)
    earlier = (ray & (iota((lanes, lanes), 0) < iota((lanes, lanes), 1))).astype(F32).astype(BF16)
    later = (ray & (iota((lanes, lanes), 0) > iota((lanes, lanes), 1))).astype(F32).astype(BF16)
    total = ((iota((TILE, lanes), 1) % TILE) == iota((TILE, lanes), 0)).astype(F32).astype(BF16)
    density = jax.nn.softplus(raw)
    colors = [
        jax.nn.sigmoid(
            get_channel(outputs_ref, 1 + c) + shift[:, lanes * c : lanes * (c + 1)]
        )
        for c in range(3)
    ]
    optical = density * spacing
    transmit = jnp.exp(-pick_nn(optical, earlier))
    opacity = 1.0 - jnp.exp(-optical)
    blend = transmit * opacity
    sums = [pick_nt(total, blend * color) for color in colors] + [-pick_nt(total, optical)]
    dealt = pick_nn(jnp.concatenate(sums, axis=0), place)
    parts = [
        jnp.sum(mask * dealt[TILE * c : TILE * (c + 1), :], axis=0, keepdims=True) for c in range(4)
    ]

    def crossed(row, k):
        return row[:, rays * k : rays * (k + 1)]

    reach, logs = [], jnp.zeros((1, rays), F32)
    for k in range(crossings):
        reach.append(jnp.exp(logs))
        logs = logs + crossed(parts[3], k)
    residuals, channel_grads = [], [[] for _ in range(3)]
    for c in range(3):
        rendered = sum(reach[k] * crossed(parts[c], k) for k in range(crossings))
        rendered_ref[c : c + 1, :] = rendered
        residuals.append(rendered - target_ref[c : c + 1, :])
    log_grads, after = [], jnp.zeros((1, rays), F32)
    for k in reversed(range(crossings)):
        log_grads.append(after)
        weight = sum(residuals[c] * crossed(parts[c], k) for c in range(3))
        after = after + weight * reach[k]
    log_row = jnp.concatenate(log_grads[::-1], axis=1)
    color_rows = [
        jnp.concatenate([reach[k] * residuals[c] for k in range(crossings)], axis=1)
        for c in range(3)
    ]
    back = pick_nt(place, jnp.concatenate([mask * row for row in color_rows + [log_row]], axis=0))
    back = pick_nn(back, spread3)
    color_grads = [back[:, lanes * c : lanes * (c + 1)] for c in range(3)]
    log_grad = back[:, 3 * lanes : 4 * lanes]

    blend_grad = sum(color_grads[c] * colors[c] for c in range(3))
    before_grad = -(blend_grad * opacity) * transmit
    optical_grad = blend_grad * transmit * (1.0 - opacity) - log_grad
    optical_grad = optical_grad + pick_nn(before_grad, later)
    put_channel(grads_ref, 0, optical_grad * spacing * jax.nn.sigmoid(raw))
    logits = []
    for c in range(3):
        logit = color_grads[c] * blend * colors[c] * (1.0 - colors[c])
        put_channel(grads_ref, 1 + c, logit)
        put_channel(grads_ref, 4 + c, jnp.zeros((tiles, lanes), F32))
        logits.append(pick_nt(total, logit))
    put_channel(grads_ref, 7, jnp.zeros((tiles, lanes), F32))
    dealt = pick_nn(jnp.concatenate(logits, axis=0), place)
    per_cell = []
    for c in range(3):
        row = jnp.sum(mask * dealt[TILE * c : TILE * (c + 1), :], axis=0, keepdims=True)
        per_cell.append(sum(onehots[k] * crossed(row, k) for k in range(crossings)))
    per_cell = jnp.concatenate(per_cell, axis=0)
    map_grads = exact_nn(per_cell, codes.T)
    codes_grad_ref[...] = exact_nn(maps.T, per_cell)
    for v in range(cells):
        for c in range(3):
            sums_ref[v, APP_ROW + c : APP_ROW + c + 1, 0:width] = map_grads[
                cells * c + v : cells * c + v + 1, :
            ]

    def backward(trip, carry):
        some = [trip * UNROLL + u for u in range(UNROLL)]
        owner = [tile_cell_ref[0, t] for t in some]
        outputs = [get_tile(grads_ref, t).astype(BF16) for t in some]
        second_grads = [dot_nn(head_turned_ref[v], output) for v, output in zip(owner, outputs)]
        second_grads = [
            jnp.where(second_ref[t].astype(F32) > 0, grad, 0.0).astype(BF16)
            for t, grad in zip(some, second_grads)
        ]
        first_grads = [dot_nn(backward2_ref[v], grad) for v, grad in zip(owner, second_grads)]
        first_grads = [
            jnp.where(first_ref[t].astype(F32) > 0, grad, 0.0).astype(BF16)
            for t, grad in zip(some, first_grads)
        ]
        head_parts = [dot_nt(output, second_ref[t]) for t, output in zip(some, outputs)]
        second_parts = [dot_nt(first_ref[t], grad) for t, grad in zip(some, second_grads)]
        first_parts = [dot_nt(encoded_ref[t], grad) for t, grad in zip(some, first_grads)]
        for v, head, second, first in zip(owner, head_parts, second_parts, first_parts):
            sums_ref[v, HEAD_ROW:ROWS, :] += head
            sums_ref[v, 128:256, :] += second
            sums_ref[v, 0:128, :] += first
        return carry

    lax.fori_loop(0, trips, backward, 0)
    num_cell = cells // 4
    copies = []
    for district in range(4):
        members = sums_ref.at[pl.ds(district * num_cell, num_cell)]
        total = sums_ref[district * num_cell]
        for s in range(1, num_cell):
            total = total + sums_ref[district * num_cell + s]
        sums_ref[cells + district] = total
        out_ref = (keep_ref, send_ref)[district // 2]
        at = (district % 2) * (num_cell + 1)
        for n, (source, sink) in enumerate(
            [
                (members, out_ref.at[pl.ds(at, num_cell)]),
                (sums_ref.at[cells + district], out_ref.at[at + num_cell]),
            ]
        ):
            copies.append(
                pltpu.make_async_copy(source, sink, semaphore.at[district * 2 + n])
            )
    for copy in copies:
        copy.start()
    for copy in copies:
        copy.wait()


def resident(
    ray_geometry,
    segment_length,
    jitter,
    appearance_codes,
    target,
    crossing,
    frequencies,
    cell_layers,
    district_prior,
    head_weight,
    appearance_weight,
):
    num_cell = lax.axis_size("cell")
    num_district = lax.axis_size("district")
    cells = num_cell * num_district
    rays, crossings = crossing.shape
    samples = jitter.shape[1] // crossings
    segments = rays * crossings
    width = appearance_codes.shape[1]
    lanes = TILE * samples
    tiles = -(-(segments // TILE + cells) // UNROLL) * UNROLL
    me_cell, me_district = lax.axis_index("cell"), lax.axis_index("district")

    def along_cell(x, steps):
        return lax.ppermute(x, "cell", [(i, (i + steps) % num_cell) for i in range(num_cell)])

    def flip(x, bit):
        return lax.ppermute(x, "district", [(i, i ^ bit) for i in range(num_district)])

    own = pl.pallas_call(
        pack_kernel, out_shape=jax.ShapeDtypeStruct((ROWS, 128), F32), name="pack"
    )(cell_layers, district_prior, head_weight, jnp.transpose(appearance_weight, (1, 0, 2)))
    vmem, smem = pl.BlockSpec(memory_space=pltpu.VMEM), pl.BlockSpec(memory_space=pltpu.SMEM)
    anywhere = pl.BlockSpec(memory_space=pl.ANY)
    params = pltpu.CompilerParams(vmem_limit_bytes=VMEM_LIMIT)

    near = [own] + [along_cell(own, s) for s in range(1, num_cell)]
    flipped = [flip(piece, 2) for piece in near]
    weights = near + flipped + [flip(piece, 1) for piece in near + flipped]

    away = (crossing % num_district) ^ me_district
    steps = (me_cell - crossing // num_district) % num_cell
    virtual = (((away & 1) * 2 + (away >> 1)) * num_cell + steps).T
    halves = lanes // 128
    meta, spacing, tile_cell, tile_start, position, factor = pl.pallas_call(
        functools.partial(deal_kernel, cells, samples),
        out_shape=[
            jax.ShapeDtypeStruct((8, segments), F32),
            jax.ShapeDtypeStruct((tiles, lanes), F32),
            jax.ShapeDtypeStruct((8, 256), jnp.int32),
            jax.ShapeDtypeStruct((cells + 8, 128), jnp.int32),
            jax.ShapeDtypeStruct((halves, tiles * 8, 128), F32),
            jax.ShapeDtypeStruct((128, 48), BF16),
        ],
        compiler_params=params,
        cost_estimate=pl.CostEstimate(flops=6 << 30, bytes_accessed=4 << 20, transcendentals=0),
        name="deal",
    )(virtual, ray_geometry, segment_length.T, jitter, frequencies)

    half = 2 * (num_cell + 1)
    rendered, codes_grad, keep, send = pl.pallas_call(
        functools.partial(step_kernel, cells, samples),
        in_specs=[smem, smem] + [vmem] * (7 + cells),
        out_specs=[vmem, vmem, anywhere, anywhere],
        out_shape=[
            jax.ShapeDtypeStruct((3, rays), F32),
            jax.ShapeDtypeStruct((width, rays), F32),
            jax.ShapeDtypeStruct((half, ROWS, 128), F32),
            jax.ShapeDtypeStruct((half, ROWS, 128), F32),
        ],
        scratch_shapes=[
            pltpu.VMEM((tiles, 128, lanes), BF16),
            pltpu.VMEM((tiles, 128, lanes), BF16),
            pltpu.VMEM((tiles, 128, lanes), BF16),
            pltpu.VMEM((cells, 128, 128), BF16),
            pltpu.VMEM((cells, 128, 128), BF16),
            pltpu.VMEM((cells, 128, 128), BF16),
            pltpu.VMEM((cells, 8, 128), BF16),
            pltpu.VMEM((cells, 128, 8), BF16),
            pltpu.VMEM((halves, tiles * 8, 128), F32),
            pltpu.VMEM((halves, tiles * 8, 128), F32),
            pltpu.VMEM((cells + 4, ROWS, 128), F32),
            pltpu.SemaphoreType.DMA((8,)),
        ],
        compiler_params=params,
        name="step",
    )(
        tile_cell,
        tile_start,
        meta,
        virtual,
        spacing,
        position,
        factor,
        appearance_codes.T,
        target,
        *weights,
    )

    crossed = flip(send, 1)
    order = [num_cell, num_cell // 2]
    order += [s for s in range(1, num_cell) if s != num_cell // 2] + [0]
    far = num_cell + 1
    pieces = {s: flip(keep[far + s] + crossed[far + s], 2) for s in order}
    for s in order:
        near_part, cross_part, other = lax.optimization_barrier((keep[s], crossed[s], pieces[s]))
        pieces[s] = near_part + cross_part + other
    prior = pieces[num_cell][0:HEAD_ROW]
    bit = 1
    while bit < num_cell:
        prior = prior + lax.ppermute(prior, "cell", [(i, i ^ bit) for i in range(num_cell)])
        bit *= 2
    prior = (prior / num_cell).reshape(2, 128, 128)
    arrived = [along_cell(pieces[s], -s) for s in order[1:-1]]
    own_sum = pieces[0] + sum(arrived)
    return (
        rendered,
        own_sum[0:HEAD_ROW].reshape(1, 2, 128, 128),
        prior[None],
        own_sum[None, HEAD_ROW : HEAD_ROW + 4],
        own_sum[None, APP_ROW : APP_ROW + 3, 0:width],
        codes_grad.T,
    )


def local(*args):
    cells = lax.axis_size("cell") * lax.axis_size("district")
    if cells <= 16 and lax.axis_size("district") == 4:
        return resident(*args)
    return routed(*args)


def solution(mesh):
    placed = (
        P(None, ("scene", "cell", "district")),
        P(("scene", "cell", "district"), None),
        P(("scene", "cell", "district"), None),
        P(("scene", "cell", "district"), None),
        P(None, ("scene", "cell", "district")),
        P(("scene", "cell", "district"), None),
        P(),
        P(("scene", "cell", "district"), None, None, None),
        P(("scene", "district"), None, None, None),
        P(("scene", "cell", "district"), None, None),
        P(("scene", "cell", "district"), None, None),
    )
    return jax.shard_map(
        local,
        mesh=mesh,
        in_specs=placed,
        out_specs=(
            P(None, ("scene", "cell", "district")),
            P(("scene", "cell", "district"), None, None, None),
            P(("scene", "district"), None, None, None),
            P(("scene", "cell", "district"), None, None),
            P(("scene", "cell", "district"), None, None),
            P(("scene", "cell", "district"), None),
        ),
        check_vma=False,
    )
```

```python
import functools

import jax
import jax.numpy as jnp
from jax import lax
from jax.experimental import pallas as pl
from jax.experimental.pallas import tpu as pltpu
from jax.sharding import PartitionSpec as P

GEOMETRY = 8
HIGHEST_PRECISION = lax.Precision.HIGHEST


def build_front(ray_geometry, segment_length, jitter):
    ray_count, crossings = segment_length.shape
    samples = jitter.shape[1] // crossings
    near_depth = jnp.cumsum(segment_length, axis=1) - segment_length
    geometry = jnp.broadcast_to(ray_geometry.T[:, None, :], (ray_count, crossings, 6))
    front = jnp.concatenate(
        [
            geometry,
            near_depth[:, :, None],
            segment_length[:, :, None],
            jitter.reshape(ray_count, crossings, samples),
        ],
        axis=2,
    )
    return front.reshape(ray_count * crossings, front.shape[2])


def slot_positions(crossing, cell_total, capacity):
    target_cell = crossing.reshape(-1)
    total_rows = target_cell.shape[0]
    onehot = target_cell[:, None] == jnp.arange(cell_total, dtype=jnp.int32)[None, :]
    triangle = (
        lax.broadcasted_iota(jnp.int32, (total_rows, total_rows), 0)
        > lax.broadcasted_iota(jnp.int32, (total_rows, total_rows), 1)
    ).astype(jnp.bfloat16)
    earlier = jnp.dot(triangle, onehot.astype(jnp.bfloat16), preferred_element_type=jnp.float32)
    position = jnp.sum(jnp.where(onehot, earlier, 0.0), axis=1).astype(jnp.int32)
    return target_cell * capacity + position


def sample_spacing(payload, samples):
    near_depth = payload[:, 6:7]
    extent = payload[:, 7:8]
    offsets = jnp.arange(samples, dtype=jnp.float32)[None, :]
    depths = near_depth + extent * (offsets + payload[:, GEOMETRY : GEOMETRY + samples]) / samples
    ending = jnp.concatenate([depths[:, 1:], near_depth + extent], axis=1)
    return (depths, ending - depths)


def cell_forward(payload, frequencies, first_weight, second_weight, head_one, samples):
    depths, spacing = sample_spacing(payload, samples)
    phases = jnp.zeros((payload.shape[0], samples, frequencies.shape[1]), jnp.float32)
    for component in range(3):
        position = (
            payload[:, component : component + 1]
            + depths * payload[:, 3 + component : 4 + component]
        )
        phases = phases + position[:, :, None] * frequencies[component][None, None, :]
    encoded = jnp.concatenate([jnp.sin(phases), jnp.cos(phases)], axis=2)
    encoded = encoded.reshape(payload.shape[0] * samples, encoded.shape[2]).astype(jnp.bfloat16)
    first_act = jax.nn.relu(
        jnp.dot(encoded, first_weight, preferred_element_type=jnp.float32)
    ).astype(jnp.bfloat16)
    second_act = jax.nn.relu(
        jnp.dot(first_act, second_weight, preferred_element_type=jnp.float32)
    ).astype(jnp.bfloat16)
    raw_outputs = lax.dot_general(
        head_one, second_act, (((1,), (1,)), ((), ())), preferred_element_type=jnp.float32
    )
    return ((encoded, first_act, second_act, raw_outputs), spacing)


def shade(raw_outputs, payload, spacing, appearance_one, samples):
    slot_count = payload.shape[0]
    outputs = raw_outputs.reshape(4, slot_count, samples)
    code_part = payload[:, GEOMETRY + samples :]
    color_shift = jnp.dot(code_part, appearance_one.T, precision=HIGHEST_PRECISION)
    density = jax.nn.softplus(outputs[0])
    colors = jax.nn.sigmoid(outputs[1:] + color_shift.T[:, :, None])
    optical = density * spacing
    transmit = jnp.exp(-(jnp.cumsum(optical, axis=1) - optical))
    opacity = 1.0 - jnp.exp(-optical)
    blend_weight = transmit * opacity
    return (outputs, colors, optical, transmit, opacity, blend_weight, code_part)


def segment_partials(raw_outputs, payload, spacing, appearance_one, samples):
    shaded = shade(raw_outputs, payload, spacing, appearance_one, samples)
    colors, optical, blend_weight = (shaded[1], shaded[2], shaded[5])
    segment_color = jnp.sum(blend_weight[None] * colors, axis=2)
    segment_log = -jnp.sum(optical, axis=1)
    return jnp.concatenate([segment_color.T, segment_log[:, None]], axis=1)


def cell_backward(
    payload, saved_acts, spacing, cotangent, second_weight, head_one, appearance_one, samples
):
    encoded, first_act, second_act, raw_outputs = saved_acts
    outputs, colors, optical, transmit, opacity, blend_weight, code_part = shade(
        raw_outputs, payload, spacing, appearance_one, samples
    )
    color_grad = cotangent[:, :3].T
    log_grad = cotangent[:, 3]
    blend_grad = jnp.sum(color_grad[:, :, None] * colors, axis=0)
    colors_grad = color_grad[:, :, None] * blend_weight[None]
    transmit_grad = blend_grad * opacity
    optical_grad = blend_grad * transmit * (1.0 - opacity) - log_grad[:, None]
    before_grad = -transmit_grad * transmit
    later_sum = jnp.flip(jnp.cumsum(jnp.flip(before_grad, axis=1), axis=1), axis=1) - before_grad
    optical_grad = optical_grad + later_sum
    density_grad = optical_grad * spacing * jax.nn.sigmoid(outputs[0])
    logit_grad = colors_grad * colors * (1.0 - colors)
    slot_count = payload.shape[0]
    output_grad = (
        jnp.concatenate([density_grad[None], logit_grad], axis=0)
        .reshape(4, slot_count * samples)
        .astype(jnp.bfloat16)
    )
    head_grad = jnp.dot(output_grad, second_act, preferred_element_type=jnp.float32)
    shift_grad = jnp.sum(logit_grad, axis=2)
    second_grad = lax.dot_general(
        output_grad, head_one, (((0,), (0,)), ((), ())), preferred_element_type=jnp.float32
    )
    second_grad = jnp.where(second_act > 0, second_grad, 0.0).astype(jnp.bfloat16)
    second_weight_grad = lax.dot_general(
        first_act, second_grad, (((0,), (0,)), ((), ())), preferred_element_type=jnp.float32
    )
    first_grad = lax.dot_general(
        second_grad, second_weight, (((1,), (1,)), ((), ())), preferred_element_type=jnp.float32
    )
    first_grad = jnp.where(first_act > 0, first_grad, 0.0).astype(jnp.bfloat16)
    first_weight_grad = lax.dot_general(
        encoded, first_grad, (((0,), (0,)), ((), ())), preferred_element_type=jnp.float32
    )
    return (first_weight_grad, second_weight_grad, head_grad, shift_grad, code_part)


def composite(gathered, target):
    segment_color = gathered[:, :, :3]
    segment_log = gathered[:, :, 3]
    reach_weight = jnp.exp(jnp.cumsum(segment_log, axis=1) - segment_log)
    rendered = jnp.sum(reach_weight[:, :, None] * segment_color, axis=1).T
    residual = rendered - target
    color_grad = reach_weight[:, :, None] * residual.T[:, None, :]
    reach_grad = jnp.sum(residual.T[:, None, :] * segment_color, axis=2) * reach_weight
    log_grad = jnp.flip(jnp.cumsum(jnp.flip(reach_grad, axis=1), axis=1), axis=1) - reach_grad
    return (rendered, jnp.concatenate([color_grad, log_grad[:, :, None]], axis=2))


def routed(
    ray_geometry,
    segment_length,
    jitter,
    appearance_codes,
    target,
    crossing,
    frequencies,
    cell_layers,
    district_prior,
    head_weight,
    appearance_weight,
):
    num_cell = lax.axis_size("cell")
    num_district = lax.axis_size("district")
    cell_total = num_cell * num_district
    ray_count, crossings = crossing.shape
    samples = jitter.shape[1] // crossings
    segments = ray_count * crossings
    capacity = 2 * segments // cell_total
    slot_total = cell_total * capacity
    code_width = appearance_codes.shape[1]
    front = build_front(ray_geometry, segment_length, jitter)
    codes_seg = jnp.broadcast_to(
        appearance_codes[:, None, :], (ray_count, crossings, code_width)
    ).reshape(segments, code_width)
    payload = jnp.concatenate([front, codes_seg], axis=1)
    appearance_one = appearance_weight[0]
    row_width = payload.shape[1]
    places = slot_positions(crossing, cell_total, capacity)
    outbox = (
        jnp.zeros((slot_total, row_width), jnp.float32)
        .at[places]
        .set(payload)
        .reshape(cell_total, capacity * row_width)
    )
    arrived = lax.all_to_all(outbox, ("cell", "district"), split_axis=0, concat_axis=0, tiled=True)
    arrived = arrived.reshape(slot_total, row_width)
    effective = (cell_layers[0].astype(jnp.float32) + district_prior[0].astype(jnp.float32)).astype(
        jnp.bfloat16
    )
    head_one = head_weight[0]
    block_rows = min(512, slot_total)
    blocked = arrived.reshape(slot_total // block_rows, block_rows, row_width)

    def forward_keep(slot_rows):
        saved_acts, spacing = cell_forward(
            slot_rows, frequencies, effective[0], effective[1], head_one, samples
        )
        return (
            segment_partials(saved_acts[3], slot_rows, spacing, appearance_one, samples),
            saved_acts,
        )

    partials, stored = lax.map(forward_keep, blocked)
    partials = partials.reshape(cell_total, capacity * 4)
    returned = lax.all_to_all(
        partials, ("cell", "district"), split_axis=0, concat_axis=0, tiled=True
    )
    returned = returned.reshape(slot_total, 4)
    rendered, cotangent = composite(returned[places].reshape(ray_count, crossings, 4), target)
    grad_box = (
        jnp.zeros((slot_total, 4), jnp.float32)
        .at[places]
        .set(cotangent.reshape(segments, 4))
        .reshape(cell_total, capacity * 4)
    )
    incoming = lax.all_to_all(
        grad_box, ("cell", "district"), split_axis=0, concat_axis=0, tiled=True
    )
    incoming = incoming.reshape(slot_total // block_rows, block_rows, 4)

    def finish(result):
        first_part, second_part, head_part, shift_grad, code_part = result
        appearance_part = jnp.dot(shift_grad, code_part, precision=HIGHEST_PRECISION)
        code_part_grad = jnp.dot(shift_grad.T, appearance_one, precision=HIGHEST_PRECISION)
        return (first_part, second_part, head_part, appearance_part, code_part_grad)

    def backward_keep(bundle):
        slot_rows, incoming_rows, saved_acts = bundle
        spacing = sample_spacing(slot_rows, samples)[1]
        return finish(
            cell_backward(
                slot_rows,
                saved_acts,
                spacing,
                incoming_rows,
                effective[1],
                head_one,
                appearance_one,
                samples,
            )
        )

    pieces = lax.map(backward_keep, (blocked, incoming, stored))
    first_w = jnp.sum(pieces[0], axis=0)
    second_w = jnp.sum(pieces[1], axis=0)
    head_grad = jnp.sum(pieces[2], axis=0)
    appearance_grad = jnp.sum(pieces[3], axis=0)
    code_box = pieces[4].reshape(cell_total, capacity * code_width)
    code_back = lax.all_to_all(
        code_box, ("cell", "district"), split_axis=0, concat_axis=0, tiled=True
    )
    code_back = code_back.reshape(slot_total, code_width)
    grad_codes = jnp.sum(code_back[places].reshape(ray_count, crossings, code_width), axis=1)
    grad_pair = jnp.stack([first_w, second_w], axis=0)
    grad_prior = lax.psum(grad_pair, "cell") / num_cell
    return (
        rendered,
        grad_pair[None],
        grad_prior[None],
        head_grad[None],
        appearance_grad[None],
        grad_codes,
    )


TILE = 8
UNROLL = 16
ROWS = 264
HEAD_ROW = 256
APP_ROW = 260
VMEM_LIMIT = 56 * 1024 * 1024
COS = (
    0.9999992251396179,
    -19.738981246948242,
    64.92865753173828,
    -85.27162170410156,
    58.79049301147461,
    -21.07110595703125,
)
F32 = jnp.float32
BF16 = jnp.bfloat16


def iota(shape, axis):
    return lax.broadcasted_iota(jnp.int32, shape, axis)


def dot_nn(a, b):
    return jnp.dot(a, b, preferred_element_type=F32)


def dot_nt(a, b):
    return lax.dot_general(a, b, (((1,), (1,)), ((), ())), preferred_element_type=F32)


def split3(x):
    high = x.astype(BF16)
    rest = x - high.astype(F32)
    mid = rest.astype(BF16)
    low = (rest - mid.astype(F32)).astype(BF16)
    return high, mid, low


def pick_nn(x, select):
    high, mid, low = split3(x)
    return (dot_nn(low, select) + dot_nn(mid, select)) + dot_nn(high, select)


def pick_nt(select, x):
    high, mid, low = split3(x)
    return (dot_nt(select, low) + dot_nt(select, mid)) + dot_nt(select, high)


def exact_nn(a, b):
    return jnp.dot(a, b, precision=HIGHEST_PRECISION, preferred_element_type=F32)


def put_channel(ref, c, x):
    for h in range(ref.shape[0]):
        ref[h, pl.ds(c, x.shape[0], 8), :] = x[:, 128 * h : 128 * (h + 1)]


def get_channel(ref, c):
    tiles = ref.shape[1] // 8
    return jnp.concatenate([ref[h, pl.ds(c, tiles, 8), :] for h in range(ref.shape[0])], axis=1)


def get_tile(ref, t):
    rows = pl.ds(pl.multiple_of(t * 8, 8), 8)
    return jnp.concatenate([ref[h, rows, :] for h in range(ref.shape[0])], axis=1)


def put_tile(ref, t, x):
    rows = pl.ds(pl.multiple_of(t * 8, 8), 8)
    for h in range(ref.shape[0]):
        ref[h, rows, :] = x[:, 128 * h : 128 * (h + 1)]


def pack_kernel(layers_ref, prior_ref, head_ref, app_ref, out_ref, again_ref):
    for layer in range(2):
        both = layers_ref[0, layer].astype(F32) + prior_ref[0, layer].astype(F32)
        out_ref[128 * layer : 128 * (layer + 1), :] = both.T
    out_ref[HEAD_ROW:ROWS, :] = jnp.zeros((ROWS - HEAD_ROW, 128), F32)
    out_ref[HEAD_ROW : HEAD_ROW + 4, :] = head_ref[0].astype(F32)
    for c in range(3):
        out_ref[APP_ROW + c : APP_ROW + c + 1, 0 : app_ref.shape[2]] = app_ref[c]
    again_ref[...] = out_ref[...]


def slot_mask(place_row):
    return (iota((TILE, place_row.shape[1]), 0) == place_row.astype(jnp.int32)).astype(F32)


def tile_onehot(tile_row, tiles):
    return (iota((tiles, tile_row.shape[1]), 0) == tile_row.astype(jnp.int32)).astype(F32).astype(BF16)


def cell_onehot(cells_ref, cells):
    return [
        (iota((cells, cells_ref.shape[1]), 0) == cells_ref[k : k + 1, :]).astype(F32)
        for k in range(cells_ref.shape[0])
    ]


def lane_select(channels, lanes):
    rows = channels * TILE
    row, column = iota((rows, channels * lanes), 0), iota((rows, channels * lanes), 1)
    same = (row // TILE == column // lanes) & (row % TILE == column % TILE)
    return same.astype(F32).astype(BF16)


def deal_kernel(
    cells,
    samples,
    cells_ref,
    geometry_ref,
    length_ref,
    jitter_ref,
    frequency_ref,
    own_ref,
    meta_ref,
    spacing_ref,
    tile_cell_ref,
    tile_start_ref,
    position_ref,
    factor_ref,
    passed_ref,
):
    del own_ref, passed_ref
    tiles = spacing_ref.shape[0]
    lanes = TILE * samples
    crossings, rays = cells_ref.shape
    segments = crossings * rays

    onehot = jnp.concatenate(cell_onehot(cells_ref, cells), axis=1)
    chunks = [onehot[:, 128 * c : 128 * (c + 1)] for c in range(segments // 128)]
    before = (iota((128, 128), 0) < iota((128, 128), 1)).astype(F32).astype(BF16)
    prefix = dot_nn(jnp.concatenate(chunks, axis=0).astype(BF16), before)
    running = jnp.zeros((cells, 1), F32)
    ranks = []
    for c, chunk in enumerate(chunks):
        earlier = prefix[cells * c : cells * (c + 1), :] + running
        ranks.append(jnp.sum(chunk * earlier, axis=0, keepdims=True))
        running = running + jnp.sum(chunk, axis=1, keepdims=True)
    rank = jnp.concatenate(ranks, axis=1)
    needed = jnp.broadcast_to(jnp.floor((running + (TILE - 1)) * (1.0 / TILE)), (cells, 128))
    lower = (iota((cells, cells), 1) < iota((cells, cells), 0)).astype(F32).astype(BF16)
    start = dot_nn(lower, needed.astype(BF16))
    inside = jnp.floor(rank * (1.0 / TILE))
    tile_row = jnp.sum(onehot * start[:, 0:1], axis=0, keepdims=True) + inside
    place_row = rank - inside * TILE
    meta_ref[...] = jnp.concatenate(
        [tile_row, place_row, jnp.zeros((6, segments), F32)], axis=0
    )
    ends = start[:, 0:1] + needed[:, 0:1]
    owner = jnp.sum(
        (ends <= iota((cells, tile_cell_ref.shape[1]), 1).astype(F32)).astype(F32),
        axis=0,
        keepdims=True,
    )
    owner = jnp.minimum(owner, cells - 1.0).astype(jnp.int32)
    tile_cell_ref[...] = jnp.broadcast_to(owner, tile_cell_ref.shape)
    tile_start_ref[0:cells, :] = start.astype(jnp.int32)
    tile_start_ref[cells : cells + 8, :] = jnp.broadcast_to(
        ends[cells - 1 : cells, :], (8, 128)
    ).astype(jnp.int32)

    mask = slot_mask(place_row)
    place = tile_onehot(tile_row, tiles)
    lengths = length_ref[...]
    near = jnp.zeros((1, rays), F32)
    nears, extents = [], []
    for k in range(crossings):
        nears.append(near)
        extents.append(lengths[k : k + 1, :])
        near = near + lengths[k : k + 1, :]
    rows = [
        jnp.concatenate([geometry_ref[c : c + 1, :]] * crossings, axis=1) for c in range(6)
    ]
    rows += [jnp.concatenate(nears, axis=1), jnp.concatenate(extents, axis=1)]
    wide = pick_nt(place, jnp.concatenate([mask * row for row in rows], axis=0))
    wide = pick_nn(wide, lane_select(8, lanes))
    channel = [wide[:, lanes * c : lanes * (c + 1)] for c in range(8)]
    turned = jitter_ref[...].T
    offsets = jnp.concatenate(
        [turned[samples * k : samples * (k + 1), :] for k in range(crossings)], axis=1
    )
    dealt = jnp.concatenate([mask * offsets[i : i + 1, :] for i in range(samples)], axis=0)
    jitter = pick_nt(place, dealt)
    step = (iota((tiles, lanes), 1) // TILE).astype(F32)
    near, extent = channel[6], channel[7]
    depths = near + extent * (step + jitter) / samples
    following = pltpu.roll(depths, lanes - TILE, 1)
    ending = jnp.where(iota((tiles, lanes), 1) >= lanes - TILE, near + extent, following)
    spacing_ref[...] = ending - depths
    for c in range(3):
        put_channel(position_ref, c, channel[c] + depths * channel[3 + c])
    put_channel(position_ref, 3, jnp.ones((tiles, lanes), F32))
    for c in range(4, 8):
        put_channel(position_ref, c, jnp.zeros((tiles, lanes), F32))
    turns = frequency_ref[...] * 0.15915494309189535
    turns = jnp.concatenate([turns, turns], axis=1)
    features = turns.shape[1]
    quarter = jnp.where(iota((1, features), 1) < features // 2, -0.25, 0.0)
    block = jnp.concatenate([turns, quarter, jnp.zeros((4, features), F32)], axis=0)
    high, mid, low = [part.astype(F32) for part in split3(block)]
    stack = [high, high, high, mid, mid, low, jnp.zeros((features - 48, features), F32)]
    factor_ref[...] = jnp.concatenate(stack, axis=0).T[:, 0:48].astype(BF16)


def encode(position_ref, factor, encoded_ref, some):
    phases = []
    for t in some:
        high, mid, low = split3(get_tile(position_ref, t))
        high, mid, low = high.astype(F32), mid.astype(F32), low.astype(F32)
        points = jnp.concatenate([high, mid, low, high, mid, high], axis=0).astype(BF16)
        phases.append(dot_nn(factor, points))
    for t, phase in zip(some, phases):
        phase = phase - jnp.round(phase)
        square = phase * phase
        value = square * COS[5] + COS[4]
        for c in (3, 2, 1, 0):
            value = value * square + COS[c]
        encoded_ref[t] = value.astype(BF16)


def step_kernel(
    cells,
    samples,
    tile_cell_ref,
    tile_start_ref,
    meta_ref,
    cells_ref,
    spacing_ref,
    position_ref,
    factor_ref,
    codes_ref,
    target_ref,
    *refs,
):
    weights, refs = refs[:cells], refs[cells:]
    (
        rendered_ref,
        codes_grad_ref,
        keep_ref,
        send_ref,
        encoded_ref,
        first_ref,
        second_ref,
        forward1_ref,
        forward2_ref,
        backward2_ref,
        head_ref,
        head_turned_ref,
        outputs_ref,
        grads_ref,
        sums_ref,
        semaphore,
    ) = refs
    tiles, lanes = spacing_ref.shape
    crossings, rays = cells_ref.shape
    segments = crossings * rays
    width = codes_ref.shape[0]
    used = tile_start_ref[cells, 0]
    trips = (used + UNROLL - 1) // UNROLL

    appearance = []
    for v, ref in enumerate(weights):
        forward1_ref[v] = ref[0:128, :].astype(BF16)
        second = ref[128:256, :]
        forward2_ref[v] = second.astype(BF16)
        backward2_ref[v] = second.T.astype(BF16)
        tail = ref[HEAD_ROW:ROWS, :]
        head = jnp.where(iota((8, 128), 0) < 4, tail, 0.0)
        head_ref[v] = head.astype(BF16)
        square = jnp.concatenate([head, jnp.zeros((120, 128), F32)], axis=0)
        head_turned_ref[v] = square.T[:, 0:8].astype(BF16)
        appearance.append(tail)
    outputs_ref[...] = jnp.zeros_like(outputs_ref)
    sums_ref[...] = jnp.zeros_like(sums_ref)

    factor = factor_ref[...]
    encode(position_ref, factor, encoded_ref, range(UNROLL))

    def forward(trip, carry):
        following = jnp.minimum(trip + 1, trips - 1) * UNROLL
        some = [trip * UNROLL + u for u in range(UNROLL)]
        owner = [tile_cell_ref[0, t] for t in some]
        firsts = [dot_nn(forward1_ref[v], encoded_ref[t]) for t, v in zip(some, owner)]
        firsts = [jnp.maximum(first, 0.0).astype(BF16) for first in firsts]
        for t, first in zip(some, firsts):
            first_ref[t] = first
        seconds = [dot_nn(forward2_ref[v], first) for v, first in zip(owner, firsts)]
        seconds = [jnp.maximum(second, 0.0).astype(BF16) for second in seconds]
        for t, second in zip(some, seconds):
            second_ref[t] = second
        outputs = [dot_nn(head_ref[v], second) for v, second in zip(owner, seconds)]
        for t, output in zip(some, outputs):
            put_tile(outputs_ref, t, output)
        encode(position_ref, factor, encoded_ref, [following + u for u in range(UNROLL)])
        return carry

    lax.fori_loop(0, trips, forward, 0)

    tile_row, place_row = meta_ref[0:1, :], meta_ref[1:2, :]
    mask = slot_mask(place_row)
    place = tile_onehot(tile_row, tiles)
    onehots = cell_onehot(cells_ref, cells)
    maps = jnp.concatenate(
        [jnp.concatenate([tail[4 + c : 5 + c, :] for tail in appearance], axis=0) for c in range(3)],
        axis=0,
    )[:, 0:width]
    codes = codes_ref[...]
    shifts = exact_nn(maps, codes)
    rows = [
        jnp.concatenate(
            [
                jnp.sum(onehots[k] * shifts[cells * c : cells * (c + 1), :], axis=0, keepdims=True)
                for k in range(crossings)
            ],
            axis=1,
        )
        for c in range(3)
    ]
    spread3 = lane_select(4, lanes)
    shift = pick_nt(place, jnp.concatenate([mask * row for row in rows], axis=0))
    shift = pick_nn(shift, spread3[0:24, 0 : 3 * lanes])

    spacing = spacing_ref[...]
    raw = get_channel(outputs_ref, 0)
    ray = (iota((lanes, lanes), 0) % TILE) == (iota((lanes, lanes), 1) % TILE)
    earlier = (ray & (iota((lanes, lanes), 0) < iota((lanes, lanes), 1))).astype(F32).astype(BF16)
    later = (ray & (iota((lanes, lanes), 0) > iota((lanes, lanes), 1))).astype(F32).astype(BF16)
    total = ((iota((TILE, lanes), 1) % TILE) == iota((TILE, lanes), 0)).astype(F32).astype(BF16)
    density = jax.nn.softplus(raw)
    colors = [
        jax.nn.sigmoid(
            get_channel(outputs_ref, 1 + c) + shift[:, lanes * c : lanes * (c + 1)]
        )
        for c in range(3)
    ]
    optical = density * spacing
    transmit = jnp.exp(-pick_nn(optical, earlier))
    opacity = 1.0 - jnp.exp(-optical)
    blend = transmit * opacity
    sums = [pick_nt(total, blend * color) for color in colors] + [-pick_nt(total, optical)]
    dealt = pick_nn(jnp.concatenate(sums, axis=0), place)
    parts = [
        jnp.sum(mask * dealt[TILE * c : TILE * (c + 1), :], axis=0, keepdims=True) for c in range(4)
    ]

    def crossed(row, k):
        return row[:, rays * k : rays * (k + 1)]

    reach, logs = [], jnp.zeros((1, rays), F32)
    for k in range(crossings):
        reach.append(jnp.exp(logs))
        logs = logs + crossed(parts[3], k)
    residuals, channel_grads = [], [[] for _ in range(3)]
    for c in range(3):
        rendered = sum(reach[k] * crossed(parts[c], k) for k in range(crossings))
        rendered_ref[c : c + 1, :] = rendered
        residuals.append(rendered - target_ref[c : c + 1, :])
    log_grads, after = [], jnp.zeros((1, rays), F32)
    for k in reversed(range(crossings)):
        log_grads.append(after)
        weight = sum(residuals[c] * crossed(parts[c], k) for c in range(3))
        after = after + weight * reach[k]
    log_row = jnp.concatenate(log_grads[::-1], axis=1)
    color_rows = [
        jnp.concatenate([reach[k] * residuals[c] for k in range(crossings)], axis=1)
        for c in range(3)
    ]
    back = pick_nt(place, jnp.concatenate([mask * row for row in color_rows + [log_row]], axis=0))
    back = pick_nn(back, spread3)
    color_grads = [back[:, lanes * c : lanes * (c + 1)] for c in range(3)]
    log_grad = back[:, 3 * lanes : 4 * lanes]

    blend_grad = sum(color_grads[c] * colors[c] for c in range(3))
    before_grad = -(blend_grad * opacity) * transmit
    optical_grad = blend_grad * transmit * (1.0 - opacity) - log_grad
    optical_grad = optical_grad + pick_nn(before_grad, later)
    put_channel(grads_ref, 0, optical_grad * spacing * jax.nn.sigmoid(raw))
    logits = []
    for c in range(3):
        logit = color_grads[c] * blend * colors[c] * (1.0 - colors[c])
        put_channel(grads_ref, 1 + c, logit)
        put_channel(grads_ref, 4 + c, jnp.zeros((tiles, lanes), F32))
        logits.append(pick_nt(total, logit))
    put_channel(grads_ref, 7, jnp.zeros((tiles, lanes), F32))
    dealt = pick_nn(jnp.concatenate(logits, axis=0), place)
    per_cell = []
    for c in range(3):
        row = jnp.sum(mask * dealt[TILE * c : TILE * (c + 1), :], axis=0, keepdims=True)
        per_cell.append(sum(onehots[k] * crossed(row, k) for k in range(crossings)))
    per_cell = jnp.concatenate(per_cell, axis=0)
    map_grads = exact_nn(per_cell, codes.T)
    codes_grad_ref[...] = exact_nn(maps.T, per_cell)
    for v in range(cells):
        for c in range(3):
            sums_ref[v, APP_ROW + c : APP_ROW + c + 1, 0:width] = map_grads[
                cells * c + v : cells * c + v + 1, :
            ]

    def backward(trip, carry):
        some = [trip * UNROLL + u for u in range(UNROLL)]
        owner = [tile_cell_ref[0, t] for t in some]
        outputs = [get_tile(grads_ref, t).astype(BF16) for t in some]
        second_grads = [dot_nn(head_turned_ref[v], output) for v, output in zip(owner, outputs)]
        second_grads = [
            jnp.where(second_ref[t] > 0, grad.astype(BF16), jnp.zeros((), BF16))
            for t, grad in zip(some, second_grads)
        ]
        first_grads = [dot_nn(backward2_ref[v], grad) for v, grad in zip(owner, second_grads)]
        first_grads = [
            jnp.where(first_ref[t] > 0, grad.astype(BF16), jnp.zeros((), BF16))
            for t, grad in zip(some, first_grads)
        ]
        head_parts = [dot_nt(output, second_ref[t]) for t, output in zip(some, outputs)]
        second_parts = [dot_nt(first_ref[t], grad) for t, grad in zip(some, second_grads)]
        first_parts = [dot_nt(encoded_ref[t], grad) for t, grad in zip(some, first_grads)]
        for v, head, second, first in zip(owner, head_parts, second_parts, first_parts):
            sums_ref[v, HEAD_ROW:ROWS, :] += head
            sums_ref[v, 128:256, :] += second
            sums_ref[v, 0:128, :] += first
        return carry

    lax.fori_loop(0, trips, backward, 0)
    num_cell = cells // 4
    copies = []
    for district in range(4):
        members = sums_ref.at[pl.ds(district * num_cell, num_cell)]
        total = sums_ref[district * num_cell]
        for s in range(1, num_cell):
            total = total + sums_ref[district * num_cell + s]
        sums_ref[cells + district] = total
        out_ref = (keep_ref, send_ref)[district // 2]
        at = (district % 2) * (num_cell + 1)
        for n, (source, sink) in enumerate(
            [
                (members, out_ref.at[pl.ds(at, num_cell)]),
                (sums_ref.at[cells + district], out_ref.at[at + num_cell]),
            ]
        ):
            copies.append(
                pltpu.make_async_copy(source, sink, semaphore.at[district * 2 + n])
            )
    for copy in copies:
        copy.start()
    for copy in copies:
        copy.wait()


def resident(
    ray_geometry,
    segment_length,
    jitter,
    appearance_codes,
    target,
    crossing,
    frequencies,
    cell_layers,
    district_prior,
    head_weight,
    appearance_weight,
):
    num_cell = lax.axis_size("cell")
    num_district = lax.axis_size("district")
    cells = num_cell * num_district
    rays, crossings = crossing.shape
    samples = jitter.shape[1] // crossings
    segments = rays * crossings
    width = appearance_codes.shape[1]
    lanes = TILE * samples
    tiles = -(-(segments // TILE + cells) // UNROLL) * UNROLL
    me_cell, me_district = lax.axis_index("cell"), lax.axis_index("district")

    def flip(x, bits, axis="district"):
        return lax.ppermute(x, axis, [(i, i ^ bits) for i in range(lax.axis_size(axis))])

    own, again = pl.pallas_call(
        pack_kernel, out_shape=[jax.ShapeDtypeStruct((ROWS, 128), F32)] * 2, name="pack"
    )(cell_layers, district_prior, head_weight, jnp.transpose(appearance_weight, (1, 0, 2)))
    vmem, smem = pl.BlockSpec(memory_space=pltpu.VMEM), pl.BlockSpec(memory_space=pltpu.SMEM)
    anywhere = pl.BlockSpec(memory_space=pl.ANY)
    params = pltpu.CompilerParams(vmem_limit_bytes=VMEM_LIMIT)

    away = (crossing % num_district) ^ me_district
    steps = (crossing // num_district) ^ me_cell
    virtual = (((away & 1) * 2 + (away >> 1)) * num_cell + steps).T
    halves = lanes // 128
    default = pl.BlockSpec()
    meta, spacing, tile_cell, tile_start, position, factor, passed = pl.pallas_call(
        functools.partial(deal_kernel, cells, samples),
        in_specs=[default] * 5 + [anywhere],
        out_specs=[default] * 6 + [anywhere],
        input_output_aliases={5: 6},
        out_shape=[
            jax.ShapeDtypeStruct((8, segments), F32),
            jax.ShapeDtypeStruct((tiles, lanes), F32),
            jax.ShapeDtypeStruct((8, 256), jnp.int32),
            jax.ShapeDtypeStruct((cells + 8, 128), jnp.int32),
            jax.ShapeDtypeStruct((halves, tiles * 8, 128), F32),
            jax.ShapeDtypeStruct((128, 48), BF16),
            jax.ShapeDtypeStruct((ROWS, 128), F32),
        ],
        compiler_params=params,
        cost_estimate=pl.CostEstimate(flops=6 << 30, bytes_accessed=4 << 20, transcendentals=0),
        name="deal",
    )(virtual, ray_geometry, segment_length.T, jitter, frequencies, again)
    near = [own]
    for s in range(1, num_cell):
        near.append(flip(near[s & (s - 1)] if s > 1 else passed, s & -s, "cell"))
    flipped = [flip(piece, 2) for piece in near]
    weights = near + flipped + [flip(piece, 1) for piece in near + flipped]


    half = 2 * (num_cell + 1)
    rendered, codes_grad, keep, send = pl.pallas_call(
        functools.partial(step_kernel, cells, samples),
        in_specs=[smem, smem] + [vmem] * (7 + cells),
        out_specs=[vmem, vmem, anywhere, anywhere],
        out_shape=[
            jax.ShapeDtypeStruct((3, rays), F32),
            jax.ShapeDtypeStruct((width, rays), F32),
            jax.ShapeDtypeStruct((half, ROWS, 128), F32),
            jax.ShapeDtypeStruct((half, ROWS, 128), F32),
        ],
        scratch_shapes=[
            pltpu.VMEM((tiles, 128, lanes), BF16),
            pltpu.VMEM((tiles, 128, lanes), BF16),
            pltpu.VMEM((tiles, 128, lanes), BF16),
            pltpu.VMEM((cells, 128, 128), BF16),
            pltpu.VMEM((cells, 128, 128), BF16),
            pltpu.VMEM((cells, 128, 128), BF16),
            pltpu.VMEM((cells, 8, 128), BF16),
            pltpu.VMEM((cells, 128, 8), BF16),
            pltpu.VMEM((halves, tiles * 8, 128), F32),
            pltpu.VMEM((halves, tiles * 8, 128), F32),
            pltpu.VMEM((cells + 4, ROWS, 128), F32),
            pltpu.SemaphoreType.DMA((8,)),
        ],
        compiler_params=params,
        name="step",
    )(
        tile_cell,
        tile_start,
        meta,
        virtual,
        spacing,
        position,
        factor,
        appearance_codes.T,
        target,
        *weights,
    )

    crossed = flip(send, 1)
    order = [num_cell, num_cell // 2]
    order += [s for s in range(1, num_cell) if s != num_cell // 2] + [0]
    far = num_cell + 1
    pieces = {s: flip(keep[far + s] + crossed[far + s], 2) for s in order}
    for s in order:
        near_part, cross_part, other = lax.optimization_barrier((keep[s], crossed[s], pieces[s]))
        pieces[s] = near_part + cross_part + other
    prior = pieces[num_cell][0:HEAD_ROW]
    bit = 1
    while bit < num_cell:
        prior = prior + flip(prior, bit, "cell")
        bit *= 2
    prior = (prior / num_cell).reshape(2, 128, 128)
    arrived = [flip(pieces[s], s, "cell") for s in order[1:-1]]
    own_sum = pieces[0] + sum(arrived)
    return (
        rendered,
        own_sum[0:HEAD_ROW].reshape(1, 2, 128, 128),
        prior[None],
        own_sum[None, HEAD_ROW : HEAD_ROW + 4],
        own_sum[None, APP_ROW : APP_ROW + 3, 0:width],
        codes_grad.T,
    )


def local(*args):
    cells = lax.axis_size("cell") * lax.axis_size("district")
    if cells <= 16 and lax.axis_size("district") == 4:
        return resident(*args)
    return routed(*args)


def solution(mesh):
    placed = (
        P(None, ("scene", "cell", "district")),
        P(("scene", "cell", "district"), None),
        P(("scene", "cell", "district"), None),
        P(("scene", "cell", "district"), None),
        P(None, ("scene", "cell", "district")),
        P(("scene", "cell", "district"), None),
        P(),
        P(("scene", "cell", "district"), None, None, None),
        P(("scene", "district"), None, None, None),
        P(("scene", "cell", "district"), None, None),
        P(("scene", "cell", "district"), None, None),
    )
    return jax.shard_map(
        local,
        mesh=mesh,
        in_specs=placed,
        out_specs=(
            P(None, ("scene", "cell", "district")),
            P(("scene", "cell", "district"), None, None, None),
            P(("scene", "district"), None, None, None),
            P(("scene", "cell", "district"), None, None),
            P(("scene", "cell", "district"), None, None),
            P(("scene", "cell", "district"), None),
        ),
        check_vma=False,
    )
```

```python
import functools

import jax
import jax.numpy as jnp
from jax import lax
from jax.experimental import pallas as pl
from jax.experimental.pallas import tpu as pltpu
from jax.sharding import PartitionSpec as P

GEOMETRY = 8
HIGHEST_PRECISION = lax.Precision.HIGHEST


def build_front(ray_geometry, segment_length, jitter):
    ray_count, crossings = segment_length.shape
    samples = jitter.shape[1] // crossings
    near_depth = jnp.cumsum(segment_length, axis=1) - segment_length
    geometry = jnp.broadcast_to(ray_geometry.T[:, None, :], (ray_count, crossings, 6))
    front = jnp.concatenate(
        [
            geometry,
            near_depth[:, :, None],
            segment_length[:, :, None],
            jitter.reshape(ray_count, crossings, samples),
        ],
        axis=2,
    )
    return front.reshape(ray_count * crossings, front.shape[2])


def slot_positions(crossing, cell_total, capacity):
    target_cell = crossing.reshape(-1)
    total_rows = target_cell.shape[0]
    onehot = target_cell[:, None] == jnp.arange(cell_total, dtype=jnp.int32)[None, :]
    triangle = (
        lax.broadcasted_iota(jnp.int32, (total_rows, total_rows), 0)
        > lax.broadcasted_iota(jnp.int32, (total_rows, total_rows), 1)
    ).astype(jnp.bfloat16)
    earlier = jnp.dot(triangle, onehot.astype(jnp.bfloat16), preferred_element_type=jnp.float32)
    position = jnp.sum(jnp.where(onehot, earlier, 0.0), axis=1).astype(jnp.int32)
    return target_cell * capacity + position


def sample_spacing(payload, samples):
    near_depth = payload[:, 6:7]
    extent = payload[:, 7:8]
    offsets = jnp.arange(samples, dtype=jnp.float32)[None, :]
    depths = near_depth + extent * (offsets + payload[:, GEOMETRY : GEOMETRY + samples]) / samples
    ending = jnp.concatenate([depths[:, 1:], near_depth + extent], axis=1)
    return (depths, ending - depths)


def cell_forward(payload, frequencies, first_weight, second_weight, head_one, samples):
    depths, spacing = sample_spacing(payload, samples)
    phases = jnp.zeros((payload.shape[0], samples, frequencies.shape[1]), jnp.float32)
    for component in range(3):
        position = (
            payload[:, component : component + 1]
            + depths * payload[:, 3 + component : 4 + component]
        )
        phases = phases + position[:, :, None] * frequencies[component][None, None, :]
    encoded = jnp.concatenate([jnp.sin(phases), jnp.cos(phases)], axis=2)
    encoded = encoded.reshape(payload.shape[0] * samples, encoded.shape[2]).astype(jnp.bfloat16)
    first_act = jax.nn.relu(
        jnp.dot(encoded, first_weight, preferred_element_type=jnp.float32)
    ).astype(jnp.bfloat16)
    second_act = jax.nn.relu(
        jnp.dot(first_act, second_weight, preferred_element_type=jnp.float32)
    ).astype(jnp.bfloat16)
    raw_outputs = lax.dot_general(
        head_one, second_act, (((1,), (1,)), ((), ())), preferred_element_type=jnp.float32
    )
    return ((encoded, first_act, second_act, raw_outputs), spacing)


def shade(raw_outputs, payload, spacing, appearance_one, samples):
    slot_count = payload.shape[0]
    outputs = raw_outputs.reshape(4, slot_count, samples)
    code_part = payload[:, GEOMETRY + samples :]
    color_shift = jnp.dot(code_part, appearance_one.T, precision=HIGHEST_PRECISION)
    density = jax.nn.softplus(outputs[0])
    colors = jax.nn.sigmoid(outputs[1:] + color_shift.T[:, :, None])
    optical = density * spacing
    transmit = jnp.exp(-(jnp.cumsum(optical, axis=1) - optical))
    opacity = 1.0 - jnp.exp(-optical)
    blend_weight = transmit * opacity
    return (outputs, colors, optical, transmit, opacity, blend_weight, code_part)


def segment_partials(raw_outputs, payload, spacing, appearance_one, samples):
    shaded = shade(raw_outputs, payload, spacing, appearance_one, samples)
    colors, optical, blend_weight = (shaded[1], shaded[2], shaded[5])
    segment_color = jnp.sum(blend_weight[None] * colors, axis=2)
    segment_log = -jnp.sum(optical, axis=1)
    return jnp.concatenate([segment_color.T, segment_log[:, None]], axis=1)


def cell_backward(
    payload, saved_acts, spacing, cotangent, second_weight, head_one, appearance_one, samples
):
    encoded, first_act, second_act, raw_outputs = saved_acts
    outputs, colors, optical, transmit, opacity, blend_weight, code_part = shade(
        raw_outputs, payload, spacing, appearance_one, samples
    )
    color_grad = cotangent[:, :3].T
    log_grad = cotangent[:, 3]
    blend_grad = jnp.sum(color_grad[:, :, None] * colors, axis=0)
    colors_grad = color_grad[:, :, None] * blend_weight[None]
    transmit_grad = blend_grad * opacity
    optical_grad = blend_grad * transmit * (1.0 - opacity) - log_grad[:, None]
    before_grad = -transmit_grad * transmit
    later_sum = jnp.flip(jnp.cumsum(jnp.flip(before_grad, axis=1), axis=1), axis=1) - before_grad
    optical_grad = optical_grad + later_sum
    density_grad = optical_grad * spacing * jax.nn.sigmoid(outputs[0])
    logit_grad = colors_grad * colors * (1.0 - colors)
    slot_count = payload.shape[0]
    output_grad = (
        jnp.concatenate([density_grad[None], logit_grad], axis=0)
        .reshape(4, slot_count * samples)
        .astype(jnp.bfloat16)
    )
    head_grad = jnp.dot(output_grad, second_act, preferred_element_type=jnp.float32)
    shift_grad = jnp.sum(logit_grad, axis=2)
    second_grad = lax.dot_general(
        output_grad, head_one, (((0,), (0,)), ((), ())), preferred_element_type=jnp.float32
    )
    second_grad = jnp.where(second_act > 0, second_grad, 0.0).astype(jnp.bfloat16)
    second_weight_grad = lax.dot_general(
        first_act, second_grad, (((0,), (0,)), ((), ())), preferred_element_type=jnp.float32
    )
    first_grad = lax.dot_general(
        second_grad, second_weight, (((1,), (1,)), ((), ())), preferred_element_type=jnp.float32
    )
    first_grad = jnp.where(first_act > 0, first_grad, 0.0).astype(jnp.bfloat16)
    first_weight_grad = lax.dot_general(
        encoded, first_grad, (((0,), (0,)), ((), ())), preferred_element_type=jnp.float32
    )
    return (first_weight_grad, second_weight_grad, head_grad, shift_grad, code_part)


def composite(gathered, target):
    segment_color = gathered[:, :, :3]
    segment_log = gathered[:, :, 3]
    reach_weight = jnp.exp(jnp.cumsum(segment_log, axis=1) - segment_log)
    rendered = jnp.sum(reach_weight[:, :, None] * segment_color, axis=1).T
    residual = rendered - target
    color_grad = reach_weight[:, :, None] * residual.T[:, None, :]
    reach_grad = jnp.sum(residual.T[:, None, :] * segment_color, axis=2) * reach_weight
    log_grad = jnp.flip(jnp.cumsum(jnp.flip(reach_grad, axis=1), axis=1), axis=1) - reach_grad
    return (rendered, jnp.concatenate([color_grad, log_grad[:, :, None]], axis=2))


def routed(
    ray_geometry,
    segment_length,
    jitter,
    appearance_codes,
    target,
    crossing,
    frequencies,
    cell_layers,
    district_prior,
    head_weight,
    appearance_weight,
):
    num_cell = lax.axis_size("cell")
    num_district = lax.axis_size("district")
    cell_total = num_cell * num_district
    ray_count, crossings = crossing.shape
    samples = jitter.shape[1] // crossings
    segments = ray_count * crossings
    capacity = 2 * segments // cell_total
    slot_total = cell_total * capacity
    code_width = appearance_codes.shape[1]
    front = build_front(ray_geometry, segment_length, jitter)
    codes_seg = jnp.broadcast_to(
        appearance_codes[:, None, :], (ray_count, crossings, code_width)
    ).reshape(segments, code_width)
    payload = jnp.concatenate([front, codes_seg], axis=1)
    appearance_one = appearance_weight[0]
    row_width = payload.shape[1]
    places = slot_positions(crossing, cell_total, capacity)
    outbox = (
        jnp.zeros((slot_total, row_width), jnp.float32)
        .at[places]
        .set(payload)
        .reshape(cell_total, capacity * row_width)
    )
    arrived = lax.all_to_all(outbox, ("cell", "district"), split_axis=0, concat_axis=0, tiled=True)
    arrived = arrived.reshape(slot_total, row_width)
    effective = (cell_layers[0].astype(jnp.float32) + district_prior[0].astype(jnp.float32)).astype(
        jnp.bfloat16
    )
    head_one = head_weight[0]
    block_rows = min(512, slot_total)
    blocked = arrived.reshape(slot_total // block_rows, block_rows, row_width)

    def forward_keep(slot_rows):
        saved_acts, spacing = cell_forward(
            slot_rows, frequencies, effective[0], effective[1], head_one, samples
        )
        return (
            segment_partials(saved_acts[3], slot_rows, spacing, appearance_one, samples),
            saved_acts,
        )

    partials, stored = lax.map(forward_keep, blocked)
    partials = partials.reshape(cell_total, capacity * 4)
    returned = lax.all_to_all(
        partials, ("cell", "district"), split_axis=0, concat_axis=0, tiled=True
    )
    returned = returned.reshape(slot_total, 4)
    rendered, cotangent = composite(returned[places].reshape(ray_count, crossings, 4), target)
    grad_box = (
        jnp.zeros((slot_total, 4), jnp.float32)
        .at[places]
        .set(cotangent.reshape(segments, 4))
        .reshape(cell_total, capacity * 4)
    )
    incoming = lax.all_to_all(
        grad_box, ("cell", "district"), split_axis=0, concat_axis=0, tiled=True
    )
    incoming = incoming.reshape(slot_total // block_rows, block_rows, 4)

    def finish(result):
        first_part, second_part, head_part, shift_grad, code_part = result
        appearance_part = jnp.dot(shift_grad, code_part, precision=HIGHEST_PRECISION)
        code_part_grad = jnp.dot(shift_grad.T, appearance_one, precision=HIGHEST_PRECISION)
        return (first_part, second_part, head_part, appearance_part, code_part_grad)

    def backward_keep(bundle):
        slot_rows, incoming_rows, saved_acts = bundle
        spacing = sample_spacing(slot_rows, samples)[1]
        return finish(
            cell_backward(
                slot_rows,
                saved_acts,
                spacing,
                incoming_rows,
                effective[1],
                head_one,
                appearance_one,
                samples,
            )
        )

    pieces = lax.map(backward_keep, (blocked, incoming, stored))
    first_w = jnp.sum(pieces[0], axis=0)
    second_w = jnp.sum(pieces[1], axis=0)
    head_grad = jnp.sum(pieces[2], axis=0)
    appearance_grad = jnp.sum(pieces[3], axis=0)
    code_box = pieces[4].reshape(cell_total, capacity * code_width)
    code_back = lax.all_to_all(
        code_box, ("cell", "district"), split_axis=0, concat_axis=0, tiled=True
    )
    code_back = code_back.reshape(slot_total, code_width)
    grad_codes = jnp.sum(code_back[places].reshape(ray_count, crossings, code_width), axis=1)
    grad_pair = jnp.stack([first_w, second_w], axis=0)
    grad_prior = lax.psum(grad_pair, "cell") / num_cell
    return (
        rendered,
        grad_pair[None],
        grad_prior[None],
        head_grad[None],
        appearance_grad[None],
        grad_codes,
    )


TILE = 8
UNROLL = 16
ROWS = 264
HEAD_ROW = 256
APP_ROW = 260
VMEM_LIMIT = 56 * 1024 * 1024
SIN = (
    6.283185005187988,
    -41.341590881347656,
    81.59994506835938,
    -76.61447143554688,
    41.3428840637207,
    -12.471243858337402,
)
COS = (
    0.9999992251396179,
    -19.738981246948242,
    64.92865753173828,
    -85.27162170410156,
    58.79049301147461,
    -21.07110595703125,
)
F32 = jnp.float32
BF16 = jnp.bfloat16


def iota(shape, axis):
    return lax.broadcasted_iota(jnp.int32, shape, axis)


def dot_nn(a, b):
    return jnp.dot(a, b, preferred_element_type=F32)


def dot_nt(a, b):
    return lax.dot_general(a, b, (((1,), (1,)), ((), ())), preferred_element_type=F32)


def split3(x):
    high = x.astype(BF16)
    rest = x - high.astype(F32)
    mid = rest.astype(BF16)
    low = (rest - mid.astype(F32)).astype(BF16)
    return high, mid, low


def pick_nn(x, select):
    rows = x.shape[0]
    parts = jnp.concatenate([part.astype(F32) for part in split3(x)], axis=0)
    parts = dot_nn(parts.astype(BF16), select)
    return (parts[2 * rows :] + parts[rows : 2 * rows]) + parts[:rows]


def pick_nt(select, x):
    high, mid, low = split3(x)
    return (dot_nt(select, low) + dot_nt(select, mid)) + dot_nt(select, high)


def exact_nn(a, b):
    return jnp.dot(a, b, precision=HIGHEST_PRECISION, preferred_element_type=F32)


def put_channel(ref, c, x):
    for h in range(ref.shape[0]):
        ref[h, pl.ds(c, x.shape[0], 8), :] = x[:, 128 * h : 128 * (h + 1)]


def get_channel(ref, c):
    tiles = ref.shape[1] // 8
    return jnp.concatenate([ref[h, pl.ds(c, tiles, 8), :] for h in range(ref.shape[0])], axis=1)


def get_tile(ref, t):
    rows = pl.ds(pl.multiple_of(t * 8, 8), 8)
    return jnp.concatenate([ref[h, rows, :] for h in range(ref.shape[0])], axis=1)


def put_tile(ref, t, x):
    rows = pl.ds(pl.multiple_of(t * 8, 8), 8)
    for h in range(ref.shape[0]):
        ref[h, rows, :] = x[:, 128 * h : 128 * (h + 1)]


def pack_kernel(layers_ref, prior_ref, head_ref, app_ref, out_ref, again_ref):
    for layer in range(2):
        both = layers_ref[0, layer].astype(F32) + prior_ref[0, layer].astype(F32)
        out_ref[128 * layer : 128 * (layer + 1), :] = both.T
    out_ref[HEAD_ROW:ROWS, :] = jnp.zeros((ROWS - HEAD_ROW, 128), F32)
    out_ref[HEAD_ROW : HEAD_ROW + 4, :] = head_ref[0].astype(F32)
    for c in range(3):
        out_ref[APP_ROW + c : APP_ROW + c + 1, 0 : app_ref.shape[2]] = app_ref[c]
    again_ref[...] = out_ref[...]


def slot_mask(place_row):
    return (iota((TILE, place_row.shape[1]), 0) == place_row.astype(jnp.int32)).astype(F32)


def tile_onehot(tile_row, tiles):
    return (iota((tiles, tile_row.shape[1]), 0) == tile_row.astype(jnp.int32)).astype(F32).astype(BF16)


def cell_onehot(cells_ref, cells):
    return [
        (iota((cells, cells_ref.shape[1]), 0) == cells_ref[k : k + 1, :]).astype(F32)
        for k in range(cells_ref.shape[0])
    ]


def lane_select(channels, lanes):
    rows = channels * TILE
    row, column = iota((rows, channels * lanes), 0), iota((rows, channels * lanes), 1)
    same = (row // TILE == column // lanes) & (row % TILE == column % TILE)
    return same.astype(F32).astype(BF16)


def deal_kernel(
    cells,
    samples,
    cells_ref,
    geometry_ref,
    length_ref,
    jitter_ref,
    frequency_ref,
    own_ref,
    other_ref,
    meta_ref,
    spacing_ref,
    tile_cell_ref,
    tile_start_ref,
    position_ref,
    factor_ref,
    passed_ref,
):
    del own_ref, other_ref, passed_ref
    tiles = spacing_ref.shape[0]
    lanes = TILE * samples
    crossings, rays = cells_ref.shape
    segments = crossings * rays

    onehot = jnp.concatenate(cell_onehot(cells_ref, cells), axis=1)
    chunks = [onehot[:, 128 * c : 128 * (c + 1)] for c in range(segments // 128)]
    before = (iota((128, 128), 0) < iota((128, 128), 1)).astype(F32).astype(BF16)
    prefix = dot_nn(jnp.concatenate(chunks, axis=0).astype(BF16), before)
    running = jnp.zeros((cells, 1), F32)
    ranks = []
    for c, chunk in enumerate(chunks):
        earlier = prefix[cells * c : cells * (c + 1), :] + running
        ranks.append(jnp.sum(chunk * earlier, axis=0, keepdims=True))
        running = running + jnp.sum(chunk, axis=1, keepdims=True)
    rank = jnp.concatenate(ranks, axis=1)
    needed = jnp.broadcast_to(jnp.floor((running + (TILE - 1)) * (1.0 / TILE)), (cells, 128))
    lower = (iota((cells, cells), 1) < iota((cells, cells), 0)).astype(F32).astype(BF16)
    start = dot_nn(lower, needed.astype(BF16))
    inside = jnp.floor(rank * (1.0 / TILE))
    tile_row = jnp.sum(onehot * start[:, 0:1], axis=0, keepdims=True) + inside
    place_row = rank - inside * TILE
    meta_ref[...] = jnp.concatenate(
        [tile_row, place_row, jnp.zeros((6, segments), F32)], axis=0
    )
    ends = start[:, 0:1] + needed[:, 0:1]
    owner = jnp.sum(
        (ends <= iota((cells, tile_cell_ref.shape[1]), 1).astype(F32)).astype(F32),
        axis=0,
        keepdims=True,
    )
    owner = jnp.minimum(owner, cells - 1.0).astype(jnp.int32)
    tile_cell_ref[...] = jnp.broadcast_to(owner, tile_cell_ref.shape)
    tile_start_ref[0:cells, :] = start.astype(jnp.int32)
    tile_start_ref[cells : cells + 8, :] = jnp.broadcast_to(
        ends[cells - 1 : cells, :], (8, 128)
    ).astype(jnp.int32)

    mask = slot_mask(place_row)
    place = tile_onehot(tile_row, tiles)
    lengths = length_ref[...]
    near = jnp.zeros((1, rays), F32)
    nears, extents = [], []
    for k in range(crossings):
        nears.append(near)
        extents.append(lengths[k : k + 1, :])
        near = near + lengths[k : k + 1, :]
    rows = [
        jnp.concatenate([geometry_ref[c : c + 1, :]] * crossings, axis=1) for c in range(6)
    ]
    rows += [jnp.concatenate(nears, axis=1), jnp.concatenate(extents, axis=1)]
    wide = pick_nt(place, jnp.concatenate([mask * row for row in rows], axis=0))
    wide = pick_nn(wide, lane_select(8, lanes))
    channel = [wide[:, lanes * c : lanes * (c + 1)] for c in range(8)]
    turned = jitter_ref[...].T
    offsets = jnp.concatenate(
        [turned[samples * k : samples * (k + 1), :] for k in range(crossings)], axis=1
    )
    dealt = jnp.concatenate([mask * offsets[i : i + 1, :] for i in range(samples)], axis=0)
    jitter = pick_nt(place, dealt)
    step = (iota((tiles, lanes), 1) // TILE).astype(F32)
    near, extent = channel[6], channel[7]
    depths = near + extent * (step + jitter) / samples
    following = pltpu.roll(depths, lanes - TILE, 1)
    ending = jnp.where(iota((tiles, lanes), 1) >= lanes - TILE, near + extent, following)
    spacing_ref[...] = ending - depths
    for c in range(3):
        put_channel(position_ref, c, channel[c] + depths * channel[3 + c])
    for c in range(3, 8):
        put_channel(position_ref, c, jnp.zeros((tiles, lanes), F32))
    turns = frequency_ref[...] * 0.15915494309189535
    count = turns.shape[1]
    block = jnp.concatenate([turns, jnp.zeros((5, count), F32)], axis=0)
    block = jnp.concatenate([block, jnp.zeros((8, 128 - count), F32)], axis=1)
    high, mid, low = [part.astype(F32) for part in split3(block)]
    stack = [high, high, high, mid, mid, low, jnp.zeros((128 - 48, 128), F32)]
    factor_ref[...] = jnp.concatenate(stack, axis=0).T[0:count, 0:48].astype(BF16)


def encode(position_ref, factor, encoded_ref, some):
    phases = []
    for t in some:
        high, mid, low = split3(get_tile(position_ref, t))
        high, mid, low = high.astype(F32), mid.astype(F32), low.astype(F32)
        points = jnp.concatenate([high, mid, low, high, mid, high], axis=0).astype(BF16)
        phases.append(dot_nn(factor, points))
    for t, phase in zip(some, phases):
        phase = phase - jnp.round(phase)
        square = phase * phase
        sine, cosine = square * SIN[5] + SIN[4], square * COS[5] + COS[4]
        for c in (3, 2, 1, 0):
            sine, cosine = sine * square + SIN[c], cosine * square + COS[c]
        half = phase.shape[0]
        encoded_ref[t, 0:half, :] = (sine * phase).astype(BF16)
        encoded_ref[t, half:, :] = cosine.astype(BF16)


def step_kernel(
    cells,
    samples,
    tile_cell_ref,
    tile_start_ref,
    meta_ref,
    cells_ref,
    spacing_ref,
    position_ref,
    factor_ref,
    codes_ref,
    target_ref,
    *refs,
):
    weights, refs = refs[:cells], refs[cells:]
    (
        rendered_ref,
        codes_grad_ref,
        keep_ref,
        send_ref,
        encoded_ref,
        first_ref,
        second_ref,
        forward1_ref,
        forward2_ref,
        backward2_ref,
        head_ref,
        head_turned_ref,
        outputs_ref,
        grads_ref,
        sums_ref,
        semaphore,
    ) = refs
    tiles, lanes = spacing_ref.shape
    crossings, rays = cells_ref.shape
    segments = crossings * rays
    width = codes_ref.shape[0]
    used = tile_start_ref[cells, 0]
    trips = (used + UNROLL - 1) // UNROLL

    appearance = []
    for v, ref in enumerate(weights):
        forward1_ref[v] = ref[0:128, :].astype(BF16)
        second = ref[128:256, :]
        forward2_ref[v] = second.astype(BF16)
        backward2_ref[v] = second.T.astype(BF16)
        tail = ref[HEAD_ROW:ROWS, :]
        head = jnp.where(iota((8, 128), 0) < 4, tail, 0.0)
        head_ref[v] = head.astype(BF16)
        square = jnp.concatenate([head, jnp.zeros((120, 128), F32)], axis=0)
        head_turned_ref[v] = square.T[:, 0:8].astype(BF16)
        appearance.append(tail)
    outputs_ref[...] = jnp.zeros_like(outputs_ref)
    sums_ref[...] = jnp.zeros_like(sums_ref)

    factor = factor_ref[...]
    encode(position_ref, factor, encoded_ref, range(UNROLL))

    def forward(trip, carry):
        following = jnp.minimum(trip + 1, trips - 1) * UNROLL
        some = [trip * UNROLL + u for u in range(UNROLL)]
        owner = [tile_cell_ref[0, t] for t in some]
        firsts = [dot_nn(forward1_ref[v], encoded_ref[t]) for t, v in zip(some, owner)]
        firsts = [jnp.maximum(first, 0.0).astype(BF16) for first in firsts]
        for t, first in zip(some, firsts):
            first_ref[t] = first
        seconds = [dot_nn(forward2_ref[v], first) for v, first in zip(owner, firsts)]
        seconds = [jnp.maximum(second, 0.0).astype(BF16) for second in seconds]
        for t, second in zip(some, seconds):
            second_ref[t] = second
        outputs = [dot_nn(head_ref[v], second) for v, second in zip(owner, seconds)]
        for t, output in zip(some, outputs):
            put_tile(outputs_ref, t, output)
        encode(position_ref, factor, encoded_ref, [following + u for u in range(UNROLL)])
        return carry

    lax.fori_loop(0, trips, forward, 0)

    tile_row, place_row = meta_ref[0:1, :], meta_ref[1:2, :]
    mask = slot_mask(place_row)
    place = tile_onehot(tile_row, tiles)
    onehots = cell_onehot(cells_ref, cells)
    maps = jnp.concatenate(
        [jnp.concatenate([tail[4 + c : 5 + c, :] for tail in appearance], axis=0) for c in range(3)],
        axis=0,
    )[:, 0:width]
    codes = codes_ref[...]
    shifts = exact_nn(maps, codes)
    rows = [
        jnp.concatenate(
            [
                jnp.sum(onehots[k] * shifts[cells * c : cells * (c + 1), :], axis=0, keepdims=True)
                for k in range(crossings)
            ],
            axis=1,
        )
        for c in range(3)
    ]
    spread3 = lane_select(4, lanes)
    shift = pick_nt(place, jnp.concatenate([mask * row for row in rows], axis=0))
    shift = pick_nn(shift, spread3[0:24, 0 : 3 * lanes])

    spacing = spacing_ref[...]
    raw = get_channel(outputs_ref, 0)
    ray = (iota((lanes, lanes), 0) % TILE) == (iota((lanes, lanes), 1) % TILE)
    earlier = (ray & (iota((lanes, lanes), 0) < iota((lanes, lanes), 1))).astype(F32).astype(BF16)
    later = (ray & (iota((lanes, lanes), 0) > iota((lanes, lanes), 1))).astype(F32).astype(BF16)
    total = ((iota((TILE, lanes), 1) % TILE) == iota((TILE, lanes), 0)).astype(F32).astype(BF16)
    density = jax.nn.softplus(raw)
    colors = [
        jax.nn.sigmoid(
            get_channel(outputs_ref, 1 + c) + shift[:, lanes * c : lanes * (c + 1)]
        )
        for c in range(3)
    ]
    optical = density * spacing
    transmit = jnp.exp(-pick_nn(optical, earlier))
    opacity = 1.0 - jnp.exp(-optical)
    blend = transmit * opacity
    sums = [pick_nt(total, blend * color) for color in colors] + [-pick_nt(total, optical)]
    dealt = pick_nn(jnp.concatenate(sums, axis=0), place)
    parts = [
        jnp.sum(mask * dealt[TILE * c : TILE * (c + 1), :], axis=0, keepdims=True) for c in range(4)
    ]

    def crossed(row, k):
        return row[:, rays * k : rays * (k + 1)]

    reach, logs = [], jnp.zeros((1, rays), F32)
    for k in range(crossings):
        reach.append(jnp.exp(logs))
        logs = logs + crossed(parts[3], k)
    residuals, channel_grads = [], [[] for _ in range(3)]
    for c in range(3):
        rendered = sum(reach[k] * crossed(parts[c], k) for k in range(crossings))
        rendered_ref[c : c + 1, :] = rendered
        residuals.append(rendered - target_ref[c : c + 1, :])
    log_grads, after = [], jnp.zeros((1, rays), F32)
    for k in reversed(range(crossings)):
        log_grads.append(after)
        weight = sum(residuals[c] * crossed(parts[c], k) for c in range(3))
        after = after + weight * reach[k]
    log_row = jnp.concatenate(log_grads[::-1], axis=1)
    color_rows = [
        jnp.concatenate([reach[k] * residuals[c] for k in range(crossings)], axis=1)
        for c in range(3)
    ]
    back = pick_nt(place, jnp.concatenate([mask * row for row in color_rows + [log_row]], axis=0))
    back = pick_nn(back, spread3)
    color_grads = [back[:, lanes * c : lanes * (c + 1)] for c in range(3)]
    log_grad = back[:, 3 * lanes : 4 * lanes]

    blend_grad = sum(color_grads[c] * colors[c] for c in range(3))
    before_grad = -(blend_grad * opacity) * transmit
    optical_grad = blend_grad * transmit * (1.0 - opacity) - log_grad
    optical_grad = optical_grad + pick_nn(before_grad, later)
    put_channel(grads_ref, 0, optical_grad * spacing * jax.nn.sigmoid(raw))
    logits = []
    for c in range(3):
        logit = color_grads[c] * blend * colors[c] * (1.0 - colors[c])
        put_channel(grads_ref, 1 + c, logit)
        put_channel(grads_ref, 4 + c, jnp.zeros((tiles, lanes), F32))
        logits.append(pick_nt(total, logit))
    put_channel(grads_ref, 7, jnp.zeros((tiles, lanes), F32))
    dealt = pick_nn(jnp.concatenate(logits, axis=0), place)
    per_cell = []
    for c in range(3):
        row = jnp.sum(mask * dealt[TILE * c : TILE * (c + 1), :], axis=0, keepdims=True)
        per_cell.append(sum(onehots[k] * crossed(row, k) for k in range(crossings)))
    per_cell = jnp.concatenate(per_cell, axis=0)
    map_grads = exact_nn(per_cell, codes.T)
    codes_grad_ref[...] = exact_nn(maps.T, per_cell)
    for v in range(cells):
        for c in range(3):
            sums_ref[v, APP_ROW + c : APP_ROW + c + 1, 0:width] = map_grads[
                cells * c + v : cells * c + v + 1, :
            ]

    def backward(trip, carry):
        some = [trip * UNROLL + u for u in range(UNROLL)]
        owner = [tile_cell_ref[0, t] for t in some]
        outputs = [get_tile(grads_ref, t).astype(BF16) for t in some]
        second_grads = [dot_nn(head_turned_ref[v], output) for v, output in zip(owner, outputs)]
        second_grads = [
            jnp.where(second_ref[t] > 0, grad.astype(BF16), jnp.zeros((), BF16))
            for t, grad in zip(some, second_grads)
        ]
        first_grads = [dot_nn(backward2_ref[v], grad) for v, grad in zip(owner, second_grads)]
        first_grads = [
            jnp.where(first_ref[t] > 0, grad.astype(BF16), jnp.zeros((), BF16))
            for t, grad in zip(some, first_grads)
        ]
        head_parts = [dot_nt(output, second_ref[t]) for t, output in zip(some, outputs)]
        second_parts = [dot_nt(first_ref[t], grad) for t, grad in zip(some, second_grads)]
        first_parts = [dot_nt(encoded_ref[t], grad) for t, grad in zip(some, first_grads)]
        for v, head, second, first in zip(owner, head_parts, second_parts, first_parts):
            sums_ref[v, HEAD_ROW:ROWS, :] += head
            sums_ref[v, 128:256, :] += second
            sums_ref[v, 0:128, :] += first
        return carry

    num_cell = cells // 4
    copies = []

    def emit(half):
        for district in (2 * half, 2 * half + 1):
            members = sums_ref.at[pl.ds(district * num_cell, num_cell)]
            total = sums_ref[district * num_cell]
            for s in range(1, num_cell):
                total = total + sums_ref[district * num_cell + s]
            sums_ref[cells + district] = total
            out_ref = (keep_ref, send_ref)[half]
            at = (district % 2) * (num_cell + 1)
            for source, sink in (
                (members, out_ref.at[pl.ds(at, num_cell)]),
                (sums_ref.at[cells + district], out_ref.at[at + num_cell]),
            ):
                copies.append(pltpu.make_async_copy(source, sink, semaphore.at[len(copies)]))
                copies[-1].start()

    middle = (tile_start_ref[cells // 2, 0] + UNROLL - 1) // UNROLL
    lax.fori_loop(0, middle, backward, 0)
    emit(0)
    lax.fori_loop(middle, trips, backward, 0)
    emit(1)
    for copy in copies:
        copy.wait()


def resident(
    ray_geometry,
    segment_length,
    jitter,
    appearance_codes,
    target,
    crossing,
    frequencies,
    cell_layers,
    district_prior,
    head_weight,
    appearance_weight,
):
    num_cell = lax.axis_size("cell")
    num_district = lax.axis_size("district")
    cells = num_cell * num_district
    rays, crossings = crossing.shape
    samples = jitter.shape[1] // crossings
    segments = rays * crossings
    width = appearance_codes.shape[1]
    lanes = TILE * samples
    tiles = -(-(segments // TILE + cells) // UNROLL) * UNROLL
    me_cell, me_district = lax.axis_index("cell"), lax.axis_index("district")

    def flip(x, bits, axis="district"):
        return lax.ppermute(x, axis, [(i, i ^ bits) for i in range(lax.axis_size(axis))])

    own, again = pl.pallas_call(
        pack_kernel, out_shape=[jax.ShapeDtypeStruct((ROWS, 128), F32)] * 2, name="pack"
    )(cell_layers, district_prior, head_weight, jnp.transpose(appearance_weight, (1, 0, 2)))
    vmem, smem = pl.BlockSpec(memory_space=pltpu.VMEM), pl.BlockSpec(memory_space=pltpu.SMEM)
    anywhere = pl.BlockSpec(memory_space=pl.ANY)
    params = pltpu.CompilerParams(vmem_limit_bytes=VMEM_LIMIT)

    crossed_own = flip(own, 2)
    away = (crossing % num_district) ^ me_district
    steps = (crossing // num_district) ^ me_cell
    virtual = (((away & 1) * 2 + (away >> 1)) * num_cell + steps).T
    halves = lanes // 128
    default = pl.BlockSpec()
    meta, spacing, tile_cell, tile_start, position, factor, passed = pl.pallas_call(
        functools.partial(deal_kernel, cells, samples),
        in_specs=[default] * 5 + [anywhere, anywhere],
        out_specs=[default] * 6 + [anywhere],
        input_output_aliases={5: 6},
        out_shape=[
            jax.ShapeDtypeStruct((8, segments), F32),
            jax.ShapeDtypeStruct((tiles, lanes), F32),
            jax.ShapeDtypeStruct((8, 256), jnp.int32),
            jax.ShapeDtypeStruct((cells + 8, 128), jnp.int32),
            jax.ShapeDtypeStruct((halves, tiles * 8, 128), F32),
            jax.ShapeDtypeStruct((frequencies.shape[1], 48), BF16),
            jax.ShapeDtypeStruct((ROWS, 128), F32),
        ],
        compiler_params=params,
        cost_estimate=pl.CostEstimate(flops=6 << 30, bytes_accessed=4 << 20, transcendentals=0),
        name="deal",
    )(virtual, ray_geometry, segment_length.T, jitter, frequencies, again, crossed_own)
    near = [own]
    for s in range(1, num_cell):
        near.append(flip(near[s & (s - 1)], s & -s, "cell"))
    flipped = [crossed_own] + [flip(piece, 2) for piece in near[1:]]
    weights = near + flipped + [flip(piece, 1) for piece in [passed] + near[1:] + flipped]


    half = 2 * (num_cell + 1)
    rendered, codes_grad, keep, send = pl.pallas_call(
        functools.partial(step_kernel, cells, samples),
        in_specs=[smem, smem] + [vmem] * (7 + cells),
        out_specs=[vmem, vmem, anywhere, anywhere],
        out_shape=[
            jax.ShapeDtypeStruct((3, rays), F32),
            jax.ShapeDtypeStruct((width, rays), F32),
            jax.ShapeDtypeStruct((half, ROWS, 128), F32),
            jax.ShapeDtypeStruct((half, ROWS, 128), F32),
        ],
        scratch_shapes=[
            pltpu.VMEM((tiles, 128, lanes), BF16),
            pltpu.VMEM((tiles, 128, lanes), BF16),
            pltpu.VMEM((tiles, 128, lanes), BF16),
            pltpu.VMEM((cells, 128, 128), BF16),
            pltpu.VMEM((cells, 128, 128), BF16),
            pltpu.VMEM((cells, 128, 128), BF16),
            pltpu.VMEM((cells, 8, 128), BF16),
            pltpu.VMEM((cells, 128, 8), BF16),
            pltpu.VMEM((halves, tiles * 8, 128), F32),
            pltpu.VMEM((halves, tiles * 8, 128), F32),
            pltpu.VMEM((cells + 4, ROWS, 128), F32),
            pltpu.SemaphoreType.DMA((8,)),
        ],
        compiler_params=params,
        name="step",
    )(
        tile_cell,
        tile_start,
        meta,
        virtual,
        spacing,
        position,
        factor,
        appearance_codes.T,
        target,
        *weights,
    )

    crossed = flip(send, 1)
    order = [3, 2, num_cell, 1, 0]
    far = num_cell + 1
    pieces = {s: flip(keep[far + s] + crossed[far + s], 2) for s in order}
    for s in order:
        near_part, cross_part, other = lax.optimization_barrier((keep[s], crossed[s], pieces[s]))
        pieces[s] = near_part + cross_part + other
    prior = pieces[num_cell][0:HEAD_ROW]
    bit = num_cell // 2
    while bit > 0:
        prior = prior + flip(prior, bit, "cell")
        bit //= 2
    prior = (prior / num_cell).reshape(2, 128, 128)
    bit = 1
    while bit < num_cell:
        for s in reversed(range(bit, num_cell, 2 * bit)):
            pieces[s - bit] = pieces[s - bit] + flip(pieces[s], bit, "cell")
        bit *= 2
    own_sum = pieces[0]
    return (
        rendered,
        own_sum[0:HEAD_ROW].reshape(1, 2, 128, 128),
        prior[None],
        own_sum[None, HEAD_ROW : HEAD_ROW + 4],
        own_sum[None, APP_ROW : APP_ROW + 3, 0:width],
        codes_grad.T,
    )


def local(*args):
    cells = lax.axis_size("cell") * lax.axis_size("district")
    if cells <= 16 and lax.axis_size("district") == 4:
        return resident(*args)
    return routed(*args)


def solution(mesh):
    placed = (
        P(None, ("scene", "cell", "district")),
        P(("scene", "cell", "district"), None),
        P(("scene", "cell", "district"), None),
        P(("scene", "cell", "district"), None),
        P(None, ("scene", "cell", "district")),
        P(("scene", "cell", "district"), None),
        P(),
        P(("scene", "cell", "district"), None, None, None),
        P(("scene", "district"), None, None, None),
        P(("scene", "cell", "district"), None, None),
        P(("scene", "cell", "district"), None, None),
    )
    return jax.shard_map(
        local,
        mesh=mesh,
        in_specs=placed,
        out_specs=(
            P(None, ("scene", "cell", "district")),
            P(("scene", "cell", "district"), None, None, None),
            P(("scene", "district"), None, None, None),
            P(("scene", "cell", "district"), None, None),
            P(("scene", "cell", "district"), None, None),
            P(("scene", "cell", "district"), None),
        ),
        check_vma=False,
    )
```

```python
import functools

import jax
import jax.numpy as jnp
from jax import lax
from jax.experimental import pallas as pl
from jax.experimental.pallas import tpu as pltpu
from jax.sharding import PartitionSpec as P

GEOMETRY = 8
HIGHEST_PRECISION = lax.Precision.HIGHEST


def build_front(ray_geometry, segment_length, jitter):
    ray_count, crossings = segment_length.shape
    samples = jitter.shape[1] // crossings
    near_depth = jnp.cumsum(segment_length, axis=1) - segment_length
    geometry = jnp.broadcast_to(ray_geometry.T[:, None, :], (ray_count, crossings, 6))
    front = jnp.concatenate(
        [
            geometry,
            near_depth[:, :, None],
            segment_length[:, :, None],
            jitter.reshape(ray_count, crossings, samples),
        ],
        axis=2,
    )
    return front.reshape(ray_count * crossings, front.shape[2])


def slot_positions(crossing, cell_total, capacity):
    target_cell = crossing.reshape(-1)
    total_rows = target_cell.shape[0]
    onehot = target_cell[:, None] == jnp.arange(cell_total, dtype=jnp.int32)[None, :]
    triangle = (
        lax.broadcasted_iota(jnp.int32, (total_rows, total_rows), 0)
        > lax.broadcasted_iota(jnp.int32, (total_rows, total_rows), 1)
    ).astype(jnp.bfloat16)
    earlier = jnp.dot(triangle, onehot.astype(jnp.bfloat16), preferred_element_type=jnp.float32)
    position = jnp.sum(jnp.where(onehot, earlier, 0.0), axis=1).astype(jnp.int32)
    return target_cell * capacity + position


def sample_spacing(payload, samples):
    near_depth = payload[:, 6:7]
    extent = payload[:, 7:8]
    offsets = jnp.arange(samples, dtype=jnp.float32)[None, :]
    depths = near_depth + extent * (offsets + payload[:, GEOMETRY : GEOMETRY + samples]) / samples
    ending = jnp.concatenate([depths[:, 1:], near_depth + extent], axis=1)
    return (depths, ending - depths)


def cell_forward(payload, frequencies, first_weight, second_weight, head_one, samples):
    depths, spacing = sample_spacing(payload, samples)
    phases = jnp.zeros((payload.shape[0], samples, frequencies.shape[1]), jnp.float32)
    for component in range(3):
        position = (
            payload[:, component : component + 1]
            + depths * payload[:, 3 + component : 4 + component]
        )
        phases = phases + position[:, :, None] * frequencies[component][None, None, :]
    encoded = jnp.concatenate([jnp.sin(phases), jnp.cos(phases)], axis=2)
    encoded = encoded.reshape(payload.shape[0] * samples, encoded.shape[2]).astype(jnp.bfloat16)
    first_act = jax.nn.relu(
        jnp.dot(encoded, first_weight, preferred_element_type=jnp.float32)
    ).astype(jnp.bfloat16)
    second_act = jax.nn.relu(
        jnp.dot(first_act, second_weight, preferred_element_type=jnp.float32)
    ).astype(jnp.bfloat16)
    raw_outputs = lax.dot_general(
        head_one, second_act, (((1,), (1,)), ((), ())), preferred_element_type=jnp.float32
    )
    return ((encoded, first_act, second_act, raw_outputs), spacing)


def shade(raw_outputs, payload, spacing, appearance_one, samples):
    slot_count = payload.shape[0]
    outputs = raw_outputs.reshape(4, slot_count, samples)
    code_part = payload[:, GEOMETRY + samples :]
    color_shift = jnp.dot(code_part, appearance_one.T, precision=HIGHEST_PRECISION)
    density = jax.nn.softplus(outputs[0])
    colors = jax.nn.sigmoid(outputs[1:] + color_shift.T[:, :, None])
    optical = density * spacing
    transmit = jnp.exp(-(jnp.cumsum(optical, axis=1) - optical))
    opacity = 1.0 - jnp.exp(-optical)
    blend_weight = transmit * opacity
    return (outputs, colors, optical, transmit, opacity, blend_weight, code_part)


def segment_partials(raw_outputs, payload, spacing, appearance_one, samples):
    shaded = shade(raw_outputs, payload, spacing, appearance_one, samples)
    colors, optical, blend_weight = (shaded[1], shaded[2], shaded[5])
    segment_color = jnp.sum(blend_weight[None] * colors, axis=2)
    segment_log = -jnp.sum(optical, axis=1)
    return jnp.concatenate([segment_color.T, segment_log[:, None]], axis=1)


def cell_backward(
    payload, saved_acts, spacing, cotangent, second_weight, head_one, appearance_one, samples
):
    encoded, first_act, second_act, raw_outputs = saved_acts
    outputs, colors, optical, transmit, opacity, blend_weight, code_part = shade(
        raw_outputs, payload, spacing, appearance_one, samples
    )
    color_grad = cotangent[:, :3].T
    log_grad = cotangent[:, 3]
    blend_grad = jnp.sum(color_grad[:, :, None] * colors, axis=0)
    colors_grad = color_grad[:, :, None] * blend_weight[None]
    transmit_grad = blend_grad * opacity
    optical_grad = blend_grad * transmit * (1.0 - opacity) - log_grad[:, None]
    before_grad = -transmit_grad * transmit
    later_sum = jnp.flip(jnp.cumsum(jnp.flip(before_grad, axis=1), axis=1), axis=1) - before_grad
    optical_grad = optical_grad + later_sum
    density_grad = optical_grad * spacing * jax.nn.sigmoid(outputs[0])
    logit_grad = colors_grad * colors * (1.0 - colors)
    slot_count = payload.shape[0]
    output_grad = (
        jnp.concatenate([density_grad[None], logit_grad], axis=0)
        .reshape(4, slot_count * samples)
        .astype(jnp.bfloat16)
    )
    head_grad = jnp.dot(output_grad, second_act, preferred_element_type=jnp.float32)
    shift_grad = jnp.sum(logit_grad, axis=2)
    second_grad = lax.dot_general(
        output_grad, head_one, (((0,), (0,)), ((), ())), preferred_element_type=jnp.float32
    )
    second_grad = jnp.where(second_act > 0, second_grad, 0.0).astype(jnp.bfloat16)
    second_weight_grad = lax.dot_general(
        first_act, second_grad, (((0,), (0,)), ((), ())), preferred_element_type=jnp.float32
    )
    first_grad = lax.dot_general(
        second_grad, second_weight, (((1,), (1,)), ((), ())), preferred_element_type=jnp.float32
    )
    first_grad = jnp.where(first_act > 0, first_grad, 0.0).astype(jnp.bfloat16)
    first_weight_grad = lax.dot_general(
        encoded, first_grad, (((0,), (0,)), ((), ())), preferred_element_type=jnp.float32
    )
    return (first_weight_grad, second_weight_grad, head_grad, shift_grad, code_part)


def composite(gathered, target):
    segment_color = gathered[:, :, :3]
    segment_log = gathered[:, :, 3]
    reach_weight = jnp.exp(jnp.cumsum(segment_log, axis=1) - segment_log)
    rendered = jnp.sum(reach_weight[:, :, None] * segment_color, axis=1).T
    residual = rendered - target
    color_grad = reach_weight[:, :, None] * residual.T[:, None, :]
    reach_grad = jnp.sum(residual.T[:, None, :] * segment_color, axis=2) * reach_weight
    log_grad = jnp.flip(jnp.cumsum(jnp.flip(reach_grad, axis=1), axis=1), axis=1) - reach_grad
    return (rendered, jnp.concatenate([color_grad, log_grad[:, :, None]], axis=2))


def routed(
    ray_geometry,
    segment_length,
    jitter,
    appearance_codes,
    target,
    crossing,
    frequencies,
    cell_layers,
    district_prior,
    head_weight,
    appearance_weight,
):
    num_cell = lax.axis_size("cell")
    num_district = lax.axis_size("district")
    cell_total = num_cell * num_district
    ray_count, crossings = crossing.shape
    samples = jitter.shape[1] // crossings
    segments = ray_count * crossings
    capacity = 2 * segments // cell_total
    slot_total = cell_total * capacity
    code_width = appearance_codes.shape[1]
    front = build_front(ray_geometry, segment_length, jitter)
    codes_seg = jnp.broadcast_to(
        appearance_codes[:, None, :], (ray_count, crossings, code_width)
    ).reshape(segments, code_width)
    payload = jnp.concatenate([front, codes_seg], axis=1)
    appearance_one = appearance_weight[0]
    row_width = payload.shape[1]
    places = slot_positions(crossing, cell_total, capacity)
    outbox = (
        jnp.zeros((slot_total, row_width), jnp.float32)
        .at[places]
        .set(payload)
        .reshape(cell_total, capacity * row_width)
    )
    arrived = lax.all_to_all(outbox, ("cell", "district"), split_axis=0, concat_axis=0, tiled=True)
    arrived = arrived.reshape(slot_total, row_width)
    effective = (cell_layers[0].astype(jnp.float32) + district_prior[0].astype(jnp.float32)).astype(
        jnp.bfloat16
    )
    head_one = head_weight[0]
    block_rows = min(512, slot_total)
    blocked = arrived.reshape(slot_total // block_rows, block_rows, row_width)

    def forward_keep(slot_rows):
        saved_acts, spacing = cell_forward(
            slot_rows, frequencies, effective[0], effective[1], head_one, samples
        )
        return (
            segment_partials(saved_acts[3], slot_rows, spacing, appearance_one, samples),
            saved_acts,
        )

    partials, stored = lax.map(forward_keep, blocked)
    partials = partials.reshape(cell_total, capacity * 4)
    returned = lax.all_to_all(
        partials, ("cell", "district"), split_axis=0, concat_axis=0, tiled=True
    )
    returned = returned.reshape(slot_total, 4)
    rendered, cotangent = composite(returned[places].reshape(ray_count, crossings, 4), target)
    grad_box = (
        jnp.zeros((slot_total, 4), jnp.float32)
        .at[places]
        .set(cotangent.reshape(segments, 4))
        .reshape(cell_total, capacity * 4)
    )
    incoming = lax.all_to_all(
        grad_box, ("cell", "district"), split_axis=0, concat_axis=0, tiled=True
    )
    incoming = incoming.reshape(slot_total // block_rows, block_rows, 4)

    def finish(result):
        first_part, second_part, head_part, shift_grad, code_part = result
        appearance_part = jnp.dot(shift_grad, code_part, precision=HIGHEST_PRECISION)
        code_part_grad = jnp.dot(shift_grad.T, appearance_one, precision=HIGHEST_PRECISION)
        return (first_part, second_part, head_part, appearance_part, code_part_grad)

    def backward_keep(bundle):
        slot_rows, incoming_rows, saved_acts = bundle
        spacing = sample_spacing(slot_rows, samples)[1]
        return finish(
            cell_backward(
                slot_rows,
                saved_acts,
                spacing,
                incoming_rows,
                effective[1],
                head_one,
                appearance_one,
                samples,
            )
        )

    pieces = lax.map(backward_keep, (blocked, incoming, stored))
    first_w = jnp.sum(pieces[0], axis=0)
    second_w = jnp.sum(pieces[1], axis=0)
    head_grad = jnp.sum(pieces[2], axis=0)
    appearance_grad = jnp.sum(pieces[3], axis=0)
    code_box = pieces[4].reshape(cell_total, capacity * code_width)
    code_back = lax.all_to_all(
        code_box, ("cell", "district"), split_axis=0, concat_axis=0, tiled=True
    )
    code_back = code_back.reshape(slot_total, code_width)
    grad_codes = jnp.sum(code_back[places].reshape(ray_count, crossings, code_width), axis=1)
    grad_pair = jnp.stack([first_w, second_w], axis=0)
    grad_prior = lax.psum(grad_pair, "cell") / num_cell
    return (
        rendered,
        grad_pair[None],
        grad_prior[None],
        head_grad[None],
        appearance_grad[None],
        grad_codes,
    )


TILE = 8
UNROLL = 16
ROWS = 264
HEAD_ROW = 256
APP_ROW = 260
VMEM_LIMIT = 48 * 1024 * 1024
SIN = (
    6.283185005187988,
    -41.341590881347656,
    81.59994506835938,
    -76.61447143554688,
    41.3428840637207,
    -12.471243858337402,
)
COS = (
    0.9999992251396179,
    -19.738981246948242,
    64.92865753173828,
    -85.27162170410156,
    58.79049301147461,
    -21.07110595703125,
)
F32 = jnp.float32
BF16 = jnp.bfloat16


def iota(shape, axis):
    return lax.broadcasted_iota(jnp.int32, shape, axis)


def dot_nn(a, b):
    return jnp.dot(a, b, preferred_element_type=F32)


def dot_nt(a, b):
    return lax.dot_general(a, b, (((1,), (1,)), ((), ())), preferred_element_type=F32)


def split3(x):
    high = x.astype(BF16)
    rest = x - high.astype(F32)
    mid = rest.astype(BF16)
    low = (rest - mid.astype(F32)).astype(BF16)
    return high, mid, low


def pick_nn(x, select):
    rows = x.shape[0]
    parts = jnp.concatenate([part.astype(F32) for part in split3(x)], axis=0)
    parts = dot_nn(parts.astype(BF16), select)
    return (parts[2 * rows :] + parts[rows : 2 * rows]) + parts[:rows]


def pick_nt(select, x):
    high, mid, low = split3(x)
    return (dot_nt(select, low) + dot_nt(select, mid)) + dot_nt(select, high)


def exact_nn(a, b):
    return jnp.dot(a, b, precision=HIGHEST_PRECISION, preferred_element_type=F32)


def put_channel(ref, c, x):
    for h in range(ref.shape[0]):
        ref[h, pl.ds(c, x.shape[0], 8), :] = x[:, 128 * h : 128 * (h + 1)]


def get_channel(ref, c):
    tiles = ref.shape[1] // 8
    return jnp.concatenate([ref[h, pl.ds(c, tiles, 8), :] for h in range(ref.shape[0])], axis=1)


def get_tile(ref, t):
    rows = pl.ds(pl.multiple_of(t * 8, 8), 8)
    return jnp.concatenate([ref[h, rows, :] for h in range(ref.shape[0])], axis=1)


def put_tile(ref, t, x):
    rows = pl.ds(pl.multiple_of(t * 8, 8), 8)
    for h in range(ref.shape[0]):
        ref[h, rows, :] = x[:, 128 * h : 128 * (h + 1)]


def pack_kernel(layers_ref, prior_ref, head_ref, app_ref, out_ref, again_ref):
    for layer in range(2):
        both = layers_ref[0, layer].astype(F32) + prior_ref[0, layer].astype(F32)
        out_ref[128 * layer : 128 * (layer + 1), :] = both.T
    out_ref[HEAD_ROW:ROWS, :] = jnp.zeros((ROWS - HEAD_ROW, 128), F32)
    out_ref[HEAD_ROW : HEAD_ROW + 4, :] = head_ref[0].astype(F32)
    for c in range(3):
        out_ref[APP_ROW + c : APP_ROW + c + 1, 0 : app_ref.shape[2]] = app_ref[c]
    again_ref[...] = out_ref[...]


def slot_mask(place_row):
    return (iota((TILE, place_row.shape[1]), 0) == place_row.astype(jnp.int32)).astype(F32)


def tile_onehot(tile_row, tiles):
    return (iota((tiles, tile_row.shape[1]), 0) == tile_row.astype(jnp.int32)).astype(F32).astype(BF16)


def cell_onehot(cells_ref, cells):
    return [
        (iota((cells, cells_ref.shape[1]), 0) == cells_ref[k : k + 1, :]).astype(F32)
        for k in range(cells_ref.shape[0])
    ]


def lane_select(channels, lanes):
    rows = channels * TILE
    row, column = iota((rows, channels * lanes), 0), iota((rows, channels * lanes), 1)
    same = (row // TILE == column // lanes) & (row % TILE == column % TILE)
    return same.astype(F32).astype(BF16)


def deal_kernel(
    cells,
    samples,
    cells_ref,
    geometry_ref,
    length_ref,
    jitter_ref,
    frequency_ref,
    own_ref,
    other_ref,
    meta_ref,
    spacing_ref,
    tile_cell_ref,
    tile_start_ref,
    position_ref,
    factor_ref,
    passed_ref,
):
    del own_ref, other_ref, passed_ref
    tiles = spacing_ref.shape[0]
    lanes = TILE * samples
    crossings, rays = cells_ref.shape
    segments = crossings * rays

    onehot = jnp.concatenate(cell_onehot(cells_ref, cells), axis=1)
    chunks = [onehot[:, 128 * c : 128 * (c + 1)] for c in range(segments // 128)]
    before = (iota((128, 128), 0) < iota((128, 128), 1)).astype(F32).astype(BF16)
    prefix = dot_nn(jnp.concatenate(chunks, axis=0).astype(BF16), before)
    running = jnp.zeros((cells, 1), F32)
    ranks = []
    for c, chunk in enumerate(chunks):
        earlier = prefix[cells * c : cells * (c + 1), :] + running
        ranks.append(jnp.sum(chunk * earlier, axis=0, keepdims=True))
        running = running + jnp.sum(chunk, axis=1, keepdims=True)
    rank = jnp.concatenate(ranks, axis=1)
    needed = jnp.broadcast_to(jnp.floor((running + (TILE - 1)) * (1.0 / TILE)), (cells, 128))
    lower = (iota((cells, cells), 1) < iota((cells, cells), 0)).astype(F32).astype(BF16)
    start = dot_nn(lower, needed.astype(BF16))
    inside = jnp.floor(rank * (1.0 / TILE))
    tile_row = jnp.sum(onehot * start[:, 0:1], axis=0, keepdims=True) + inside
    place_row = rank - inside * TILE
    meta_ref[...] = jnp.concatenate(
        [tile_row, place_row, jnp.zeros((6, segments), F32)], axis=0
    )
    ends = start[:, 0:1] + needed[:, 0:1]
    owner = jnp.sum(
        (ends <= iota((cells, tile_cell_ref.shape[1]), 1).astype(F32)).astype(F32),
        axis=0,
        keepdims=True,
    )
    owner = jnp.minimum(owner, cells - 1.0).astype(jnp.int32)
    tile_cell_ref[...] = jnp.broadcast_to(owner, tile_cell_ref.shape)
    tile_start_ref[0:cells, :] = start.astype(jnp.int32)
    tile_start_ref[cells : cells + 8, :] = jnp.broadcast_to(
        ends[cells - 1 : cells, :], (8, 128)
    ).astype(jnp.int32)

    mask = slot_mask(place_row)
    place = tile_onehot(tile_row, tiles)
    lengths = length_ref[...]
    near = jnp.zeros((1, rays), F32)
    nears, extents = [], []
    for k in range(crossings):
        nears.append(near)
        extents.append(lengths[k : k + 1, :])
        near = near + lengths[k : k + 1, :]
    rows = [
        jnp.concatenate([geometry_ref[c : c + 1, :]] * crossings, axis=1) for c in range(6)
    ]
    rows += [jnp.concatenate(nears, axis=1), jnp.concatenate(extents, axis=1)]
    wide = pick_nt(place, jnp.concatenate([mask * row for row in rows], axis=0))
    wide = pick_nn(wide, lane_select(8, lanes))
    channel = [wide[:, lanes * c : lanes * (c + 1)] for c in range(8)]
    turned = jitter_ref[...].T
    offsets = jnp.concatenate(
        [turned[samples * k : samples * (k + 1), :] for k in range(crossings)], axis=1
    )
    dealt = jnp.concatenate([mask * offsets[i : i + 1, :] for i in range(samples)], axis=0)
    jitter = pick_nt(place, dealt)
    step = (iota((tiles, lanes), 1) // TILE).astype(F32)
    near, extent = channel[6], channel[7]
    depths = near + extent * (step + jitter) / samples
    following = pltpu.roll(depths, lanes - TILE, 1)
    ending = jnp.where(iota((tiles, lanes), 1) >= lanes - TILE, near + extent, following)
    spacing_ref[...] = ending - depths
    for c in range(3):
        put_channel(position_ref, c, channel[c] + depths * channel[3 + c])
    for c in range(3, 8):
        put_channel(position_ref, c, jnp.zeros((tiles, lanes), F32))
    turns = frequency_ref[...] * 0.15915494309189535
    count = turns.shape[1]
    block = jnp.concatenate([turns, jnp.zeros((5, count), F32)], axis=0)
    block = jnp.concatenate([block, jnp.zeros((8, 128 - count), F32)], axis=1)
    high, mid, low = [part.astype(F32) for part in split3(block)]
    stack = [high, high, high, mid, mid, low, jnp.zeros((128 - 48, 128), F32)]
    factor_ref[...] = jnp.concatenate(stack, axis=0).T[0:count, 0:48].astype(BF16)


def encode(position_ref, factor, encoded_ref, some):
    phases = []
    for t in some:
        high, mid, low = split3(get_tile(position_ref, t))
        high, mid, low = high.astype(F32), mid.astype(F32), low.astype(F32)
        points = jnp.concatenate([high, mid, low, high, mid, high], axis=0).astype(BF16)
        phases.append(dot_nn(factor, points))
    for t, phase in zip(some, phases):
        phase = phase - jnp.round(phase)
        square = phase * phase
        sine, cosine = square * SIN[5] + SIN[4], square * COS[5] + COS[4]
        for c in (3, 2, 1, 0):
            sine, cosine = sine * square + SIN[c], cosine * square + COS[c]
        half = phase.shape[0]
        encoded_ref[t, 0:half, :] = (sine * phase).astype(BF16)
        encoded_ref[t, half:, :] = cosine.astype(BF16)


def step_kernel(
    cells,
    samples,
    tile_cell_ref,
    tile_start_ref,
    meta_ref,
    cells_ref,
    spacing_ref,
    position_ref,
    factor_ref,
    codes_ref,
    target_ref,
    *refs,
):
    weights, refs = refs[:cells], refs[cells:]
    (
        rendered_ref,
        codes_grad_ref,
        keep_near_ref,
        keep_far_ref,
        send_near_ref,
        send_far_ref,
        encoded_ref,
        first_ref,
        second_ref,
        forward1_ref,
        forward2_ref,
        backward2_ref,
        head_ref,
        head_turned_ref,
        outputs_ref,
        grads_ref,
        sums_ref,
        semaphore,
    ) = refs
    tiles, lanes = spacing_ref.shape
    crossings, rays = cells_ref.shape
    segments = crossings * rays
    width = codes_ref.shape[0]
    used = tile_start_ref[cells, 0]
    trips = (used + UNROLL - 1) // UNROLL

    appearance = []
    for v, ref in enumerate(weights):
        forward1_ref[v] = ref[0:128, :].astype(BF16)
        second = ref[128:256, :]
        forward2_ref[v] = second.astype(BF16)
        backward2_ref[v] = second.T.astype(BF16)
        tail = ref[HEAD_ROW:ROWS, :]
        head = jnp.where(iota((8, 128), 0) < 4, tail, 0.0)
        head_ref[v] = head.astype(BF16)
        square = jnp.concatenate([head, jnp.zeros((120, 128), F32)], axis=0)
        head_turned_ref[v] = square.T[:, 0:8].astype(BF16)
        appearance.append(tail)
    outputs_ref[...] = jnp.zeros_like(outputs_ref)
    sums_ref[...] = jnp.zeros_like(sums_ref)

    factor = factor_ref[...]
    encode(position_ref, factor, encoded_ref, range(UNROLL))

    def forward(trip, carry):
        following = jnp.minimum(trip + 1, trips - 1) * UNROLL
        some = [trip * UNROLL + u for u in range(UNROLL)]
        owner = [tile_cell_ref[0, t] for t in some]
        firsts = [dot_nn(forward1_ref[v], encoded_ref[t]) for t, v in zip(some, owner)]
        firsts = [jnp.maximum(first, 0.0).astype(BF16) for first in firsts]
        for t, first in zip(some, firsts):
            first_ref[t] = first
        seconds = [dot_nn(forward2_ref[v], first) for v, first in zip(owner, firsts)]
        seconds = [jnp.maximum(second, 0.0).astype(BF16) for second in seconds]
        for t, second in zip(some, seconds):
            second_ref[t] = second
        outputs = [dot_nn(head_ref[v], second) for v, second in zip(owner, seconds)]
        for t, output in zip(some, outputs):
            put_tile(outputs_ref, t, output)
        encode(position_ref, factor, encoded_ref, [following + u for u in range(UNROLL)])
        return carry

    lax.fori_loop(0, trips, forward, 0)

    tile_row, place_row = meta_ref[0:1, :], meta_ref[1:2, :]
    mask = slot_mask(place_row)
    place = tile_onehot(tile_row, tiles)
    onehots = cell_onehot(cells_ref, cells)
    maps = jnp.concatenate(
        [jnp.concatenate([tail[4 + c : 5 + c, :] for tail in appearance], axis=0) for c in range(3)],
        axis=0,
    )[:, 0:width]
    codes = codes_ref[...]
    shifts = exact_nn(maps, codes)
    rows = [
        jnp.concatenate(
            [
                jnp.sum(onehots[k] * shifts[cells * c : cells * (c + 1), :], axis=0, keepdims=True)
                for k in range(crossings)
            ],
            axis=1,
        )
        for c in range(3)
    ]
    spread3 = lane_select(4, lanes)
    shift = pick_nt(place, jnp.concatenate([mask * row for row in rows], axis=0))
    shift = pick_nn(shift, spread3[0:24, 0 : 3 * lanes])

    spacing = spacing_ref[...]
    raw = get_channel(outputs_ref, 0)
    ray = (iota((lanes, lanes), 0) % TILE) == (iota((lanes, lanes), 1) % TILE)
    earlier = (ray & (iota((lanes, lanes), 0) < iota((lanes, lanes), 1))).astype(F32).astype(BF16)
    later = (ray & (iota((lanes, lanes), 0) > iota((lanes, lanes), 1))).astype(F32).astype(BF16)
    total = ((iota((TILE, lanes), 1) % TILE) == iota((TILE, lanes), 0)).astype(F32).astype(BF16)
    density = jax.nn.softplus(raw)
    colors = [
        jax.nn.sigmoid(
            get_channel(outputs_ref, 1 + c) + shift[:, lanes * c : lanes * (c + 1)]
        )
        for c in range(3)
    ]
    optical = density * spacing
    transmit = jnp.exp(-pick_nn(optical, earlier))
    opacity = 1.0 - jnp.exp(-optical)
    blend = transmit * opacity
    sums = [pick_nt(total, blend * color) for color in colors] + [-pick_nt(total, optical)]
    dealt = pick_nn(jnp.concatenate(sums, axis=0), place)
    parts = [
        jnp.sum(mask * dealt[TILE * c : TILE * (c + 1), :], axis=0, keepdims=True) for c in range(4)
    ]

    def crossed(row, k):
        return row[:, rays * k : rays * (k + 1)]

    reach, logs = [], jnp.zeros((1, rays), F32)
    for k in range(crossings):
        reach.append(jnp.exp(logs))
        logs = logs + crossed(parts[3], k)
    residuals, channel_grads = [], [[] for _ in range(3)]
    for c in range(3):
        rendered = sum(reach[k] * crossed(parts[c], k) for k in range(crossings))
        rendered_ref[c : c + 1, :] = rendered
        residuals.append(rendered - target_ref[c : c + 1, :])
    log_grads, after = [], jnp.zeros((1, rays), F32)
    for k in reversed(range(crossings)):
        log_grads.append(after)
        weight = sum(residuals[c] * crossed(parts[c], k) for c in range(3))
        after = after + weight * reach[k]
    log_row = jnp.concatenate(log_grads[::-1], axis=1)
    color_rows = [
        jnp.concatenate([reach[k] * residuals[c] for k in range(crossings)], axis=1)
        for c in range(3)
    ]
    back = pick_nt(place, jnp.concatenate([mask * row for row in color_rows + [log_row]], axis=0))
    back = pick_nn(back, spread3)
    color_grads = [back[:, lanes * c : lanes * (c + 1)] for c in range(3)]
    log_grad = back[:, 3 * lanes : 4 * lanes]

    blend_grad = sum(color_grads[c] * colors[c] for c in range(3))
    before_grad = -(blend_grad * opacity) * transmit
    optical_grad = blend_grad * transmit * (1.0 - opacity) - log_grad
    optical_grad = optical_grad + pick_nn(before_grad, later)
    put_channel(grads_ref, 0, optical_grad * spacing * jax.nn.sigmoid(raw))
    logits = []
    for c in range(3):
        logit = color_grads[c] * blend * colors[c] * (1.0 - colors[c])
        put_channel(grads_ref, 1 + c, logit)
        put_channel(grads_ref, 4 + c, jnp.zeros((tiles, lanes), F32))
        logits.append(pick_nt(total, logit))
    put_channel(grads_ref, 7, jnp.zeros((tiles, lanes), F32))
    dealt = pick_nn(jnp.concatenate(logits, axis=0), place)
    per_cell = []
    for c in range(3):
        row = jnp.sum(mask * dealt[TILE * c : TILE * (c + 1), :], axis=0, keepdims=True)
        per_cell.append(sum(onehots[k] * crossed(row, k) for k in range(crossings)))
    per_cell = jnp.concatenate(per_cell, axis=0)
    map_grads = exact_nn(per_cell, codes.T)
    codes_grad_ref[...] = exact_nn(maps.T, per_cell)
    for v in range(cells):
        for c in range(3):
            sums_ref[v, APP_ROW + c : APP_ROW + c + 1, 0:width] = map_grads[
                cells * c + v : cells * c + v + 1, :
            ]

    def backward(trip, carry):
        some = [trip * UNROLL + u for u in range(UNROLL)]
        owner = [tile_cell_ref[0, t] for t in some]
        outputs = [get_tile(grads_ref, t).astype(BF16) for t in some]
        second_grads = [dot_nn(head_turned_ref[v], output) for v, output in zip(owner, outputs)]
        second_grads = [
            jnp.where(second_ref[t] > 0, grad.astype(BF16), jnp.zeros((), BF16))
            for t, grad in zip(some, second_grads)
        ]
        first_grads = [dot_nn(backward2_ref[v], grad) for v, grad in zip(owner, second_grads)]
        first_grads = [
            jnp.where(first_ref[t] > 0, grad.astype(BF16), jnp.zeros((), BF16))
            for t, grad in zip(some, first_grads)
        ]
        head_parts = [dot_nt(output, second_ref[t]) for t, output in zip(some, outputs)]
        second_parts = [dot_nt(first_ref[t], grad) for t, grad in zip(some, second_grads)]
        first_parts = [dot_nt(encoded_ref[t], grad) for t, grad in zip(some, first_grads)]
        for v, head, second, first in zip(owner, head_parts, second_parts, first_parts):
            sums_ref[v, HEAD_ROW:ROWS, :] += head
            sums_ref[v, 128:256, :] += second
            sums_ref[v, 0:128, :] += first
        return carry

    num_cell = cells // 4
    copies = []

    def emit(half):
        for district in (2 * half + 1, 2 * half):
            members = sums_ref.at[pl.ds(district * num_cell, num_cell)]
            total = sums_ref[district * num_cell]
            for s in range(1, num_cell):
                total = total + sums_ref[district * num_cell + s]
            sums_ref[cells + district] = total
            out_ref = (keep_near_ref, keep_far_ref, send_near_ref, send_far_ref)[district]
            for source, sink in (
                (members, out_ref.at[pl.ds(0, num_cell)]),
                (sums_ref.at[cells + district], out_ref.at[num_cell]),
            ):
                copies.append(pltpu.make_async_copy(source, sink, semaphore.at[len(copies)]))
                copies[-1].start()

    middle = (tile_start_ref[cells // 2, 0] + UNROLL - 1) // UNROLL
    lax.fori_loop(0, middle, backward, 0)
    emit(0)
    lax.fori_loop(middle, trips, backward, 0)
    emit(1)
    for copy in copies:
        copy.wait()


def resident(
    ray_geometry,
    segment_length,
    jitter,
    appearance_codes,
    target,
    crossing,
    frequencies,
    cell_layers,
    district_prior,
    head_weight,
    appearance_weight,
):
    num_cell = lax.axis_size("cell")
    num_district = lax.axis_size("district")
    cells = num_cell * num_district
    rays, crossings = crossing.shape
    samples = jitter.shape[1] // crossings
    segments = rays * crossings
    width = appearance_codes.shape[1]
    lanes = TILE * samples
    tiles = -(-(segments // TILE + cells) // UNROLL) * UNROLL
    me_cell, me_district = lax.axis_index("cell"), lax.axis_index("district")

    def flip(x, bits, axis="district"):
        return lax.ppermute(x, axis, [(i, i ^ bits) for i in range(lax.axis_size(axis))])

    own, again = pl.pallas_call(
        pack_kernel, out_shape=[jax.ShapeDtypeStruct((ROWS, 128), F32)] * 2, name="pack"
    )(cell_layers, district_prior, head_weight, jnp.transpose(appearance_weight, (1, 0, 2)))
    vmem, smem = pl.BlockSpec(memory_space=pltpu.VMEM), pl.BlockSpec(memory_space=pltpu.SMEM)
    anywhere = pl.BlockSpec(memory_space=pl.ANY)
    params = pltpu.CompilerParams(vmem_limit_bytes=VMEM_LIMIT)

    crossed_own = flip(own, 2)
    away = (crossing & 3) ^ me_district
    steps = (crossing >> 2) ^ me_cell
    virtual = (((away & 1) * 2 + (away >> 1)) * num_cell + steps).T
    halves = lanes // 128
    default = pl.BlockSpec()
    meta, spacing, tile_cell, tile_start, position, factor, passed = pl.pallas_call(
        functools.partial(deal_kernel, cells, samples),
        in_specs=[default] * 5 + [anywhere, anywhere],
        out_specs=[default] * 6 + [anywhere],
        input_output_aliases={5: 6},
        out_shape=[
            jax.ShapeDtypeStruct((8, segments), F32),
            jax.ShapeDtypeStruct((tiles, lanes), F32),
            jax.ShapeDtypeStruct((8, 256), jnp.int32),
            jax.ShapeDtypeStruct((cells + 8, 128), jnp.int32),
            jax.ShapeDtypeStruct((halves, tiles * 8, 128), F32),
            jax.ShapeDtypeStruct((frequencies.shape[1], 48), BF16),
            jax.ShapeDtypeStruct((ROWS, 128), F32),
        ],
        compiler_params=params,
        cost_estimate=pl.CostEstimate(flops=6 << 30, bytes_accessed=4 << 20, transcendentals=0),
        name="deal",
    )(virtual, ray_geometry, segment_length.T, jitter, frequencies, again, crossed_own)
    near = [own]
    for s in range(1, num_cell):
        near.append(flip(near[s & (s - 1)], s & -s, "cell"))
    flipped = [crossed_own] + [flip(piece, 2) for piece in near[1:]]
    weights = near + flipped + [flip(piece, 1) for piece in [passed] + near[1:] + flipped]


    rendered, codes_grad, keep, keep_far, send, send_far = pl.pallas_call(
        functools.partial(step_kernel, cells, samples),
        in_specs=[smem, smem] + [vmem] * (7 + cells),
        out_specs=[vmem, vmem, anywhere, vmem, anywhere, anywhere],
        out_shape=[
            jax.ShapeDtypeStruct((3, rays), F32),
            jax.ShapeDtypeStruct((width, rays), F32),
            *[jax.ShapeDtypeStruct((num_cell + 1, ROWS, 128), F32)] * 4,
        ],
        scratch_shapes=[
            pltpu.VMEM((tiles, 128, lanes), BF16),
            pltpu.VMEM((tiles, 128, lanes), BF16),
            pltpu.VMEM((tiles, 128, lanes), BF16),
            pltpu.VMEM((cells, 128, 128), BF16),
            pltpu.VMEM((cells, 128, 128), BF16),
            pltpu.VMEM((cells, 128, 128), BF16),
            pltpu.VMEM((cells, 8, 128), BF16),
            pltpu.VMEM((cells, 128, 8), BF16),
            pltpu.VMEM((halves, tiles * 8, 128), F32),
            pltpu.VMEM((halves, tiles * 8, 128), F32),
            pltpu.VMEM((cells + 4, ROWS, 128), F32),
            pltpu.SemaphoreType.DMA((8,)),
        ],
        compiler_params=params,
        name="step",
    )(
        tile_cell,
        tile_start,
        meta,
        virtual,
        spacing,
        position,
        factor,
        appearance_codes.T,
        target,
        *weights,
    )

    cross_far, crossed = flip(send_far, 1), flip(send, 1)
    order = [3, 2, num_cell, 1, 0]
    pieces = {s: flip(keep_far[s] + cross_far[s], 2) for s in order}
    for s in order:
        near_part, cross_part, other = lax.optimization_barrier((keep[s], crossed[s], pieces[s]))
        pieces[s] = near_part + cross_part + other
    prior = pieces[num_cell][0:HEAD_ROW]
    bit = num_cell // 2
    while bit > 0:
        prior = prior + flip(prior, bit, "cell")
        bit //= 2
    prior = (prior / num_cell).reshape(2, 128, 128)
    bit = 1
    while bit < num_cell:
        for s in reversed(range(bit, num_cell, 2 * bit)):
            pieces[s - bit] = pieces[s - bit] + flip(pieces[s], bit, "cell")
        bit *= 2
    own_sum = pieces[0]
    return (
        rendered,
        own_sum[0:HEAD_ROW].reshape(1, 2, 128, 128),
        prior[None],
        own_sum[None, HEAD_ROW : HEAD_ROW + 4],
        own_sum[None, APP_ROW : APP_ROW + 3, 0:width],
        codes_grad.T,
    )


def local(*args):
    cells = lax.axis_size("cell") * lax.axis_size("district")
    if cells <= 16 and lax.axis_size("district") == 4:
        return resident(*args)
    return routed(*args)


def solution(mesh):
    placed = (
        P(None, ("scene", "cell", "district")),
        P(("scene", "cell", "district"), None),
        P(("scene", "cell", "district"), None),
        P(("scene", "cell", "district"), None),
        P(None, ("scene", "cell", "district")),
        P(("scene", "cell", "district"), None),
        P(),
        P(("scene", "cell", "district"), None, None, None),
        P(("scene", "district"), None, None, None),
        P(("scene", "cell", "district"), None, None),
        P(("scene", "cell", "district"), None, None),
    )
    return jax.shard_map(
        local,
        mesh=mesh,
        in_specs=placed,
        out_specs=(
            P(None, ("scene", "cell", "district")),
            P(("scene", "cell", "district"), None, None, None),
            P(("scene", "district"), None, None, None),
            P(("scene", "cell", "district"), None, None),
            P(("scene", "cell", "district"), None, None),
            P(("scene", "cell", "district"), None),
        ),
        check_vma=False,
    )
```

```python
import functools

import jax
import jax.numpy as jnp
from jax import lax
from jax.experimental import pallas as pl
from jax.experimental.pallas import tpu as pltpu
from jax.sharding import PartitionSpec as P

GEOMETRY = 8
HIGHEST_PRECISION = lax.Precision.HIGHEST


def build_front(ray_geometry, segment_length, jitter):
    ray_count, crossings = segment_length.shape
    samples = jitter.shape[1] // crossings
    near_depth = jnp.cumsum(segment_length, axis=1) - segment_length
    geometry = jnp.broadcast_to(ray_geometry.T[:, None, :], (ray_count, crossings, 6))
    front = jnp.concatenate(
        [
            geometry,
            near_depth[:, :, None],
            segment_length[:, :, None],
            jitter.reshape(ray_count, crossings, samples),
        ],
        axis=2,
    )
    return front.reshape(ray_count * crossings, front.shape[2])


def slot_positions(crossing, cell_total, capacity):
    target_cell = crossing.reshape(-1)
    total_rows = target_cell.shape[0]
    onehot = target_cell[:, None] == jnp.arange(cell_total, dtype=jnp.int32)[None, :]
    triangle = (
        lax.broadcasted_iota(jnp.int32, (total_rows, total_rows), 0)
        > lax.broadcasted_iota(jnp.int32, (total_rows, total_rows), 1)
    ).astype(jnp.bfloat16)
    earlier = jnp.dot(triangle, onehot.astype(jnp.bfloat16), preferred_element_type=jnp.float32)
    position = jnp.sum(jnp.where(onehot, earlier, 0.0), axis=1).astype(jnp.int32)
    return target_cell * capacity + position


def sample_spacing(payload, samples):
    near_depth = payload[:, 6:7]
    extent = payload[:, 7:8]
    offsets = jnp.arange(samples, dtype=jnp.float32)[None, :]
    depths = near_depth + extent * (offsets + payload[:, GEOMETRY : GEOMETRY + samples]) / samples
    ending = jnp.concatenate([depths[:, 1:], near_depth + extent], axis=1)
    return (depths, ending - depths)


def cell_forward(payload, frequencies, first_weight, second_weight, head_one, samples):
    depths, spacing = sample_spacing(payload, samples)
    phases = jnp.zeros((payload.shape[0], samples, frequencies.shape[1]), jnp.float32)
    for component in range(3):
        position = (
            payload[:, component : component + 1]
            + depths * payload[:, 3 + component : 4 + component]
        )
        phases = phases + position[:, :, None] * frequencies[component][None, None, :]
    encoded = jnp.concatenate([jnp.sin(phases), jnp.cos(phases)], axis=2)
    encoded = encoded.reshape(payload.shape[0] * samples, encoded.shape[2]).astype(jnp.bfloat16)
    first_act = jax.nn.relu(
        jnp.dot(encoded, first_weight, preferred_element_type=jnp.float32)
    ).astype(jnp.bfloat16)
    second_act = jax.nn.relu(
        jnp.dot(first_act, second_weight, preferred_element_type=jnp.float32)
    ).astype(jnp.bfloat16)
    raw_outputs = lax.dot_general(
        head_one, second_act, (((1,), (1,)), ((), ())), preferred_element_type=jnp.float32
    )
    return ((encoded, first_act, second_act, raw_outputs), spacing)


def shade(raw_outputs, payload, spacing, appearance_one, samples):
    slot_count = payload.shape[0]
    outputs = raw_outputs.reshape(4, slot_count, samples)
    code_part = payload[:, GEOMETRY + samples :]
    color_shift = jnp.dot(code_part, appearance_one.T, precision=HIGHEST_PRECISION)
    density = jax.nn.softplus(outputs[0])
    colors = jax.nn.sigmoid(outputs[1:] + color_shift.T[:, :, None])
    optical = density * spacing
    transmit = jnp.exp(-(jnp.cumsum(optical, axis=1) - optical))
    opacity = 1.0 - jnp.exp(-optical)
    blend_weight = transmit * opacity
    return (outputs, colors, optical, transmit, opacity, blend_weight, code_part)


def segment_partials(raw_outputs, payload, spacing, appearance_one, samples):
    shaded = shade(raw_outputs, payload, spacing, appearance_one, samples)
    colors, optical, blend_weight = (shaded[1], shaded[2], shaded[5])
    segment_color = jnp.sum(blend_weight[None] * colors, axis=2)
    segment_log = -jnp.sum(optical, axis=1)
    return jnp.concatenate([segment_color.T, segment_log[:, None]], axis=1)


def cell_backward(
    payload, saved_acts, spacing, cotangent, second_weight, head_one, appearance_one, samples
):
    encoded, first_act, second_act, raw_outputs = saved_acts
    outputs, colors, optical, transmit, opacity, blend_weight, code_part = shade(
        raw_outputs, payload, spacing, appearance_one, samples
    )
    color_grad = cotangent[:, :3].T
    log_grad = cotangent[:, 3]
    blend_grad = jnp.sum(color_grad[:, :, None] * colors, axis=0)
    colors_grad = color_grad[:, :, None] * blend_weight[None]
    transmit_grad = blend_grad * opacity
    optical_grad = blend_grad * transmit * (1.0 - opacity) - log_grad[:, None]
    before_grad = -transmit_grad * transmit
    later_sum = jnp.flip(jnp.cumsum(jnp.flip(before_grad, axis=1), axis=1), axis=1) - before_grad
    optical_grad = optical_grad + later_sum
    density_grad = optical_grad * spacing * jax.nn.sigmoid(outputs[0])
    logit_grad = colors_grad * colors * (1.0 - colors)
    slot_count = payload.shape[0]
    output_grad = (
        jnp.concatenate([density_grad[None], logit_grad], axis=0)
        .reshape(4, slot_count * samples)
        .astype(jnp.bfloat16)
    )
    head_grad = jnp.dot(output_grad, second_act, preferred_element_type=jnp.float32)
    shift_grad = jnp.sum(logit_grad, axis=2)
    second_grad = lax.dot_general(
        output_grad, head_one, (((0,), (0,)), ((), ())), preferred_element_type=jnp.float32
    )
    second_grad = jnp.where(second_act > 0, second_grad, 0.0).astype(jnp.bfloat16)
    second_weight_grad = lax.dot_general(
        first_act, second_grad, (((0,), (0,)), ((), ())), preferred_element_type=jnp.float32
    )
    first_grad = lax.dot_general(
        second_grad, second_weight, (((1,), (1,)), ((), ())), preferred_element_type=jnp.float32
    )
    first_grad = jnp.where(first_act > 0, first_grad, 0.0).astype(jnp.bfloat16)
    first_weight_grad = lax.dot_general(
        encoded, first_grad, (((0,), (0,)), ((), ())), preferred_element_type=jnp.float32
    )
    return (first_weight_grad, second_weight_grad, head_grad, shift_grad, code_part)


def composite(gathered, target):
    segment_color = gathered[:, :, :3]
    segment_log = gathered[:, :, 3]
    reach_weight = jnp.exp(jnp.cumsum(segment_log, axis=1) - segment_log)
    rendered = jnp.sum(reach_weight[:, :, None] * segment_color, axis=1).T
    residual = rendered - target
    color_grad = reach_weight[:, :, None] * residual.T[:, None, :]
    reach_grad = jnp.sum(residual.T[:, None, :] * segment_color, axis=2) * reach_weight
    log_grad = jnp.flip(jnp.cumsum(jnp.flip(reach_grad, axis=1), axis=1), axis=1) - reach_grad
    return (rendered, jnp.concatenate([color_grad, log_grad[:, :, None]], axis=2))


def routed(
    ray_geometry,
    segment_length,
    jitter,
    appearance_codes,
    target,
    crossing,
    frequencies,
    cell_layers,
    district_prior,
    head_weight,
    appearance_weight,
):
    num_cell = lax.axis_size("cell")
    num_district = lax.axis_size("district")
    cell_total = num_cell * num_district
    ray_count, crossings = crossing.shape
    samples = jitter.shape[1] // crossings
    segments = ray_count * crossings
    capacity = 2 * segments // cell_total
    slot_total = cell_total * capacity
    code_width = appearance_codes.shape[1]
    front = build_front(ray_geometry, segment_length, jitter)
    codes_seg = jnp.broadcast_to(
        appearance_codes[:, None, :], (ray_count, crossings, code_width)
    ).reshape(segments, code_width)
    payload = jnp.concatenate([front, codes_seg], axis=1)
    appearance_one = appearance_weight[0]
    row_width = payload.shape[1]
    places = slot_positions(crossing, cell_total, capacity)
    outbox = (
        jnp.zeros((slot_total, row_width), jnp.float32)
        .at[places]
        .set(payload)
        .reshape(cell_total, capacity * row_width)
    )
    arrived = lax.all_to_all(outbox, ("cell", "district"), split_axis=0, concat_axis=0, tiled=True)
    arrived = arrived.reshape(slot_total, row_width)
    effective = (cell_layers[0].astype(jnp.float32) + district_prior[0].astype(jnp.float32)).astype(
        jnp.bfloat16
    )
    head_one = head_weight[0]
    block_rows = min(512, slot_total)
    blocked = arrived.reshape(slot_total // block_rows, block_rows, row_width)

    def forward_keep(slot_rows):
        saved_acts, spacing = cell_forward(
            slot_rows, frequencies, effective[0], effective[1], head_one, samples
        )
        return (
            segment_partials(saved_acts[3], slot_rows, spacing, appearance_one, samples),
            saved_acts,
        )

    partials, stored = lax.map(forward_keep, blocked)
    partials = partials.reshape(cell_total, capacity * 4)
    returned = lax.all_to_all(
        partials, ("cell", "district"), split_axis=0, concat_axis=0, tiled=True
    )
    returned = returned.reshape(slot_total, 4)
    rendered, cotangent = composite(returned[places].reshape(ray_count, crossings, 4), target)
    grad_box = (
        jnp.zeros((slot_total, 4), jnp.float32)
        .at[places]
        .set(cotangent.reshape(segments, 4))
        .reshape(cell_total, capacity * 4)
    )
    incoming = lax.all_to_all(
        grad_box, ("cell", "district"), split_axis=0, concat_axis=0, tiled=True
    )
    incoming = incoming.reshape(slot_total // block_rows, block_rows, 4)

    def finish(result):
        first_part, second_part, head_part, shift_grad, code_part = result
        appearance_part = jnp.dot(shift_grad, code_part, precision=HIGHEST_PRECISION)
        code_part_grad = jnp.dot(shift_grad.T, appearance_one, precision=HIGHEST_PRECISION)
        return (first_part, second_part, head_part, appearance_part, code_part_grad)

    def backward_keep(bundle):
        slot_rows, incoming_rows, saved_acts = bundle
        spacing = sample_spacing(slot_rows, samples)[1]
        return finish(
            cell_backward(
                slot_rows,
                saved_acts,
                spacing,
                incoming_rows,
                effective[1],
                head_one,
                appearance_one,
                samples,
            )
        )

    pieces = lax.map(backward_keep, (blocked, incoming, stored))
    first_w = jnp.sum(pieces[0], axis=0)
    second_w = jnp.sum(pieces[1], axis=0)
    head_grad = jnp.sum(pieces[2], axis=0)
    appearance_grad = jnp.sum(pieces[3], axis=0)
    code_box = pieces[4].reshape(cell_total, capacity * code_width)
    code_back = lax.all_to_all(
        code_box, ("cell", "district"), split_axis=0, concat_axis=0, tiled=True
    )
    code_back = code_back.reshape(slot_total, code_width)
    grad_codes = jnp.sum(code_back[places].reshape(ray_count, crossings, code_width), axis=1)
    grad_pair = jnp.stack([first_w, second_w], axis=0)
    grad_prior = lax.psum(grad_pair, "cell") / num_cell
    return (
        rendered,
        grad_pair[None],
        grad_prior[None],
        head_grad[None],
        appearance_grad[None],
        grad_codes,
    )


TILE = 8
UNROLL = 16
ROWS = 264
HEAD_ROW = 256
APP_ROW = 260
VMEM_LIMIT = 48 * 1024 * 1024
SIN = (
    6.283185005187988,
    -41.341590881347656,
    81.59994506835938,
    -76.61447143554688,
    41.3428840637207,
    -12.471243858337402,
)
COS = (
    0.9999992251396179,
    -19.738981246948242,
    64.92865753173828,
    -85.27162170410156,
    58.79049301147461,
    -21.07110595703125,
)
F32 = jnp.float32
BF16 = jnp.bfloat16


def iota(shape, axis):
    return lax.broadcasted_iota(jnp.int32, shape, axis)


def dot_nn(a, b):
    return jnp.dot(a, b, preferred_element_type=F32)


def dot_nt(a, b):
    return lax.dot_general(a, b, (((1,), (1,)), ((), ())), preferred_element_type=F32)


def split3(x):
    high = x.astype(BF16)
    rest = x - high.astype(F32)
    mid = rest.astype(BF16)
    low = (rest - mid.astype(F32)).astype(BF16)
    return high, mid, low


def pick_nn(x, select):
    rows = x.shape[0]
    parts = jnp.concatenate([part.astype(F32) for part in split3(x)], axis=0)
    parts = dot_nn(parts.astype(BF16), select)
    return (parts[2 * rows :] + parts[rows : 2 * rows]) + parts[:rows]


def pick_nt(select, x):
    high, mid, low = split3(x)
    return (dot_nt(select, low) + dot_nt(select, mid)) + dot_nt(select, high)


def exact_nn(a, b):
    return jnp.dot(a, b, precision=HIGHEST_PRECISION, preferred_element_type=F32)


def put_channel(ref, c, x):
    for h in range(ref.shape[0]):
        ref[h, pl.ds(c, x.shape[0], 8), :] = x[:, 128 * h : 128 * (h + 1)]


def get_channel(ref, c):
    tiles = ref.shape[1] // 8
    return jnp.concatenate([ref[h, pl.ds(c, tiles, 8), :] for h in range(ref.shape[0])], axis=1)


def get_tile(ref, t):
    rows = pl.ds(pl.multiple_of(t * 8, 8), 8)
    return jnp.concatenate([ref[h, rows, :] for h in range(ref.shape[0])], axis=1)


def put_tile(ref, t, x):
    rows = pl.ds(pl.multiple_of(t * 8, 8), 8)
    for h in range(ref.shape[0]):
        ref[h, rows, :] = x[:, 128 * h : 128 * (h + 1)]


def pack_kernel(layers_ref, prior_ref, head_ref, app_ref, out_ref, again_ref):
    for layer in range(2):
        both = layers_ref[0, layer].astype(F32) + prior_ref[0, layer].astype(F32)
        out_ref[128 * layer : 128 * (layer + 1), :] = both.T
    out_ref[HEAD_ROW:ROWS, :] = jnp.zeros((ROWS - HEAD_ROW, 128), F32)
    out_ref[HEAD_ROW : HEAD_ROW + 4, :] = head_ref[0].astype(F32)
    for c in range(3):
        out_ref[APP_ROW + c : APP_ROW + c + 1, 0 : app_ref.shape[2]] = app_ref[c]
    again_ref[...] = out_ref[...]


def slot_mask(place_row):
    return (iota((TILE, place_row.shape[1]), 0) == place_row.astype(jnp.int32)).astype(F32)


def tile_onehot(tile_row, tiles):
    return (iota((tiles, tile_row.shape[1]), 0) == tile_row.astype(jnp.int32)).astype(F32).astype(BF16)


def cell_onehot(cells_ref, cells):
    return [
        (iota((cells, cells_ref.shape[1]), 0) == cells_ref[k : k + 1, :]).astype(F32)
        for k in range(cells_ref.shape[0])
    ]


def lane_select(channels, lanes):
    rows = channels * TILE
    row, column = iota((rows, channels * lanes), 0), iota((rows, channels * lanes), 1)
    same = (row // TILE == column // lanes) & (row % TILE == column % TILE)
    return same.astype(F32).astype(BF16)


def deal_kernel(
    cells,
    samples,
    cells_ref,
    geometry_ref,
    length_ref,
    jitter_ref,
    frequency_ref,
    own_ref,
    other_ref,
    meta_ref,
    spacing_ref,
    tile_cell_ref,
    tile_start_ref,
    position_ref,
    factor_ref,
    passed_ref,
):
    del own_ref, other_ref, passed_ref
    tiles = spacing_ref.shape[0]
    lanes = TILE * samples
    crossings, rays = cells_ref.shape
    segments = crossings * rays

    onehot = jnp.concatenate(cell_onehot(cells_ref, cells), axis=1)
    chunks = [onehot[:, 128 * c : 128 * (c + 1)] for c in range(segments // 128)]
    before = (iota((128, 128), 0) < iota((128, 128), 1)).astype(F32).astype(BF16)
    prefix = dot_nn(jnp.concatenate(chunks, axis=0).astype(BF16), before)
    running = jnp.zeros((cells, 1), F32)
    ranks = []
    for c, chunk in enumerate(chunks):
        earlier = prefix[cells * c : cells * (c + 1), :] + running
        ranks.append(jnp.sum(chunk * earlier, axis=0, keepdims=True))
        running = running + jnp.sum(chunk, axis=1, keepdims=True)
    rank = jnp.concatenate(ranks, axis=1)
    needed = jnp.broadcast_to(jnp.floor((running + (TILE - 1)) * (1.0 / TILE)), (cells, 128))
    lower = (iota((cells, cells), 1) < iota((cells, cells), 0)).astype(F32).astype(BF16)
    start = dot_nn(lower, needed.astype(BF16))
    inside = jnp.floor(rank * (1.0 / TILE))
    tile_row = jnp.sum(onehot * start[:, 0:1], axis=0, keepdims=True) + inside
    place_row = rank - inside * TILE
    meta_ref[...] = jnp.concatenate(
        [tile_row, place_row, jnp.zeros((6, segments), F32)], axis=0
    )
    ends = start[:, 0:1] + needed[:, 0:1]
    owner = jnp.sum(
        (ends <= iota((cells, tile_cell_ref.shape[1]), 1).astype(F32)).astype(F32),
        axis=0,
        keepdims=True,
    )
    owner = jnp.minimum(owner, cells - 1.0).astype(jnp.int32)
    tile_cell_ref[...] = jnp.broadcast_to(owner, tile_cell_ref.shape)
    tile_start_ref[0:cells, :] = start.astype(jnp.int32)
    tile_start_ref[cells : cells + 8, :] = jnp.broadcast_to(
        ends[cells - 1 : cells, :], (8, 128)
    ).astype(jnp.int32)

    mask = slot_mask(place_row)
    place = tile_onehot(tile_row, tiles)
    lengths = length_ref[...]
    near = jnp.zeros((1, rays), F32)
    nears, extents = [], []
    for k in range(crossings):
        nears.append(near)
        extents.append(lengths[k : k + 1, :])
        near = near + lengths[k : k + 1, :]
    rows = [
        jnp.concatenate([geometry_ref[c : c + 1, :]] * crossings, axis=1) for c in range(6)
    ]
    rows += [jnp.concatenate(nears, axis=1), jnp.concatenate(extents, axis=1)]
    wide = pick_nt(place, jnp.concatenate([mask * row for row in rows], axis=0))
    wide = pick_nn(wide, lane_select(8, lanes))
    channel = [wide[:, lanes * c : lanes * (c + 1)] for c in range(8)]
    turned = jitter_ref[...].T
    offsets = jnp.concatenate(
        [turned[samples * k : samples * (k + 1), :] for k in range(crossings)], axis=1
    )
    dealt = jnp.concatenate([mask * offsets[i : i + 1, :] for i in range(samples)], axis=0)
    jitter = pick_nt(place, dealt)
    step = (iota((tiles, lanes), 1) // TILE).astype(F32)
    near, extent = channel[6], channel[7]
    depths = near + extent * (step + jitter) / samples
    following = pltpu.roll(depths, lanes - TILE, 1)
    ending = jnp.where(iota((tiles, lanes), 1) >= lanes - TILE, near + extent, following)
    spacing_ref[...] = ending - depths
    for c in range(3):
        put_channel(position_ref, c, channel[c] + depths * channel[3 + c])
    for c in range(3, 8):
        put_channel(position_ref, c, jnp.zeros((tiles, lanes), F32))
    turns = frequency_ref[...] * 0.15915494309189535
    count = turns.shape[1]
    block = jnp.concatenate([turns, jnp.zeros((5, count), F32)], axis=0)
    block = jnp.concatenate([block, jnp.zeros((8, 128 - count), F32)], axis=1)
    high, mid, low = [part.astype(F32) for part in split3(block)]
    stack = [high, high, high, mid, mid, low, jnp.zeros((128 - 48, 128), F32)]
    factor_ref[...] = jnp.concatenate(stack, axis=0).T[0:count, 0:48].astype(BF16)


def encode(position_ref, factor, encoded_ref, some):
    phases = []
    for t in some:
        high, mid, low = split3(get_tile(position_ref, t))
        high, mid, low = high.astype(F32), mid.astype(F32), low.astype(F32)
        points = jnp.concatenate([high, mid, low, high, mid, high], axis=0).astype(BF16)
        phases.append(dot_nn(factor, points))
    for t, phase in zip(some, phases):
        phase = phase - jnp.round(phase)
        square = phase * phase
        sine, cosine = square * SIN[5] + SIN[4], square * COS[5] + COS[4]
        for c in (3, 2, 1, 0):
            sine, cosine = sine * square + SIN[c], cosine * square + COS[c]
        half = phase.shape[0]
        encoded_ref[t, 0:half, :] = (sine * phase).astype(BF16)
        encoded_ref[t, half:, :] = cosine.astype(BF16)


def step_kernel(
    cells,
    samples,
    tile_cell_ref,
    tile_start_ref,
    meta_ref,
    cells_ref,
    spacing_ref,
    position_ref,
    factor_ref,
    codes_ref,
    target_ref,
    *refs,
):
    weights, refs = refs[:cells], refs[cells:]
    (
        rendered_ref,
        codes_grad_ref,
        keep_near_ref,
        keep_far_ref,
        send_near_ref,
        send_far_ref,
        encoded_ref,
        first_ref,
        second_ref,
        forward1_ref,
        forward2_ref,
        backward2_ref,
        head_ref,
        head_turned_ref,
        outputs_ref,
        grads_ref,
        sums_ref,
        semaphore,
    ) = refs
    tiles, lanes = spacing_ref.shape
    crossings, rays = cells_ref.shape
    segments = crossings * rays
    width = codes_ref.shape[0]
    used = tile_start_ref[cells, 0]
    trips = (used + UNROLL - 1) // UNROLL

    appearance = []
    for v, ref in enumerate(weights):
        forward1_ref[v] = ref[0:128, :].astype(BF16)
        second = ref[128:256, :]
        forward2_ref[v] = second.astype(BF16)
        backward2_ref[v] = second.T.astype(BF16)
        tail = ref[HEAD_ROW:ROWS, :]
        head = jnp.where(iota((8, 128), 0) < 4, tail, 0.0)
        head_ref[v] = head.astype(BF16)
        square = jnp.concatenate([head, jnp.zeros((120, 128), F32)], axis=0)
        head_turned_ref[v] = square.T[:, 0:8].astype(BF16)
        appearance.append(tail)
    outputs_ref[...] = jnp.zeros_like(outputs_ref)
    sums_ref[...] = jnp.zeros_like(sums_ref)

    factor = factor_ref[...]
    encode(position_ref, factor, encoded_ref, range(UNROLL))

    def forward(trip, carry):
        following = jnp.minimum(trip + 1, trips - 1) * UNROLL
        some = [trip * UNROLL + u for u in range(UNROLL)]
        owner = [tile_cell_ref[0, t] for t in some]
        firsts = [dot_nn(forward1_ref[v], encoded_ref[t]) for t, v in zip(some, owner)]
        firsts = [jnp.maximum(first, 0.0).astype(BF16) for first in firsts]
        for t, first in zip(some, firsts):
            first_ref[t] = first
        seconds = [dot_nn(forward2_ref[v], first) for v, first in zip(owner, firsts)]
        seconds = [jnp.maximum(second, 0.0).astype(BF16) for second in seconds]
        for t, second in zip(some, seconds):
            second_ref[t] = second
        outputs = [dot_nn(head_ref[v], second) for v, second in zip(owner, seconds)]
        for t, output in zip(some, outputs):
            put_tile(outputs_ref, t, output)
        encode(position_ref, factor, encoded_ref, [following + u for u in range(UNROLL)])
        return carry

    lax.fori_loop(0, trips, forward, 0)

    tile_row, place_row = meta_ref[0:1, :], meta_ref[1:2, :]
    mask = slot_mask(place_row)
    place = tile_onehot(tile_row, tiles)
    onehots = cell_onehot(cells_ref, cells)
    maps = jnp.concatenate(
        [jnp.concatenate([tail[4 + c : 5 + c, :] for tail in appearance], axis=0) for c in range(3)],
        axis=0,
    )[:, 0:width]
    codes = codes_ref[...]
    shifts = exact_nn(maps, codes)
    rows = [
        jnp.concatenate(
            [
                jnp.sum(onehots[k] * shifts[cells * c : cells * (c + 1), :], axis=0, keepdims=True)
                for k in range(crossings)
            ],
            axis=1,
        )
        for c in range(3)
    ]
    spread3 = lane_select(4, lanes)
    shift = pick_nt(place, jnp.concatenate([mask * row for row in rows], axis=0))
    shift = pick_nn(shift, spread3[0:24, 0 : 3 * lanes])

    spacing = spacing_ref[...]
    raw = get_channel(outputs_ref, 0)
    ray = (iota((lanes, lanes), 0) % TILE) == (iota((lanes, lanes), 1) % TILE)
    earlier = (ray & (iota((lanes, lanes), 0) < iota((lanes, lanes), 1))).astype(F32).astype(BF16)
    later = (ray & (iota((lanes, lanes), 0) > iota((lanes, lanes), 1))).astype(F32).astype(BF16)
    total = ((iota((TILE, lanes), 1) % TILE) == iota((TILE, lanes), 0)).astype(F32).astype(BF16)
    density = jax.nn.softplus(raw)
    colors = [
        jax.nn.sigmoid(
            get_channel(outputs_ref, 1 + c) + shift[:, lanes * c : lanes * (c + 1)]
        )
        for c in range(3)
    ]
    optical = density * spacing
    transmit = jnp.exp(-pick_nn(optical, earlier))
    opacity = 1.0 - jnp.exp(-optical)
    blend = transmit * opacity
    sums = [pick_nt(total, blend * color) for color in colors] + [-pick_nt(total, optical)]
    dealt = pick_nn(jnp.concatenate(sums, axis=0), place)
    parts = [
        jnp.sum(mask * dealt[TILE * c : TILE * (c + 1), :], axis=0, keepdims=True) for c in range(4)
    ]

    def crossed(row, k):
        return row[:, rays * k : rays * (k + 1)]

    reach, logs = [], jnp.zeros((1, rays), F32)
    for k in range(crossings):
        reach.append(jnp.exp(logs))
        logs = logs + crossed(parts[3], k)
    residuals, channel_grads = [], [[] for _ in range(3)]
    for c in range(3):
        rendered = sum(reach[k] * crossed(parts[c], k) for k in range(crossings))
        rendered_ref[c : c + 1, :] = rendered
        residuals.append(rendered - target_ref[c : c + 1, :])
    log_grads, after = [], jnp.zeros((1, rays), F32)
    for k in reversed(range(crossings)):
        log_grads.append(after)
        weight = sum(residuals[c] * crossed(parts[c], k) for c in range(3))
        after = after + weight * reach[k]
    log_row = jnp.concatenate(log_grads[::-1], axis=1)
    color_rows = [
        jnp.concatenate([reach[k] * residuals[c] for k in range(crossings)], axis=1)
        for c in range(3)
    ]
    back = pick_nt(place, jnp.concatenate([mask * row for row in color_rows + [log_row]], axis=0))
    back = pick_nn(back, spread3)
    color_grads = [back[:, lanes * c : lanes * (c + 1)] for c in range(3)]
    log_grad = back[:, 3 * lanes : 4 * lanes]

    blend_grad = sum(color_grads[c] * colors[c] for c in range(3))
    before_grad = -(blend_grad * opacity) * transmit
    optical_grad = blend_grad * transmit * (1.0 - opacity) - log_grad
    optical_grad = optical_grad + pick_nn(before_grad, later)
    put_channel(grads_ref, 0, optical_grad * spacing * jax.nn.sigmoid(raw))
    logits = []
    for c in range(3):
        logit = color_grads[c] * blend * colors[c] * (1.0 - colors[c])
        put_channel(grads_ref, 1 + c, logit)
        put_channel(grads_ref, 4 + c, jnp.zeros((tiles, lanes), F32))
        logits.append(pick_nt(total, logit))
    put_channel(grads_ref, 7, jnp.zeros((tiles, lanes), F32))
    dealt = pick_nn(jnp.concatenate(logits, axis=0), place)
    per_cell = []
    for c in range(3):
        row = jnp.sum(mask * dealt[TILE * c : TILE * (c + 1), :], axis=0, keepdims=True)
        per_cell.append(sum(onehots[k] * crossed(row, k) for k in range(crossings)))
    per_cell = jnp.concatenate(per_cell, axis=0)
    map_grads = exact_nn(per_cell, codes.T)
    codes_grad_ref[...] = exact_nn(maps.T, per_cell)
    for v in range(cells):
        for c in range(3):
            sums_ref[v, APP_ROW + c : APP_ROW + c + 1, 0:width] = map_grads[
                cells * c + v : cells * c + v + 1, :
            ]

    def backward(trip, carry):
        some = [trip * UNROLL + u for u in range(UNROLL)]
        owner = [tile_cell_ref[0, t] for t in some]
        outputs = [get_tile(grads_ref, t).astype(BF16) for t in some]
        second_grads = [dot_nn(head_turned_ref[v], output) for v, output in zip(owner, outputs)]
        second_grads = [
            jnp.where(second_ref[t] > 0, grad.astype(BF16), jnp.zeros((), BF16))
            for t, grad in zip(some, second_grads)
        ]
        first_grads = [dot_nn(backward2_ref[v], grad) for v, grad in zip(owner, second_grads)]
        first_grads = [
            jnp.where(first_ref[t] > 0, grad.astype(BF16), jnp.zeros((), BF16))
            for t, grad in zip(some, first_grads)
        ]
        head_parts = [dot_nt(output, second_ref[t]) for t, output in zip(some, outputs)]
        second_parts = [dot_nt(first_ref[t], grad) for t, grad in zip(some, second_grads)]
        first_parts = [dot_nt(encoded_ref[t], grad) for t, grad in zip(some, first_grads)]
        for v, head, second, first in zip(owner, head_parts, second_parts, first_parts):
            sums_ref[v, HEAD_ROW:ROWS, :] += head
            sums_ref[v, 128:256, :] += second
            sums_ref[v, 0:128, :] += first
        return carry

    num_cell = cells // 4
    copies = []

    def emit(half):
        for district in (2 * half + 1, 2 * half):
            members = sums_ref.at[pl.ds(district * num_cell, num_cell)]
            total = sums_ref[district * num_cell]
            for s in range(1, num_cell):
                total = total + sums_ref[district * num_cell + s]
            sums_ref[cells + district] = total
            out_ref = (keep_near_ref, keep_far_ref, send_near_ref, send_far_ref)[district]
            for source, sink in (
                (members, out_ref.at[pl.ds(0, num_cell)]),
                (sums_ref.at[cells + district], out_ref.at[num_cell]),
            ):
                copies.append(pltpu.make_async_copy(source, sink, semaphore.at[len(copies)]))
                copies[-1].start()

    middle = (tile_start_ref[cells // 2, 0] + UNROLL - 1) // UNROLL
    lax.fori_loop(0, middle, backward, 0)
    emit(0)
    lax.fori_loop(middle, trips, backward, 0)
    emit(1)
    for copy in copies:
        copy.wait()


def resident(
    ray_geometry,
    segment_length,
    jitter,
    appearance_codes,
    target,
    crossing,
    frequencies,
    cell_layers,
    district_prior,
    head_weight,
    appearance_weight,
):
    num_cell = lax.axis_size("cell")
    num_district = lax.axis_size("district")
    cells = num_cell * num_district
    rays, crossings = crossing.shape
    samples = jitter.shape[1] // crossings
    segments = rays * crossings
    width = appearance_codes.shape[1]
    lanes = TILE * samples
    tiles = -(-(segments // TILE + cells) // UNROLL) * UNROLL
    me_cell, me_district = lax.axis_index("cell"), lax.axis_index("district")

    def flip(x, bits, axis="district"):
        return lax.ppermute(x, axis, [(i, i ^ bits) for i in range(lax.axis_size(axis))])

    own, again = pl.pallas_call(
        pack_kernel, out_shape=[jax.ShapeDtypeStruct((ROWS, 128), F32)] * 2, name="pack"
    )(cell_layers, district_prior, head_weight, jnp.transpose(appearance_weight, (1, 0, 2)))
    vmem, smem = pl.BlockSpec(memory_space=pltpu.VMEM), pl.BlockSpec(memory_space=pltpu.SMEM)
    anywhere = pl.BlockSpec(memory_space=pl.ANY)
    params = pltpu.CompilerParams(vmem_limit_bytes=VMEM_LIMIT)

    crossed_own = flip(own, 2)
    away = (crossing & 3) ^ me_district
    steps = (crossing >> 2) ^ me_cell
    virtual = (((away & 1) * 2 + (away >> 1)) * num_cell + steps).T
    halves = lanes // 128
    default = pl.BlockSpec()
    meta, spacing, tile_cell, tile_start, position, factor, passed = pl.pallas_call(
        functools.partial(deal_kernel, cells, samples),
        in_specs=[default] * 5 + [anywhere, anywhere],
        out_specs=[default] * 6 + [anywhere],
        input_output_aliases={5: 6},
        out_shape=[
            jax.ShapeDtypeStruct((8, segments), F32),
            jax.ShapeDtypeStruct((tiles, lanes), F32),
            jax.ShapeDtypeStruct((8, 256), jnp.int32),
            jax.ShapeDtypeStruct((cells + 8, 128), jnp.int32),
            jax.ShapeDtypeStruct((halves, tiles * 8, 128), F32),
            jax.ShapeDtypeStruct((frequencies.shape[1], 48), BF16),
            jax.ShapeDtypeStruct((ROWS, 128), F32),
        ],
        compiler_params=params,
        cost_estimate=pl.CostEstimate(flops=6 << 30, bytes_accessed=4 << 20, transcendentals=0),
        name="deal",
    )(virtual, ray_geometry, segment_length.T, jitter, frequencies, again, crossed_own)
    near = [own]
    for s in range(1, num_cell):
        near.append(flip(near[s & (s - 1)], s & -s, "cell"))
    flipped = [crossed_own] + [flip(piece, 2) for piece in near[1:]]
    weights = near + flipped + [flip(piece, 1) for piece in [passed] + near[1:] + flipped]


    rendered, codes_grad, keep, keep_far, send, send_far = pl.pallas_call(
        functools.partial(step_kernel, cells, samples),
        in_specs=[smem, smem] + [vmem] * (7 + cells),
        out_specs=[vmem, vmem, anywhere, vmem, anywhere, anywhere],
        out_shape=[
            jax.ShapeDtypeStruct((3, rays), F32),
            jax.ShapeDtypeStruct((width, rays), F32),
            *[jax.ShapeDtypeStruct((num_cell + 1, ROWS, 128), F32)] * 4,
        ],
        scratch_shapes=[
            pltpu.VMEM((tiles, 128, lanes), BF16),
            pltpu.VMEM((tiles, 128, lanes), BF16),
            pltpu.VMEM((tiles, 128, lanes), BF16),
            pltpu.VMEM((cells, 128, 128), BF16),
            pltpu.VMEM((cells, 128, 128), BF16),
            pltpu.VMEM((cells, 128, 128), BF16),
            pltpu.VMEM((cells, 8, 128), BF16),
            pltpu.VMEM((cells, 128, 8), BF16),
            pltpu.VMEM((halves, tiles * 8, 128), F32),
            pltpu.VMEM((halves, tiles * 8, 128), F32),
            pltpu.VMEM((cells + 4, ROWS, 128), F32),
            pltpu.SemaphoreType.DMA((8,)),
        ],
        compiler_params=params,
        name="step",
    )(
        tile_cell,
        tile_start,
        meta,
        virtual,
        spacing,
        position,
        factor,
        appearance_codes.T,
        target,
        *weights,
    )

    cross_far, crossed = flip(send_far, 1), flip(send, 1)
    order = [3, 2, num_cell, 1, 0]
    pieces = {s: flip(keep_far[s] + cross_far[s], 2) for s in order}
    for s in order:
        near_part, cross_part, other = lax.optimization_barrier((keep[s], crossed[s], pieces[s]))
        pieces[s] = near_part + cross_part + other
    prior = pieces[num_cell][0:HEAD_ROW]
    bit = num_cell // 2
    while bit > 0:
        prior = prior + flip(prior, bit, "cell")
        bit //= 2
    prior = (prior / num_cell).reshape(2, 128, 128)
    bit = 1
    while 2 * bit < num_cell:
        for s in reversed(range(bit, num_cell, 2 * bit)):
            pieces[s - bit] = pieces[s - bit] + flip(pieces[s], bit, "cell")
        bit *= 2
    last = flip(pieces[bit], bit, "cell")
    layers = pieces[0][0:HEAD_ROW] + last[0:HEAD_ROW]
    tail = pieces[0][HEAD_ROW:] + last[HEAD_ROW:]
    return (
        rendered,
        layers.reshape(1, 2, 128, 128),
        prior[None],
        tail[None, 0:4],
        tail[None, APP_ROW - HEAD_ROW : APP_ROW - HEAD_ROW + 3, 0:width],
        codes_grad.T,
    )


def local(*args):
    cells = lax.axis_size("cell") * lax.axis_size("district")
    if cells <= 16 and lax.axis_size("district") == 4:
        return resident(*args)
    return routed(*args)


def solution(mesh):
    placed = (
        P(None, ("scene", "cell", "district")),
        P(("scene", "cell", "district"), None),
        P(("scene", "cell", "district"), None),
        P(("scene", "cell", "district"), None),
        P(None, ("scene", "cell", "district")),
        P(("scene", "cell", "district"), None),
        P(),
        P(("scene", "cell", "district"), None, None, None),
        P(("scene", "district"), None, None, None),
        P(("scene", "cell", "district"), None, None),
        P(("scene", "cell", "district"), None, None),
    )
    return jax.shard_map(
        local,
        mesh=mesh,
        in_specs=placed,
        out_specs=(
            P(None, ("scene", "cell", "district")),
            P(("scene", "cell", "district"), None, None, None),
            P(("scene", "district"), None, None, None),
            P(("scene", "cell", "district"), None, None),
            P(("scene", "cell", "district"), None, None),
            P(("scene", "cell", "district"), None),
        ),
        check_vma=False,
    )
```
